128 devices in a mesh: lat: 4 (over z_hi, core), lon: 32 (over y, z_lo, x).
Axes of the slice: x: 4, y: 4, z: 4 (z_hi: 2, z_lo: 2; z = z_hi * 2 + z_lo), core: 2. Of those that a mesh axis runs over, the one named last changes fastest.
Arguments:
- initial_state: bfloat16 [69, 64, 4096], P(None, 'lat', 'lon'), may hold values from -6 to 6
- background_state: bfloat16 [69, 64, 4096], P(None, 'lat', 'lon'), may hold values from -6 to 6
- background_precision: float32 [69], replicated, may hold values from 0.2 to 2
- conv_weight: bfloat16 [9, 69, 256], replicated, may hold values from -0.25 to 0.25
- conv_bias: float32 [256], replicated, may hold values from -3 to 3
- out_weight: bfloat16 [69, 256], replicated, may hold values from -0.375 to 0.375
- swath_patch: int32 [128, 128], P(('lat', 'lon')), may hold values from 0 to 7
- obs_cell: int32 [128, 128, 128], P(('lat', 'lon')), may hold values from 0 to 17534, as said below
- obs_weights: float32 [4, 128, 128, 128], P(None, ('lat', 'lon')), may hold values from 0.05 to 1
- obs_value: float32 [128, 128, 128], P(('lat', 'lon')), may hold values from -6 to 6
- obs_precision: float32 [128, 128, 128], P(('lat', 'lon')), may hold values from 0.3 to 3
Outputs:
- gradient: float32 [69, 64, 4096], P(None, 'lat', 'lon')
- innovation: float32 [128, 128, 128], P(('lat', 'lon'))
The draws below stay inside these ranges and needn't reach their ends.
Inputs may be any that keep to these rules, and one draw needn't show every extreme that they name: `swath_patch`: entry [t, o] is the patch of tile t, numbered row by row among its 8 patches, in which owner o's observations of slot t lie. `obs_cell`: each entry is channel * 2 * 128 + row * 128 + column of the observation's upper-left neighbouring cell inside its patch, with row below 1 and column below 127.
All inputs are finite; a program needn't handle non-finite values.
Results may differ from the reference program's by a relative error of at most 0.0049.
Values may be sent and summed in bfloat16 or wider, within the bound.
A program may use at most 128 MiB of HBM per device.

```python
import math
import jax
import jax.numpy as jnp
from jax import lax

C = 69
HID = 256
PLAT = 2
PLON = 128
TLAT = 16
TLON = 128
OBS_SLOT = 128
NLAT = 64
NLON = 4096
OWNERS = 128
PPT = 8
N_LAT = 4
N_LON = 32


def draw_obs_cell(key, part):
    key = jax.random.fold_in(key, 11)
    key_chan, key_row, key_col = jax.random.split(key, 3)
    obs_shape = (OWNERS, OWNERS, OBS_SLOT)
    channel = jax.random.randint(key_chan, obs_shape, 0, C)
    lat_cell = jax.random.randint(key_row, obs_shape, 0, PLAT - 1)
    lon_cell = jax.random.randint(key_col, obs_shape, 0, PLON - 1)
    anchor = channel * (PLAT * PLON) + lat_cell * PLON + lon_cell
    top_cell = (C - 1) * PLAT * PLON + (PLAT - 2) * PLON + PLON - 2
    anchor = anchor.at[0, 0, 0].set(top_cell).at[0, 0, 1].set(0)
    return anchor.astype(jnp.int32)


def set_ends(entries, rng, low, top_value):
    longest = entries.shape.index(max(entries.shape))
    spots = []
    for shift in (0, 1):
        where = [jax.random.randint(jax.random.fold_in(rng, axis), (), 0, length) for axis, length in enumerate(entries.shape)]
        where[longest] = (where[longest] + shift) % entries.shape[longest]
        spots.append(tuple(where))
    return entries.at[spots[0]].set(low).at[spots[1]].set(top_value)


def shard_levels(rng, dims, shards, low, high):
    def one(dim, parts):
        steps = jax.random.uniform(jax.random.fold_in(jax.random.fold_in(rng, 6), dim), (parts,), jnp.float32, low / len(shards), high / len(shards))
        return jnp.repeat(jnp.exp(steps), dims[dim] // parts).reshape((-1,) + (1,) * (len(dims) - dim - 1))

    factor_of = one(*shards[0])
    for cut in shards[1:]:
        factor_of = factor_of * one(*cut)
    return factor_of


def normal_values(rng, shape, width, limit, cuts=(), kind=jnp.bfloat16):
    values = jax.random.normal(rng, shape, jnp.float32) * width
    if len(cuts) > 0:
        values = shard_levels(rng, shape, cuts, -0.22, 0.18) * values
    return jnp.clip(values, min=-limit, max=limit).astype(kind)


def setup_inputs(seed: int = 0) -> dict:
    keys = jax.random.split(jax.random.key(seed), 12)
    return {
        "initial_state": normal_values(keys[0], (C, NLAT, NLON), 1.0, 6.0, ((1, 4), (2, 32))),
        "background_state": normal_values(keys[1], (C, NLAT, NLON), 1.0, 6.0, ((1, 4), (2, 32))),
        "background_precision": jnp.clip(jnp.exp(jax.random.uniform(keys[2], (C,), jnp.float32, math.log(0.2), math.log(2.0))), 0.2, 2.0),
        "conv_weight": normal_values(keys[3], (9, C, HID), (9 * C) ** -0.5, 0.25),
        "conv_bias": normal_values(keys[4], (HID,), 0.5, 3.0, (), jnp.float32),
        "out_weight": normal_values(keys[5], (C, HID), HID ** -0.5, 0.375),
        "swath_patch": set_ends(jax.random.randint(keys[6], (OWNERS, OWNERS), 0, PPT), jax.random.fold_in(keys[6], 1), 0, PPT - 1).astype(jnp.int32),
        "obs_cell": draw_obs_cell(jax.random.fold_in(keys[11], 71), 0),
        "obs_weights": jnp.clip(0.05 + 0.95 * jax.random.uniform(keys[8], (4, OWNERS, OWNERS, OBS_SLOT), jnp.float32) ** shard_levels(keys[8], (4, OWNERS, OWNERS, OBS_SLOT), ((1, 128),), -0.2, 0.2), 0.05, 1.0),
        "obs_value": normal_values(keys[9], (OWNERS, OWNERS, OBS_SLOT), 1.0, 6.0, ((0, 128),), jnp.float32),
        "obs_precision": jnp.clip(jnp.exp(math.log(3.0) - 2.3025851 * jax.random.uniform(keys[10], (OWNERS, OWNERS, OBS_SLOT), jnp.float32) ** shard_levels(keys[10], (OWNERS, OWNERS, OBS_SLOT), ((0, 128),), -0.2, 0.2)), 0.3, 3.0),
    }


root_half = 0.7071067811865476
norm_density = 0.3989422804014327


def gelu_slope(preact):
    return 0.5 * (1.0 + lax.erf(preact * root_half)) + preact * jnp.exp(-0.5 * preact * preact) * norm_density


def wrap_pad(grid_field, margin):
    grid_field = jnp.concatenate([grid_field[:, :, -margin:], grid_field, grid_field[:, :, :margin]], axis=2)
    zero_rows = jnp.zeros((grid_field.shape[0], margin, grid_field.shape[2]), grid_field.dtype)
    return jnp.concatenate([zero_rows, grid_field, zero_rows], axis=1)


def conv_pre(slab, conv_weight, conv_bias):
    height = slab.shape[1] - 2
    breadth = slab.shape[2] - 2
    total = jnp.zeros((conv_weight.shape[2], height, breadth), jnp.float32)
    for row_shift in range(3):
        for col_shift in range(3):
            kernel = conv_weight[3 * row_shift + col_shift].astype(jnp.float32)
            window = slab[:, row_shift:row_shift + height, col_shift:col_shift + breadth].astype(jnp.float32)
            total = total + jnp.einsum("ch,crl->hrl", kernel, window)
    return total + conv_bias[:, None, None]


def advance(state_in, conv_weight, conv_bias, out_weight):
    padded = wrap_pad(state_in, 1)

    def band_step(start):
        slab = lax.dynamic_slice_in_dim(padded, start, TLAT + 2, 1)
        preact = conv_pre(slab, conv_weight, conv_bias)
        hidden = jax.nn.gelu(preact, approximate=False).astype(jnp.bfloat16)
        update = jnp.einsum("ch,hrl->crl", out_weight.astype(jnp.float32), hidden.astype(jnp.float32))
        middle = lax.dynamic_slice_in_dim(state_in, start, TLAT, 1).astype(jnp.float32)
        return (middle + update).astype(jnp.bfloat16)

    starts = (jnp.arange(N_LAT) * TLAT).astype(jnp.int32)
    band_out = lax.map(band_step, starts)
    return jnp.transpose(band_out, (1, 0, 2, 3)).reshape(state_in.shape)


def retreat(state_in, cotangent, conv_weight, conv_bias, out_weight):
    padded = wrap_pad(state_in, 2)
    cot_padded = wrap_pad(cotangent.astype(jnp.bfloat16), 1)
    breadth = state_in.shape[2]

    def band_step(start):
        slab = lax.dynamic_slice_in_dim(padded, start, TLAT + 4, 1)
        preact = conv_pre(slab, conv_weight, conv_bias)
        cot_slab = lax.dynamic_slice_in_dim(cot_padded, start, TLAT + 2, 1)
        along = jnp.einsum("ch,crl->hrl", out_weight.astype(jnp.float32), cot_slab.astype(jnp.float32))
        spread = (along * gelu_slope(preact)).astype(jnp.bfloat16)
        total = lax.dynamic_slice_in_dim(cotangent, start, TLAT, 1)
        for row_shift in range(3):
            for col_shift in range(3):
                window = spread[:, 2 - row_shift:2 - row_shift + TLAT, 2 - col_shift:2 - col_shift + breadth]
                kernel = conv_weight[3 * row_shift + col_shift].astype(jnp.float32)
                total = total + jnp.einsum("ch,hrl->crl", kernel, window.astype(jnp.float32))
        return total

    starts = (jnp.arange(N_LAT) * TLAT).astype(jnp.int32)
    band_out = lax.map(band_step, starts)
    return jnp.transpose(band_out, (1, 0, 2, 3)).reshape(state_in.shape)


def observe(second_state, swath_patch, obs_cell, obs_weights, obs_value, obs_precision):
    owners = swath_patch.shape[0]
    tile_ids = jnp.arange(owners, dtype=jnp.int32)
    per_row = TLON // PLON
    patch_ids = jnp.transpose(swath_patch)
    lat_base = (tile_ids // N_LON)[None, :] * TLAT + (patch_ids // per_row) * PLAT
    lon_base = (tile_ids % N_LON)[None, :] * TLON + (patch_ids % per_row) * PLON
    patch_area = PLAT * PLON
    channel = obs_cell // patch_area
    lat_cell = lat_base[:, :, None] + (obs_cell % patch_area) // PLON
    lon_cell = lon_base[:, :, None] + obs_cell % PLON
    anchor = (channel * NLAT + lat_cell) * NLON + lon_cell
    flat_state = second_state.reshape(-1)
    offsets = (0, 1, NLON, NLON + 1)
    estimate = jnp.zeros(obs_value.shape, jnp.float32)
    for corner in range(4):
        estimate = estimate + flat_state[anchor + offsets[corner]].astype(jnp.float32) * obs_weights[corner]
    innovation = estimate - obs_value
    weighted = obs_precision * innovation
    pull_field = jnp.zeros(flat_state.shape, jnp.float32)
    for corner in range(4):
        pull_field = pull_field.at[(anchor + offsets[corner]).reshape(-1)].add((weighted * obs_weights[corner]).reshape(-1))
    return innovation, pull_field.reshape(second_state.shape)


def reference(initial_state, background_state, background_precision, conv_weight, conv_bias, out_weight, swath_patch, obs_cell, obs_weights, obs_value, obs_precision):
    first_state = advance(initial_state, conv_weight, conv_bias, out_weight)
    second_state = advance(first_state, conv_weight, conv_bias, out_weight)
    innovation, pull_field = observe(second_state, swath_patch, obs_cell, obs_weights, obs_value, obs_precision)
    middle = retreat(first_state, pull_field, conv_weight, conv_bias, out_weight)
    last_cot = retreat(initial_state, middle, conv_weight, conv_bias, out_weight)
    departure = initial_state.astype(jnp.float32) - background_state.astype(jnp.float32)
    gradient = background_precision[:, None, None] * departure + last_cot
    return gradient, innovation
```

```python
import functools

import jax
import jax.numpy as jnp
from jax import lax
from jax.experimental import pallas as pl
from jax.experimental.pallas import tpu as pltpu
from jax.sharding import PartitionSpec as P

MESH = pl.DeviceIdType.MESH
F32 = jnp.float32
BF16 = jnp.bfloat16
CP = 80
LANES = 128
WIDE = 256
ROOT_HALF = 0.7071067811865476
NORM_DENSITY = 0.3989422804014327
UP, DOWN, LEFT, RIGHT, UL, UR, DL, DR = range(8)
GROUP = 8


def dot(a, b):
    return jnp.dot(a, b, preferred_element_type=F32)


def lane_iota(rows):
    return lax.broadcasted_iota(jnp.int32, (rows, LANES), 1)


def kernel(
    n_lat, n_lon, hid,
    x_ref, wt_ref, wb_ref, wo_ref, wot_ref, bias_ref, swath_ref, cell_ref, w_ref, val_ref, prec_ref,
    cot_ref, innov_ref,
    x32, packed, recv, s1, s2, sobs, slope1, slope2, csend, hcol, hdiag,
    bsc, qsc, inn, inn_recv, hist, ybuf, ubuf, gbuf, brow, bcol, rrow, rdiag, rcol,
    fsend, frecv, bsend, brecv, psend, precv, isend, irecv,
):
    chan, height = x_ref.shape[0], x_ref.shape[1]
    owners = n_lat * n_lon
    chunks = height // 2
    lat = lax.axis_index("lat")
    lon = lax.axis_index("lon")
    me = lat * n_lon + lon
    has_up = lat > 0
    has_down = lat < n_lat - 1
    left = lax.rem(lon + n_lon - 1, n_lon)
    right = lax.rem(lon + 1, n_lon)
    ids = {
        UP: (lat - 1, lon), DOWN: (lat + 1, lon), LEFT: (lat, left), RIGHT: (lat, right),
        UL: (lat - 1, left), UR: (lat - 1, right), DL: (lat + 1, left), DR: (lat + 1, right),
    }
    opposite = {UP: DOWN, DOWN: UP, LEFT: RIGHT, RIGHT: LEFT, UL: DR, DR: UL, UR: DL, DL: UR}

    def coords(k):
        other = lax.rem(me + k, owners)
        return other, (other // n_lon, lax.rem(other, n_lon))

    barrier = pltpu.get_barrier_semaphore()

    def greet(k, carry):
        _, where = coords(k)
        pl.semaphore_signal(barrier, inc=1, device_id=where, device_id_type=MESH)
        return carry

    lax.fori_loop(1, owners, greet, 0)

    x32[pl.ds(chan * height, (CP - chan) * height), :] = jnp.zeros(((CP - chan) * height, LANES), F32)
    x32[pl.ds(0, chan * height), :] = x_ref[...].astype(F32).reshape(chan * height, LANES)
    cell = cell_ref[...]
    packed[pl.ds(0, owners, stride=8), :] = (cell // WIDE).astype(F32)
    packed[pl.ds(1, owners, stride=8), :] = (cell % LANES).astype(F32)
    for k in range(4):
        packed[pl.ds(2 + k, owners, stride=8), :] = w_ref[k]
    packed[pl.ds(6, owners, stride=8), :] = val_ref[...]
    packed[pl.ds(7, owners, stride=8), :] = prec_ref[...]
    zero_rows = jnp.zeros((hid - 3 * CP, (height + 2) * LANES), BF16)
    s1[pl.ds(3 * CP, hid - 3 * CP), :] = zero_rows
    s2[pl.ds(3 * CP, hid - 3 * CP), :] = zero_rows
    lane = lane_iota(CP)
    first_lane = lane == 0
    last_lane = lane == LANES - 1

    def block(r):
        return pl.ds((r + 1) * LANES, LANES)

    for r in range(height):
        s1[pl.ds(CP, CP), block(r)] = x32[pl.ds(r, CP, stride=height), :].astype(BF16)

    def guarded(d):
        if d in (UP, UL, UR):
            return pl.when(has_up)
        if d in (DOWN, DL, DR):
            return pl.when(has_down)
        return lambda f: f()

    def send(src, dst, t, d, sends, recvs):
        copy = pltpu.make_async_remote_copy(
            src_ref=src, dst_ref=dst, send_sem=sends.at[t, d], recv_sem=recvs.at[t, opposite[d]],
            device_id=ids[d], device_id_type=MESH,
        )
        guarded(d)(copy.start)

    def wait_recv(dst, t, d, sends, recvs):
        copy = pltpu.make_async_remote_copy(
            src_ref=dst, dst_ref=dst, send_sem=sends.at[t, d], recv_sem=recvs.at[t, d],
            device_id=ids[d], device_id_type=MESH,
        )
        guarded(d)(copy.wait_recv)

    def wait_send(src, t, d, sends, recvs):
        copy = pltpu.make_async_remote_copy(
            src_ref=src, dst_ref=src, send_sem=sends.at[t, d], recv_sem=recvs.at[t, d],
            device_id=ids[d], device_id_type=MESH,
        )
        guarded(d)(copy.wait_send)

    def column_blocks(rows, first_of, last_of):
        to_left = jnp.zeros((CP, LANES), F32)
        to_right = jnp.zeros((CP, LANES), F32)
        for r in range(rows):
            to_left = jnp.where(lane == r, pltpu.roll(first_of(r), r, 1) if r else first_of(r), to_left)
            to_right = jnp.where(lane == r, pltpu.roll(last_of(r), r + 1, 1), to_right)
        return to_left.astype(BF16), to_right.astype(BF16)

    diag_slots = {UL: 0, UR: 1, DL: 2, DR: 3}

    def centre(s, r):
        return s.at[pl.ds(CP, CP), block(r)]

    def state_sources(s, t):
        return {
            UP: centre(s, 0), UL: centre(s, 0), UR: centre(s, 0),
            DOWN: centre(s, height - 1), DL: centre(s, height - 1), DR: centre(s, height - 1),
            LEFT: csend.at[t, 0], RIGHT: csend.at[t, 1],
        }

    def state_targets(s, t):
        table = {UP: centre(s, -1), DOWN: centre(s, height), LEFT: hcol.at[t, 0], RIGHT: hcol.at[t, 1]}
        for d, slot in diag_slots.items():
            table[d] = hdiag.at[t, slot]
        return table

    def send_state(s, t):
        src, dst = state_sources(s, t), state_targets(s, t)
        for d in (UP, DOWN, UL, UR, DL, DR):
            send(src[d], dst[opposite[d]], t, d, fsend, frecv)

        def row(r):
            return s[pl.ds(CP, CP), block(r)].astype(F32)

        to_left, to_right = column_blocks(height, row, row)
        csend[t, 0] = to_left
        csend[t, 1] = to_right
        for d in (LEFT, RIGHT):
            send(src[d], dst[opposite[d]], t, d, fsend, frecv)

    def receive_state(s, t):
        dst = state_targets(s, t)
        for d in range(8):
            wait_recv(dst[d], t, d, fsend, frecv)
        from_left = hcol[t, 0].astype(F32)
        from_right = hcol[t, 1].astype(F32)
        for r in range(height):
            row = s[pl.ds(CP, CP), block(r)].astype(F32)
            lower = jnp.where(
                first_lane, pltpu.roll(from_left, (LANES - r) % LANES, 1) if r else from_left, pltpu.roll(row, 1, 1)
            )
            upper = jnp.where(last_lane, pltpu.roll(from_right, LANES - 1 - r, 1), pltpu.roll(row, LANES - 1, 1))
            s[pl.ds(0, CP), block(r)] = lower.astype(BF16)
            s[pl.ds(2 * CP, CP), block(r)] = upper.astype(BF16)
        for r, there, a, b in ((-1, has_up, UL, UR), (height, has_down, DL, DR)):

            @pl.when(there)
            def _():
                row = s[pl.ds(CP, CP), block(r)].astype(F32)
                lower = jnp.where(last_lane, hdiag[t, diag_slots[a]].astype(F32), row)
                upper = jnp.where(first_lane, hdiag[t, diag_slots[b]].astype(F32), row)
                s[pl.ds(0, CP), block(r)] = pltpu.roll(lower, 1, 1).astype(BF16)
                s[pl.ds(2 * CP, CP), block(r)] = pltpu.roll(upper, LANES - 1, 1).astype(BF16)

            @pl.when(jnp.logical_not(there))
            def _():
                s[pl.ds(0, 3 * CP), block(r)] = jnp.zeros((3 * CP, LANES), BF16)

    def forward_chunk(s, n, slope):
        pre = bias_ref[...]
        for i in range(3):
            pre = pre + dot(wt_ref[i], s[:, pl.ds((2 * n + i) * LANES, WIDE)])
        cdf = 0.5 * (1.0 + lax.erf(pre * ROOT_HALF))
        slope[:, pl.ds(n * WIDE, WIDE)] = cdf + pre * jnp.exp(-0.5 * pre * pre) * NORM_DENSITY
        update = dot(wo_ref[...], (pre * cdf).astype(BF16))
        return (s[pl.ds(CP, CP), pl.ds((2 * n + 1) * LANES, WIDE)].astype(F32) + update).astype(BF16)

    pl.semaphore_wait(barrier, owners - 1)
    send_state(s1, 0)

    def post(k, carry):
        other, where = coords(k)
        pltpu.make_async_remote_copy(
            src_ref=packed.at[pl.ds(pl.multiple_of(other * 8, 8), 8)],
            dst_ref=recv.at[pl.ds(pl.multiple_of(me * 8, 8), 8)],
            send_sem=psend, recv_sem=precv, device_id=where, device_id_type=MESH,
        ).start()
        return carry

    lax.fori_loop(1, owners, post, 0)
    mine = pl.ds(pl.multiple_of(me * 8, 8), 8)
    recv[mine, :] = packed[mine, :]

    receive_state(s1, 0)
    for n in range(chunks):
        s2[pl.ds(CP, CP), pl.ds((2 * n + 1) * LANES, WIDE)] = forward_chunk(s1, n, slope1)
    send_state(s2, 1)
    receive_state(s2, 1)
    for n in range(chunks):
        sobs[n] = forward_chunk(s2, n, slope2)

    others = pl.ds(0, (owners - 1) * 8)
    pltpu.make_async_remote_copy(
        src_ref=packed.at[others], dst_ref=recv.at[others], send_sem=psend, recv_sem=precv,
        device_id=ids[RIGHT], device_id_type=MESH,
    ).wait()
    column = lax.broadcasted_iota(jnp.int32, (LANES, LANES), 0).astype(F32)
    channel = lax.broadcasted_iota(jnp.int32, (CP, LANES), 0).astype(F32)

    def estimate(group, carry):
        for u in range(GROUP):
            k = group * GROUP + u
            other, _ = coords(k + 1)
            packet = recv[pl.ds(pl.multiple_of(other * 8, 8), 8), :]
            here, after = column == packet[1:2], column == packet[1:2] + 1.0
            table = jnp.concatenate(
                [
                    jnp.where(here, packet[2:3], jnp.where(after, packet[3:4], 0.0)),
                    jnp.where(here, packet[4:5], jnp.where(after, packet[5:6], 0.0)),
                ],
                axis=0,
            ).astype(BF16)
            bsc[k] = table
            picked = channel == packet[0:1]
            found = dot(sobs[swath_ref[0, other]], table)
            gap = jnp.sum(jnp.where(picked, found, 0.0), axis=0, keepdims=True) - packet[6:7]
            inn[other] = gap
            qsc[k] = jnp.where(picked, packet[7:8] * gap, 0.0).astype(BF16)
        return carry

    lax.fori_loop(0, owners // GROUP, estimate, 0)
    hist[0] = jnp.zeros((CP, WIDE), F32)

    def pull(group, last):
        for u in range(GROUP):
            k = group * GROUP + u
            other, where = coords(k + 1)
            copy = pltpu.make_async_remote_copy(
                src_ref=inn.at[other], dst_ref=inn_recv.at[me], send_sem=isend, recv_sem=irecv,
                device_id=where, device_id_type=MESH,
            )
            if u < GROUP - 1:
                copy.start()
            else:
                pl.when(k < owners - 1)(copy.start)
            spot = swath_ref[0, other]
            before = sum(jnp.where(spot == m, last[m], 0) for m in range(chunks))
            share = lax.dot_general(qsc[k], bsc[k], (((1,), (1,)), ((), ())), preferred_element_type=F32)
            hist[k + 1] = hist[before] + share
            last = tuple(jnp.where(spot == m, k + 1, last[m]) for m in range(chunks))
        return last

    last = lax.fori_loop(0, owners // GROUP, pull, (jnp.int32(0),) * chunks)
    inn_recv[me] = inn[me]

    def tap(i, j, r):
        return ybuf[pl.ds((3 * (i + 1) + j + 1) * CP, CP), pl.ds(r * LANES, LANES)]

    def summed(j, r):
        total = None
        for i in (-1, 0, 1):
            if 0 <= r - i < height:
                part = tap(i, j, r - i)
                total = part if total is None else total + part
        return total

    def rim_sources(t):
        return {
            UP: brow.at[t, 0], UL: brow.at[t, 1], UR: brow.at[t, 2],
            DOWN: brow.at[t, 3], DL: brow.at[t, 4], DR: brow.at[t, 5],
            LEFT: bcol.at[t, 0], RIGHT: bcol.at[t, 1],
        }

    def rim_targets(t):
        table = {UP: rrow.at[t, 0], DOWN: rrow.at[t, 1], LEFT: rcol.at[t, 0], RIGHT: rcol.at[t, 1]}
        for d, slot in diag_slots.items():
            table[d] = rdiag.at[t, slot]
        return table

    pad = jnp.zeros((LANES - CP, WIDE), BF16)

    def backward_step(t, cotangent, slope, finish):
        src, dst = rim_sources(t), rim_targets(t)
        for n in range(chunks):
            rounded = jnp.concatenate([cotangent(n).astype(BF16), pad], axis=0)
            spread = (dot(wot_ref[...], rounded) * slope[:, pl.ds(n * WIDE, WIDE)]).astype(BF16)
            ybuf[:, pl.ds(n * WIDE, WIDE)] = dot(wb_ref[...], spread)

        def inner(t_low, t_mid, t_high):
            return (
                t_mid
                + jnp.where(first_lane, 0.0, pltpu.roll(t_high, 1, 1))
                + jnp.where(last_lane, 0.0, pltpu.roll(t_low, LANES - 1, 1))
            )

        for r, at in ((-1, 0), (height, 3)):
            t_low, t_mid, t_high = (summed(j, r) for j in (-1, 0, 1))
            brow[t, at] = inner(t_low, t_mid, t_high).astype(BF16)
            brow[t, at + 1] = t_low.astype(BF16)
            brow[t, at + 2] = t_high.astype(BF16)
        for d in (UP, DOWN, UL, UR, DL, DR):
            send(src[d], dst[opposite[d]], t, d, bsend, brecv)
        to_left, to_right = column_blocks(height, lambda r: summed(-1, r), lambda r: summed(1, r))
        bcol[t, 0] = to_left
        bcol[t, 1] = to_right
        for d in (LEFT, RIGHT):
            send(src[d], dst[opposite[d]], t, d, bsend, brecv)
        for r in range(height):
            ubuf[:, pl.ds(r * LANES, LANES)] = inner(summed(-1, r), summed(0, r), summed(1, r)) + cotangent(r // 2)[
                :, (r % 2) * LANES : (r % 2 + 1) * LANES
            ]
        for d in range(8):
            wait_recv(dst[d], t, d, bsend, brecv)
        for r, there, at, a, b in ((0, has_up, 0, UL, UR), (height - 1, has_down, 1, DL, DR)):

            @pl.when(there)
            def _():
                ubuf[:, pl.ds(r * LANES, LANES)] = (
                    ubuf[:, pl.ds(r * LANES, LANES)]
                    + rrow[t, at].astype(F32)
                    + jnp.where(first_lane, pltpu.roll(rdiag[t, diag_slots[a]].astype(F32), 1, 1), 0.0)
                    + jnp.where(last_lane, pltpu.roll(rdiag[t, diag_slots[b]].astype(F32), LANES - 1, 1), 0.0)
                )

        from_left = rcol[t, 0].astype(F32)
        from_right = rcol[t, 1].astype(F32)
        for r in range(height):
            finish(
                r,
                ubuf[:, pl.ds(r * LANES, LANES)]
                + jnp.where(first_lane, pltpu.roll(from_left, (LANES - r) % LANES, 1) if r else from_left, 0.0)
                + jnp.where(last_lane, pltpu.roll(from_right, LANES - 1 - r, 1), 0.0),
            )

    def keep(r, value):
        gbuf[:, pl.ds(r * LANES, LANES)] = value

    def write(r, value):
        cot_ref[pl.ds(r, chan, stride=height), :] = value[:chan]

    backward_step(0, lambda n: hist[last[n]], slope2, keep)
    backward_step(1, lambda n: gbuf[:, pl.ds(n * WIDE, WIDE)], slope1, write)

    rows = pl.ds(0, owners - 1)
    pltpu.make_async_remote_copy(
        src_ref=inn.at[rows], dst_ref=inn_recv.at[rows], send_sem=isend, recv_sem=irecv,
        device_id=ids[RIGHT], device_id_type=MESH,
    ).wait()
    innov_ref[...] = inn_recv[...].reshape(owners, LANES)
    for t, s in enumerate((s1, s2)):
        src = state_sources(s, t)
        for d in range(8):
            wait_send(src[d], t, d, fsend, frecv)
    for t in range(2):
        src = rim_sources(t)
        for d in range(8):
            wait_send(src[d], t, d, bsend, brecv)


def local(
    n_lat, n_lon,
    initial_state, background_state, background_precision, conv_weight, conv_bias, out_weight,
    swath_patch, obs_cell, obs_weights, obs_value, obs_precision,
):
    chan, height, breadth = initial_state.shape
    hid = conv_weight.shape[2]
    owners = n_lat * n_lon
    chunks = height // 2
    cells = height * breadth
    padded = jnp.pad(conv_weight, ((0, 0), (0, CP - chan), (0, 0)))
    wb = padded.reshape(9 * CP, hid)
    wt = jnp.transpose(jnp.pad(padded.reshape(3, 3 * CP, hid), ((0, 0), (0, hid - 3 * CP), (0, 0))), (0, 2, 1))
    wo = jnp.pad(out_weight, ((0, CP - chan), (0, 0)))
    wot = jnp.transpose(jnp.pad(out_weight, ((0, LANES - chan), (0, 0))))
    vmem = pl.BlockSpec(memory_space=pltpu.VMEM)
    smem = pl.BlockSpec(memory_space=pltpu.SMEM)
    dma = pltpu.SemaphoreType.DMA
    cot, innov = pl.pallas_call(
        functools.partial(kernel, n_lat, n_lon, hid),
        out_shape=(
            jax.ShapeDtypeStruct((chan * height, LANES), F32),
            jax.ShapeDtypeStruct((owners, LANES), F32),
        ),
        in_specs=[vmem] * 6 + [smem] + [vmem] * 4,
        out_specs=(vmem, vmem),
        scratch_shapes=[
            pltpu.VMEM((CP * height, LANES), F32),
            pltpu.VMEM((owners * 8, LANES), F32),
            pltpu.VMEM((owners * 8, LANES), F32),
            pltpu.VMEM((hid, (height + 2) * LANES), BF16),
            pltpu.VMEM((hid, (height + 2) * LANES), BF16),
            pltpu.VMEM((chunks, CP, WIDE), BF16),
            pltpu.VMEM((hid, cells), F32),
            pltpu.VMEM((hid, cells), F32),
            pltpu.VMEM((2, 2, CP, LANES), BF16),
            pltpu.VMEM((2, 2, CP, LANES), BF16),
            pltpu.VMEM((2, 4, CP, LANES), BF16),
            pltpu.VMEM((owners, WIDE, LANES), BF16),
            pltpu.VMEM((owners, CP, LANES), BF16),
            pltpu.VMEM((owners, 1, LANES), F32),
            pltpu.VMEM((owners, 1, LANES), F32),
            pltpu.VMEM((owners + 1, CP, WIDE), F32),
            pltpu.VMEM((9 * CP, cells), F32),
            pltpu.VMEM((CP, cells), F32),
            pltpu.VMEM((CP, cells), F32),
            pltpu.VMEM((2, 6, CP, LANES), BF16),
            pltpu.VMEM((2, 2, CP, LANES), BF16),
            pltpu.VMEM((2, 2, CP, LANES), BF16),
            pltpu.VMEM((2, 4, CP, LANES), BF16),
            pltpu.VMEM((2, 2, CP, LANES), BF16),
            dma((2, 8)), dma((2, 8)), dma((2, 8)), dma((2, 8)),
            dma, dma, dma, dma,
        ],
        compiler_params=pltpu.CompilerParams(
            collective_id=0, has_side_effects=True, vmem_limit_bytes=56 * 1024 * 1024
        ),
    )(
        initial_state, wt, wb, wo, wot, conv_bias[:, None], swath_patch,
        obs_cell[0], obs_weights[:, 0], obs_value[0], obs_precision[0],
    )
    departure = initial_state.astype(F32) - background_state.astype(F32)
    gradient = background_precision[:, None, None] * departure + cot.reshape(chan, height, breadth)
    return gradient, innov[None]


def solution(mesh):
    tile = P(None, "lat", "lon")
    owner = ("lat", "lon")
    in_specs = (
        tile, tile, P(), P(), P(), P(),
        P(owner, None), P(owner, None, None), P(None, owner, None, None), P(owner, None, None), P(owner, None, None),
    )
    return jax.shard_map(
        functools.partial(local, mesh.shape["lat"], mesh.shape["lon"]),
        mesh=mesh, in_specs=in_specs, out_specs=(tile, P(owner, None, None)), check_vma=False,
    )
```

```python
import functools

import jax
import jax.numpy as jnp
from jax import lax
from jax.experimental import pallas as pl
from jax.experimental.pallas import tpu as pltpu
from jax.sharding import PartitionSpec as P

MESH = pl.DeviceIdType.MESH
F32 = jnp.float32
BF16 = jnp.bfloat16
CP = 80
LANES = 128
WIDE = 256
ROOT_HALF = 0.7071067811865476
NORM_DENSITY = 0.3989422804014327
UP, DOWN, LEFT, RIGHT, UL, UR, DL, DR = range(8)
GROUP = 8


def dot(a, b):
    return jnp.dot(a, b, preferred_element_type=F32)


def lane_iota(rows):
    return lax.broadcasted_iota(jnp.int32, (rows, LANES), 1)


def kernel(
    n_lat, n_lon, hid,
    x_ref, xb_ref, bp_ref, cw_ref, cb_ref, ow_ref, swath_ref, cell_ref, w_ref, val_ref, prec_ref,
    grad_ref, innov_ref,
    wpad, wk, wt_ref, wo_ref, wot_ref, x32, packed, recv, s1, s2, sobs, slope1, slope2, csend, hcol, hdiag,
    bsc, qsc, inn, inn_recv, hist, ybuf, ubuf, gbuf, brow, bcol, rrow, rdiag, rcol,
    fsend, frecv, bsend, brecv, psend, precv, isend, irecv,
):
    chan, height = x_ref.shape[0], x_ref.shape[1]
    owners = n_lat * n_lon
    chunks = height // 2
    lat = lax.axis_index("lat")
    lon = lax.axis_index("lon")
    me = lat * n_lon + lon
    has_up = lat > 0
    has_down = lat < n_lat - 1
    left = lax.rem(lon + n_lon - 1, n_lon)
    right = lax.rem(lon + 1, n_lon)
    ids = {
        UP: (lat - 1, lon), DOWN: (lat + 1, lon), LEFT: (lat, left), RIGHT: (lat, right),
        UL: (lat - 1, left), UR: (lat - 1, right), DL: (lat + 1, left), DR: (lat + 1, right),
    }
    opposite = {UP: DOWN, DOWN: UP, LEFT: RIGHT, RIGHT: LEFT, UL: DR, DR: UL, UR: DL, DL: UR}

    barrier = pltpu.get_barrier_semaphore()

    def wrapped(value, count):
        return value - jnp.where(value >= count, count, 0)

    def to_all(steps, act):
        for step in steps:
            there = wrapped(lat + step, n_lat)

            def one(ahead, carry, there=there):
                column = wrapped(lon + ahead, n_lon)
                act(there * n_lon + column, (there, column))
                return carry

            lax.fori_loop(0 if step else 1, n_lon, one, 0, unroll=4 if step else 1)

    def greet(_, where):
        pl.semaphore_signal(barrier, inc=1, device_id=where, device_id_type=MESH)

    to_all(range(n_lat), greet)

    wpad[...] = jnp.zeros((LANES, hid), F32)
    bias = cb_ref[...]
    bias_parts = []
    for _ in range(3):
        part = bias.astype(BF16).astype(F32)
        bias_parts.append(part)
        bias = bias - part
    spare = lax.broadcasted_iota(jnp.int32, (hid - 3 * CP, hid), 0)
    bias_rows = jnp.zeros((hid - 3 * CP, hid), F32)
    for k, part in enumerate(bias_parts):
        bias_rows = jnp.where(spare == k, part, bias_rows)
    for i in range(3):
        for j in range(3):
            wpad[pl.ds(0, chan), :] = cw_ref[3 * i + j].astype(F32)
            wk[i, pl.ds(j * CP, CP), :] = wpad[pl.ds(0, CP), :].astype(BF16)
        wk[i, pl.ds(3 * CP, hid - 3 * CP), :] = (bias_rows if i == 1 else jnp.zeros_like(bias_rows)).astype(BF16)
        wt_ref[i] = jnp.transpose(wk[i].astype(F32)).astype(BF16)
    wpad[pl.ds(0, chan), :] = ow_ref[...].astype(F32)
    wo_ref[...] = wpad[pl.ds(0, CP), :].astype(BF16)
    wot_ref[...] = jnp.transpose(wpad[...]).astype(BF16)
    for c in range(chan):
        grad_ref[pl.ds(c * height, height), :] = bp_ref[0, c] * (x_ref[c].astype(F32) - xb_ref[c].astype(F32))
    x32[pl.ds(chan * height, (CP - chan) * height), :] = jnp.zeros(((CP - chan) * height, LANES), F32)
    x32[pl.ds(0, chan * height), :] = x_ref[...].astype(F32).reshape(chan * height, LANES)
    cell = cell_ref[...]
    packed[pl.ds(0, owners, stride=8), :] = (cell // WIDE).astype(F32)
    packed[pl.ds(1, owners, stride=8), :] = (cell % LANES).astype(F32)
    for k in range(4):
        packed[pl.ds(2 + k, owners, stride=8), :] = w_ref[k]
    packed[pl.ds(6, owners, stride=8), :] = val_ref[...]
    packed[pl.ds(7, owners, stride=8), :] = prec_ref[...]
    ones = jnp.ones((hid - 3 * CP, (height + 2) * LANES), BF16)
    s1[pl.ds(3 * CP, hid - 3 * CP), :] = ones
    s2[pl.ds(3 * CP, hid - 3 * CP), :] = ones
    lane = lane_iota(CP)
    first_lane = lane == 0
    last_lane = lane == LANES - 1

    def block(r):
        return pl.ds((r + 1) * LANES, LANES)

    for r in range(height):
        s1[pl.ds(CP, CP), block(r)] = x32[pl.ds(r, CP, stride=height), :].astype(BF16)

    def guarded(d):
        if d in (UP, UL, UR):
            return pl.when(has_up)
        if d in (DOWN, DL, DR):
            return pl.when(has_down)
        return lambda f: f()

    def send(src, dst, t, d, sends, recvs):
        copy = pltpu.make_async_remote_copy(
            src_ref=src, dst_ref=dst, send_sem=sends.at[t, d], recv_sem=recvs.at[t, opposite[d]],
            device_id=ids[d], device_id_type=MESH,
        )
        guarded(d)(copy.start)

    def wait_recv(dst, t, d, sends, recvs):
        copy = pltpu.make_async_remote_copy(
            src_ref=dst, dst_ref=dst, send_sem=sends.at[t, d], recv_sem=recvs.at[t, d],
            device_id=ids[d], device_id_type=MESH,
        )
        guarded(d)(copy.wait_recv)

    def wait_send(src, t, d, sends, recvs):
        copy = pltpu.make_async_remote_copy(
            src_ref=src, dst_ref=src, send_sem=sends.at[t, d], recv_sem=recvs.at[t, d],
            device_id=ids[d], device_id_type=MESH,
        )
        guarded(d)(copy.wait_send)

    def column_blocks(rows, first_of, last_of):
        to_left = jnp.zeros((CP, LANES), F32)
        to_right = jnp.zeros((CP, LANES), F32)
        for r in range(rows):
            to_left = jnp.where(lane == r, pltpu.roll(first_of(r), r, 1) if r else first_of(r), to_left)
            to_right = jnp.where(lane == r, pltpu.roll(last_of(r), r + 1, 1), to_right)
        return to_left.astype(BF16), to_right.astype(BF16)

    diag_slots = {UL: 0, UR: 1, DL: 2, DR: 3}

    def centre(s, r):
        return s.at[pl.ds(CP, CP), block(r)]

    def state_sources(s, t):
        return {
            UP: centre(s, 0), UL: centre(s, 0), UR: centre(s, 0),
            DOWN: centre(s, height - 1), DL: centre(s, height - 1), DR: centre(s, height - 1),
            LEFT: csend.at[t, 0], RIGHT: csend.at[t, 1],
        }

    def state_targets(s, t):
        table = {UP: centre(s, -1), DOWN: centre(s, height), LEFT: hcol.at[t, 0], RIGHT: hcol.at[t, 1]}
        for d, slot in diag_slots.items():
            table[d] = hdiag.at[t, slot]
        return table

    def send_state(s, t):
        src, dst = state_sources(s, t), state_targets(s, t)
        for d in (UP, DOWN, UL, UR, DL, DR):
            send(src[d], dst[opposite[d]], t, d, fsend, frecv)

        def row(r):
            return s[pl.ds(CP, CP), block(r)].astype(F32)

        to_left, to_right = column_blocks(height, row, row)
        csend[t, 0] = to_left
        csend[t, 1] = to_right
        for d in (LEFT, RIGHT):
            send(src[d], dst[opposite[d]], t, d, fsend, frecv)

    def receive_state(s, t):
        dst = state_targets(s, t)
        for d in range(8):
            wait_recv(dst[d], t, d, fsend, frecv)
        from_left = hcol[t, 0].astype(F32)
        from_right = hcol[t, 1].astype(F32)
        for r in range(height):
            row = s[pl.ds(CP, CP), block(r)].astype(F32)
            lower = jnp.where(
                first_lane, pltpu.roll(from_left, (LANES - r) % LANES, 1) if r else from_left, pltpu.roll(row, 1, 1)
            )
            upper = jnp.where(last_lane, pltpu.roll(from_right, LANES - 1 - r, 1), pltpu.roll(row, LANES - 1, 1))
            s[pl.ds(0, CP), block(r)] = lower.astype(BF16)
            s[pl.ds(2 * CP, CP), block(r)] = upper.astype(BF16)
        for r, there, a, b in ((-1, has_up, UL, UR), (height, has_down, DL, DR)):

            @pl.when(there)
            def _():
                row = s[pl.ds(CP, CP), block(r)].astype(F32)
                lower = jnp.where(last_lane, hdiag[t, diag_slots[a]].astype(F32), row)
                upper = jnp.where(first_lane, hdiag[t, diag_slots[b]].astype(F32), row)
                s[pl.ds(0, CP), block(r)] = pltpu.roll(lower, 1, 1).astype(BF16)
                s[pl.ds(2 * CP, CP), block(r)] = pltpu.roll(upper, LANES - 1, 1).astype(BF16)

            @pl.when(jnp.logical_not(there))
            def _():
                s[pl.ds(0, 3 * CP), block(r)] = jnp.zeros((3 * CP, LANES), BF16)

    def forward_chunk(s, n, slope):
        pre = sum(dot(wt_ref[i], s[:, pl.ds((2 * n + i) * LANES, WIDE)]) for i in range(3))
        cdf = 0.5 * (1.0 + lax.erf(pre * ROOT_HALF))
        slope[:, pl.ds(n * WIDE, WIDE)] = cdf + pre * jnp.exp(-0.5 * pre * pre) * NORM_DENSITY
        update = dot(wo_ref[...], (pre * cdf).astype(BF16))
        return (s[pl.ds(CP, CP), pl.ds((2 * n + 1) * LANES, WIDE)].astype(F32) + update).astype(BF16)

    pl.semaphore_wait(barrier, owners - 1)
    send_state(s1, 0)

    def post(other, where):
        pltpu.make_async_remote_copy(
            src_ref=packed.at[pl.ds(pl.multiple_of(other * 8, 8), 8)],
            dst_ref=recv.at[pl.ds(pl.multiple_of(me * 8, 8), 8)],
            send_sem=psend, recv_sem=precv, device_id=where, device_id_type=MESH,
        ).start()

    to_all(range(n_lat), post)
    mine = pl.ds(pl.multiple_of(me * 8, 8), 8)
    recv[mine, :] = packed[mine, :]

    receive_state(s1, 0)
    for n in range(chunks):
        s2[pl.ds(CP, CP), pl.ds((2 * n + 1) * LANES, WIDE)] = forward_chunk(s1, n, slope1)
    send_state(s2, 1)
    receive_state(s2, 1)
    for n in range(chunks):
        sobs[n] = forward_chunk(s2, n, slope2)

    others = pl.ds(0, (owners - 1) * 8)
    pltpu.make_async_remote_copy(
        src_ref=packed.at[others], dst_ref=recv.at[others], send_sem=psend, recv_sem=precv,
        device_id=ids[RIGHT], device_id_type=MESH,
    ).wait()
    column = lax.broadcasted_iota(jnp.int32, (LANES, LANES), 0).astype(F32)
    channel = lax.broadcasted_iota(jnp.int32, (CP, LANES), 0).astype(F32)

    def estimate(group, carry):
        for u in range(GROUP):
            k = group * GROUP + u
            packet = recv[pl.ds(pl.multiple_of(k * 8, 8), 8), :]
            here, after = column == packet[1:2], column == packet[1:2] + 1.0
            table = jnp.concatenate(
                [
                    jnp.where(here, packet[2:3], jnp.where(after, packet[3:4], 0.0)),
                    jnp.where(here, packet[4:5], jnp.where(after, packet[5:6], 0.0)),
                ],
                axis=0,
            ).astype(BF16)
            bsc[k] = table
            picked = channel == packet[0:1]
            found = dot(sobs[swath_ref[0, k]], table)
            gap = jnp.sum(jnp.where(picked, found, 0.0), axis=0, keepdims=True) - packet[6:7]
            inn[k] = gap
            qsc[k] = jnp.where(picked, packet[7:8] * gap, 0.0).astype(BF16)
        return carry

    lax.fori_loop(0, owners // GROUP, estimate, 0)
    hist[0] = jnp.zeros((CP, WIDE), F32)

    def pull(group, last):
        for u in range(GROUP):
            k = group * GROUP + u
            spot = swath_ref[0, k]
            before = sum(jnp.where(spot == m, last[m], 0) for m in range(chunks))
            share = lax.dot_general(qsc[k], bsc[k], (((1,), (1,)), ((), ())), preferred_element_type=F32)
            hist[k + 1] = hist[before] + share
            last = tuple(jnp.where(spot == m, k + 1, last[m]) for m in range(chunks))
        return last

    last = lax.fori_loop(0, owners // GROUP, pull, (jnp.int32(0),) * chunks)
    inn_recv[me] = inn[me]

    def give_back(other, where):
        pltpu.make_async_remote_copy(
            src_ref=inn.at[other], dst_ref=inn_recv.at[me], send_sem=isend, recv_sem=irecv,
            device_id=where, device_id_type=MESH,
        ).start()

    def tap(i, j, r):
        return ybuf[pl.ds((3 * (i + 1) + j + 1) * CP, CP), pl.ds(r * LANES, LANES)]

    def summed(j, r):
        total = None
        for i in (-1, 0, 1):
            if 0 <= r - i < height:
                part = tap(i, j, r - i)
                total = part if total is None else total + part
        return total

    def rim_sources(t):
        return {
            UP: brow.at[t, 0], UL: brow.at[t, 1], UR: brow.at[t, 2],
            DOWN: brow.at[t, 3], DL: brow.at[t, 4], DR: brow.at[t, 5],
            LEFT: bcol.at[t, 0], RIGHT: bcol.at[t, 1],
        }

    def rim_targets(t):
        table = {UP: rrow.at[t, 0], DOWN: rrow.at[t, 1], LEFT: rcol.at[t, 0], RIGHT: rcol.at[t, 1]}
        for d, slot in diag_slots.items():
            table[d] = rdiag.at[t, slot]
        return table

    pad = jnp.zeros((LANES - CP, WIDE), BF16)

    def backward_step(t, cotangent, slope, meanwhile, finish):
        src, dst = rim_sources(t), rim_targets(t)
        for n in range(chunks):
            rounded = jnp.concatenate([cotangent(n).astype(BF16), pad], axis=0)
            spread = (dot(wot_ref[...], rounded) * slope[:, pl.ds(n * WIDE, WIDE)]).astype(BF16)
            for i in range(3):
                ybuf[pl.ds(3 * i * CP, 3 * CP), pl.ds(n * WIDE, WIDE)] = dot(wk[i, pl.ds(0, 3 * CP), :], spread)

        def inner(t_low, t_mid, t_high):
            return (
                t_mid
                + jnp.where(first_lane, 0.0, pltpu.roll(t_high, 1, 1))
                + jnp.where(last_lane, 0.0, pltpu.roll(t_low, LANES - 1, 1))
            )

        for r, at in ((-1, 0), (height, 3)):
            t_low, t_mid, t_high = (summed(j, r) for j in (-1, 0, 1))
            brow[t, at] = inner(t_low, t_mid, t_high).astype(BF16)
            brow[t, at + 1] = t_low.astype(BF16)
            brow[t, at + 2] = t_high.astype(BF16)
        for d in (UP, DOWN, UL, UR, DL, DR):
            send(src[d], dst[opposite[d]], t, d, bsend, brecv)
        to_left, to_right = column_blocks(height, lambda r: summed(-1, r), lambda r: summed(1, r))
        bcol[t, 0] = to_left
        bcol[t, 1] = to_right
        for d in (LEFT, RIGHT):
            send(src[d], dst[opposite[d]], t, d, bsend, brecv)
        to_all(meanwhile, give_back)
        for r in range(height):
            ubuf[:, pl.ds(r * LANES, LANES)] = inner(summed(-1, r), summed(0, r), summed(1, r)) + cotangent(r // 2)[
                :, (r % 2) * LANES : (r % 2 + 1) * LANES
            ]
        for d in range(8):
            wait_recv(dst[d], t, d, bsend, brecv)
        for r, there, at, a, b in ((0, has_up, 0, UL, UR), (height - 1, has_down, 1, DL, DR)):

            @pl.when(there)
            def _():
                ubuf[:, pl.ds(r * LANES, LANES)] = (
                    ubuf[:, pl.ds(r * LANES, LANES)]
                    + rrow[t, at].astype(F32)
                    + jnp.where(first_lane, pltpu.roll(rdiag[t, diag_slots[a]].astype(F32), 1, 1), 0.0)
                    + jnp.where(last_lane, pltpu.roll(rdiag[t, diag_slots[b]].astype(F32), LANES - 1, 1), 0.0)
                )

        from_left = rcol[t, 0].astype(F32)
        from_right = rcol[t, 1].astype(F32)
        for r in range(height):
            finish(
                r,
                ubuf[:, pl.ds(r * LANES, LANES)]
                + jnp.where(first_lane, pltpu.roll(from_left, (LANES - r) % LANES, 1) if r else from_left, 0.0)
                + jnp.where(last_lane, pltpu.roll(from_right, LANES - 1 - r, 1), 0.0),
            )

    def keep(r, value):
        gbuf[:, pl.ds(r * LANES, LANES)] = value

    def write(r, value):
        here = pl.ds(r, chan, stride=height)
        grad_ref[here, :] = grad_ref[here, :] + value[:chan]

    backward_step(0, lambda n: hist[last[n]], slope2, range(n_lat - 1), keep)
    backward_step(1, lambda n: gbuf[:, pl.ds(n * WIDE, WIDE)], slope1, range(n_lat - 1, n_lat), write)

    rows = pl.ds(0, owners - 1)
    pltpu.make_async_remote_copy(
        src_ref=inn.at[rows], dst_ref=inn_recv.at[rows], send_sem=isend, recv_sem=irecv,
        device_id=ids[RIGHT], device_id_type=MESH,
    ).wait()
    innov_ref[...] = inn_recv[...].reshape(owners, LANES)
    for t, s in enumerate((s1, s2)):
        src = state_sources(s, t)
        for d in range(8):
            wait_send(src[d], t, d, fsend, frecv)
    for t in range(2):
        src = rim_sources(t)
        for d in range(8):
            wait_send(src[d], t, d, bsend, brecv)


def local(
    n_lat, n_lon,
    initial_state, background_state, background_precision, conv_weight, conv_bias, out_weight,
    swath_patch, obs_cell, obs_weights, obs_value, obs_precision,
):
    chan, height, breadth = initial_state.shape
    hid = conv_weight.shape[2]
    owners = n_lat * n_lon
    chunks = height // 2
    cells = height * breadth
    vmem = pl.BlockSpec(memory_space=pltpu.VMEM)
    smem = pl.BlockSpec(memory_space=pltpu.SMEM)
    dma = pltpu.SemaphoreType.DMA
    gradient, innov = pl.pallas_call(
        functools.partial(kernel, n_lat, n_lon, hid),
        out_shape=(
            jax.ShapeDtypeStruct((chan * height, LANES), F32),
            jax.ShapeDtypeStruct((owners, LANES), F32),
        ),
        in_specs=[vmem, vmem, smem, vmem, vmem, vmem, smem] + [vmem] * 4,
        out_specs=(vmem, vmem),
        scratch_shapes=[
            pltpu.VMEM((LANES, hid), F32),
            pltpu.VMEM((3, hid, hid), BF16),
            pltpu.VMEM((3, hid, hid), BF16),
            pltpu.VMEM((CP, hid), BF16),
            pltpu.VMEM((hid, LANES), BF16),
            pltpu.VMEM((CP * height, LANES), F32),
            pltpu.VMEM((owners * 8, LANES), F32),
            pltpu.VMEM((owners * 8, LANES), F32),
            pltpu.VMEM((hid, (height + 2) * LANES), BF16),
            pltpu.VMEM((hid, (height + 2) * LANES), BF16),
            pltpu.VMEM((chunks, CP, WIDE), BF16),
            pltpu.VMEM((hid, cells), F32),
            pltpu.VMEM((hid, cells), F32),
            pltpu.VMEM((2, 2, CP, LANES), BF16),
            pltpu.VMEM((2, 2, CP, LANES), BF16),
            pltpu.VMEM((2, 4, CP, LANES), BF16),
            pltpu.VMEM((owners, WIDE, LANES), BF16),
            pltpu.VMEM((owners, CP, LANES), BF16),
            pltpu.VMEM((owners, 1, LANES), F32),
            pltpu.VMEM((owners, 1, LANES), F32),
            pltpu.VMEM((owners + 1, CP, WIDE), F32),
            pltpu.VMEM((9 * CP, cells), F32),
            pltpu.VMEM((CP, cells), F32),
            pltpu.VMEM((CP, cells), F32),
            pltpu.VMEM((2, 6, CP, LANES), BF16),
            pltpu.VMEM((2, 2, CP, LANES), BF16),
            pltpu.VMEM((2, 2, CP, LANES), BF16),
            pltpu.VMEM((2, 4, CP, LANES), BF16),
            pltpu.VMEM((2, 2, CP, LANES), BF16),
            dma((2, 8)), dma((2, 8)), dma((2, 8)), dma((2, 8)),
            dma, dma, dma, dma,
        ],
        compiler_params=pltpu.CompilerParams(
            collective_id=0, has_side_effects=True, vmem_limit_bytes=56 * 1024 * 1024
        ),
    )(
        initial_state, background_state, background_precision[None], conv_weight, conv_bias[None], out_weight, swath_patch,
        obs_cell[0], obs_weights[:, 0], obs_value[0], obs_precision[0],
    )
    return gradient.reshape(chan, height, breadth), innov[None]


def solution(mesh):
    tile = P(None, "lat", "lon")
    owner = ("lat", "lon")
    in_specs = (
        tile, tile, P(), P(), P(), P(),
        P(owner, None), P(owner, None, None), P(None, owner, None, None), P(owner, None, None), P(owner, None, None),
    )
    return jax.shard_map(
        functools.partial(local, mesh.shape["lat"], mesh.shape["lon"]),
        mesh=mesh, in_specs=in_specs, out_specs=(tile, P(owner, None, None)), check_vma=False,
    )
```

```python
import functools

import jax
import jax.numpy as jnp
from jax import lax
from jax.experimental import pallas as pl
from jax.experimental.pallas import tpu as pltpu
from jax.sharding import PartitionSpec as P

MESH = pl.DeviceIdType.MESH
F32 = jnp.float32
BF16 = jnp.bfloat16
CP = 80
LANES = 128
WIDE = 256
ROOT_HALF = 0.7071067811865476
NORM_DENSITY = 0.3989422804014327
UP, DOWN, LEFT, RIGHT, UL, UR, DL, DR = range(8)
GROUP = 16


def dot(a, b):
    return jnp.dot(a, b, preferred_element_type=F32)


def lane_iota(rows):
    return lax.broadcasted_iota(jnp.int32, (rows, LANES), 1)


def kernel(
    n_lat, n_lon, hid,
    x_hbm, xb_hbm, bp_ref, cw_ref, cb_ref, ow_ref, swath_ref, cell_hbm, w_hbm, val_hbm, prec_hbm,
    grad_ref, innov_ref,
    x_ref, xb_ref, cell_ref, w_ref, val_ref, prec_ref, wpad, wk, wt_ref, wo_ref, wot_ref, x32, packed, recv, s1, s2, se, sobs, slope1, slope2, csend, hcol,
    bsc, qsc, inn, inn_recv, hist, ybuf, ubuf, gbuf, brow, bcol, rrow, rdiag, rcol,
    fsend, frecv, bsend, brecv, psend, precv, isend, irecv, loaded,
):
    chan, height = x_ref.shape[0], x_ref.shape[1]
    owners = n_lat * n_lon
    chunks = height // 2
    lat = lax.axis_index("lat")
    lon = lax.axis_index("lon")
    me = lat * n_lon + lon
    has_up = lat > 0
    has_down = lat < n_lat - 1
    left = lax.rem(lon + n_lon - 1, n_lon)
    right = lax.rem(lon + 1, n_lon)
    ids = {
        UP: (lat - 1, lon), DOWN: (lat + 1, lon), LEFT: (lat, left), RIGHT: (lat, right),
        UL: (lat - 1, left), UR: (lat - 1, right), DL: (lat + 1, left), DR: (lat + 1, right),
    }
    opposite = {UP: DOWN, DOWN: UP, LEFT: RIGHT, RIGHT: LEFT, UL: DR, DR: UL, UR: DL, DL: UR}

    barrier = pltpu.get_barrier_semaphore()

    def wrapped(value, count):
        return value - jnp.where(value >= count, count, 0)

    def to_all(steps, act):
        for step in steps:
            there = wrapped(lat + step, n_lat)

            def one(ahead, carry, there=there):
                column = wrapped(lon + ahead, n_lon)
                act(there * n_lon + column, (there, column))
                return carry

            lax.fori_loop(0 if step else 1, n_lon, one, 0, unroll=4 if step else 1)

    def greet(_, where):
        pl.semaphore_signal(barrier, inc=1, device_id=where, device_id_type=MESH)

    loads = [
        pltpu.make_async_copy(src, dst, loaded.at[k])
        for k, (src, dst) in enumerate(
            (
                (x_hbm, x_ref), (xb_hbm, xb_ref), (cell_hbm, cell_ref),
                (w_hbm, w_ref), (val_hbm, val_ref), (prec_hbm, prec_ref),
            )
        )
    ]
    for load in loads:
        load.start()
    to_all(range(n_lat), greet)

    x32[pl.ds(chan * height, (CP - chan) * height), :] = jnp.zeros(((CP - chan) * height, LANES), F32)
    for load in loads:
        load.wait()
    for c in range(chan):
        grad_ref[pl.ds(c * height, height), :] = bp_ref[0, c] * (x_ref[c].astype(F32) - xb_ref[c].astype(F32))
    x32[pl.ds(0, chan * height), :] = x_ref[...].astype(F32).reshape(chan * height, LANES)
    cell = cell_ref[...]
    packed[pl.ds(0, owners, stride=8), :] = (cell // WIDE).astype(F32)
    packed[pl.ds(1, owners, stride=8), :] = (cell % LANES).astype(F32)
    for k in range(4):
        packed[pl.ds(2 + k, owners, stride=8), :] = w_ref[k]
    packed[pl.ds(6, owners, stride=8), :] = val_ref[...]
    packed[pl.ds(7, owners, stride=8), :] = prec_ref[...]
    wpad[...] = jnp.zeros((LANES, hid), F32)
    bias = cb_ref[...]
    bias_parts = []
    for _ in range(3):
        part = bias.astype(BF16).astype(F32)
        bias_parts.append(part)
        bias = bias - part
    spare = lax.broadcasted_iota(jnp.int32, (hid - 3 * CP, hid), 0)
    bias_rows = jnp.zeros((hid - 3 * CP, hid), F32)
    for k, part in enumerate(bias_parts):
        bias_rows = jnp.where(spare == k, part, bias_rows)
    for i in range(3):
        for j in range(3):
            wpad[pl.ds(0, chan), :] = cw_ref[3 * i + j].astype(F32)
            wk[i, pl.ds(j * CP, CP), :] = wpad[pl.ds(0, CP), :].astype(BF16)
        wk[i, pl.ds(3 * CP, hid - 3 * CP), :] = (bias_rows if i == 1 else jnp.zeros_like(bias_rows)).astype(BF16)
        wt_ref[i] = jnp.transpose(wk[i].astype(F32)).astype(BF16)
    wpad[pl.ds(0, chan), :] = ow_ref[...].astype(F32)
    wo_ref[...] = wpad[pl.ds(0, CP), :].astype(BF16)
    wot_ref[...] = jnp.transpose(wpad[...]).astype(BF16)
    def ones(breadth):
        return jnp.ones((hid - 3 * CP, breadth), BF16)

    s1[pl.ds(3 * CP, hid - 3 * CP), :] = ones((height + 4) * LANES)
    s2[pl.ds(3 * CP, hid - 3 * CP), :] = ones((height + 2) * LANES)
    for i in range(3):
        se[i, pl.ds(3 * CP, hid - 3 * CP), :] = ones(LANES)
    lane = lane_iota(CP)
    first_lane = lane == 0
    last_lane = lane == LANES - 1

    def block(rim, r, count=1):
        return pl.ds((r + rim) * LANES, count * LANES)

    def rolled(value, shift):
        return pltpu.roll(value, shift % LANES, 1) if shift % LANES else value

    def spot(r):
        return 2 * (r + 2)

    pair_of = lane // 2
    to_left = jnp.zeros((CP, LANES), F32)
    to_right = jnp.zeros((CP, LANES), F32)
    for r in range(height):
        row = x32[pl.ds(r, CP, stride=height), :]
        s1[pl.ds(CP, CP), block(2, r)] = row.astype(BF16)
        to_left = jnp.where(pair_of == r + 2, rolled(row, spot(r)), to_left)
        to_right = jnp.where(pair_of == r + 2, rolled(row, spot(r) + 2), to_right)
    csend[0] = to_left.astype(BF16)
    csend[1] = to_right.astype(BF16)

    def guarded(d):
        if d in (UP, UL, UR):
            return pl.when(has_up)
        if d in (DOWN, DL, DR):
            return pl.when(has_down)
        return lambda f: f()

    def send(src, dst, t, d, sends, recvs):
        copy = pltpu.make_async_remote_copy(
            src_ref=src, dst_ref=dst, send_sem=sends.at[t, d], recv_sem=recvs.at[t, opposite[d]],
            device_id=ids[d], device_id_type=MESH,
        )
        guarded(d)(copy.start)

    def wait_recv(dst, t, d, sends, recvs):
        copy = pltpu.make_async_remote_copy(
            src_ref=dst, dst_ref=dst, send_sem=sends.at[t, d], recv_sem=recvs.at[t, d],
            device_id=ids[d], device_id_type=MESH,
        )
        guarded(d)(copy.wait_recv)

    def wait_send(src, t, d, sends, recvs):
        copy = pltpu.make_async_remote_copy(
            src_ref=src, dst_ref=src, send_sem=sends.at[t, d], recv_sem=recvs.at[t, d],
            device_id=ids[d], device_id_type=MESH,
        )
        guarded(d)(copy.wait_send)

    def column_blocks(rows, first_of, last_of):
        to_left = jnp.zeros((CP, LANES), F32)
        to_right = jnp.zeros((CP, LANES), F32)
        for r in range(rows):
            to_left = jnp.where(lane == r, pltpu.roll(first_of(r), r, 1) if r else first_of(r), to_left)
            to_right = jnp.where(lane == r, pltpu.roll(last_of(r), r + 1, 1), to_right)
        return to_left.astype(BF16), to_right.astype(BF16)

    diag_slots = {UL: 0, UR: 1, DL: 2, DR: 3}

    def pair(r):
        return s1.at[pl.ds(CP, CP), block(2, r, 2)]

    state_sources = {
        UP: pair(0), DOWN: pair(height - 2),
        LEFT: csend.at[0], UL: csend.at[0], DL: csend.at[0],
        RIGHT: csend.at[1], UR: csend.at[1], DR: csend.at[1],
    }
    state_targets = {UP: pair(-2), DOWN: pair(height)}
    for k, d in enumerate((LEFT, RIGHT, UL, UR, DL, DR)):
        state_targets[d] = hcol.at[k]

    def send_state():
        for d in (UP, DOWN, LEFT, RIGHT, UL, UR, DL, DR):
            send(state_sources[d], state_targets[opposite[d]], 0, d, fsend, frecv)

    def receive_state():
        for d in range(8):
            wait_recv(state_targets[d], 0, d, fsend, frecv)
        for there, r, slots in ((has_up, -2, (2, 3)), (has_down, height, (4, 5))):

            @pl.when(jnp.logical_not(there))
            def _():
                s1[pl.ds(CP, CP), block(2, r, 2)] = jnp.zeros((CP, WIDE), BF16)
                for slot in slots:
                    hcol[slot] = jnp.zeros((CP, LANES), BF16)

    def shift_rows(s, rim, rows, low, low_lane, high, high_lane):
        for r in rows:
            row = s[pl.ds(CP, CP), block(rim, r)].astype(F32)
            lower = jnp.where(first_lane, rolled(low, -low_lane(r)), rolled(row, 1))
            upper = jnp.where(last_lane, rolled(high, LANES - 1 - high_lane(r)), rolled(row, -1))
            s[pl.ds(0, CP), block(rim, r)] = lower.astype(BF16)
            s[pl.ds(2 * CP, CP), block(rim, r)] = upper.astype(BF16)

    def with_corners(side, above, below):
        middle = jnp.logical_and(pair_of >= 2, pair_of < height + 2)
        outer = jnp.where(pair_of < 2, rolled(above, -2 * height), rolled(below, 2 * height))
        return jnp.where(middle, side, outer)

    def spread_columns():
        from_left, from_right, ul, ur, dl, dr = (hcol[k].astype(F32) for k in range(6))
        low = with_corners(from_left, ul, dl)
        high = with_corners(from_right, ur, dr)
        first = csend[0].astype(F32)
        last = rolled(csend[1].astype(F32), -1)
        for r in (-2, -1, height, height + 1):
            row = s1[pl.ds(CP, CP), block(2, r)].astype(F32)
            first = jnp.where(lane == spot(r), rolled(row, spot(r)), first)
            last = jnp.where(lane == spot(r), rolled(row, spot(r) + 1), last)
        on_left = lane < LANES // 2
        taps = (
            jnp.where(on_left, low, rolled(last, LANES // 2)),
            jnp.where(on_left, rolled(low, -1), rolled(high, LANES // 2)),
            jnp.where(on_left, first, rolled(high, LANES // 2 - 1)),
        )
        for i in range(3):
            for j in range(3):
                se[i, pl.ds(j * CP, CP), :] = rolled(taps[j], 2 * (1 - i)).astype(BF16)
        return low, high, taps[1]

    def network(window, centre):
        pre = sum(dot(wt_ref[i], window(i)) for i in range(3))
        cdf = 0.5 * (1.0 + lax.erf(pre * ROOT_HALF))
        update = dot(wo_ref[...], (pre * cdf).astype(BF16))
        return centre.astype(F32) + update, lambda: cdf + pre * jnp.exp(-0.5 * pre * pre) * NORM_DENSITY

    def forward_chunk(s, rim, n, slope):
        state, tangent = network(
            lambda i: s[:, block(rim, 2 * n + i - 1, 2)], s[pl.ds(CP, CP), block(rim, 2 * n, 2)]
        )
        slope[:, pl.ds(n * WIDE, WIDE)] = tangent()
        return state.astype(BF16)

    def first_rim(centre):
        up, down = has_up.astype(F32), has_down.astype(F32)
        rows = (-1, height)
        state, _ = network(
            lambda i: jnp.concatenate([s1[:, block(2, r + i - 1)] for r in rows], axis=1),
            jnp.concatenate([s1[pl.ds(CP, CP), block(2, r)] for r in rows], axis=1),
        )
        s2[pl.ds(CP, CP), block(1, -1)] = (state[:, :LANES] * up).astype(BF16)
        s2[pl.ds(CP, CP), block(1, height)] = (state[:, LANES:] * down).astype(BF16)
        sides, _ = network(lambda i: se[i], centre)
        place = lax.rem(lane, LANES // 2)
        inside = jnp.where(place == spot(-1), up, jnp.where(place == spot(height), down, 1.0))
        return (sides * inside).astype(BF16).astype(F32)

    pl.semaphore_wait(barrier, owners - 1)
    send_state()

    def post(other, where):
        pltpu.make_async_remote_copy(
            src_ref=packed.at[pl.ds(pl.multiple_of(other * 8, 8), 8)],
            dst_ref=recv.at[pl.ds(pl.multiple_of(me * 8, 8), 8)],
            send_sem=psend, recv_sem=precv, device_id=where, device_id_type=MESH,
        ).start()

    to_all(range(n_lat), post)
    mine = pl.ds(pl.multiple_of(me * 8, 8), 8)
    recv[mine, :] = packed[mine, :]

    receive_state()
    low, high, beside = spread_columns()
    shift_rows(s1, 2, range(-2, height + 2), low, lambda r: spot(r) + 1, high, spot)
    for n in range(chunks):
        s2[pl.ds(CP, CP), block(1, 2 * n, 2)] = forward_chunk(s1, 2, n, slope1)
    sides = first_rim(beside)
    shift_rows(s2, 1, range(-1, height + 1), sides, spot, sides, lambda r: LANES // 2 + spot(r))
    for n in range(chunks):
        sobs[n] = forward_chunk(s2, 1, n, slope2)

    others = pl.ds(0, (owners - 1) * 8)
    pltpu.make_async_remote_copy(
        src_ref=packed.at[others], dst_ref=recv.at[others], send_sem=psend, recv_sem=precv,
        device_id=ids[RIGHT], device_id_type=MESH,
    ).wait()
    column = lax.broadcasted_iota(jnp.int32, (LANES, LANES), 0).astype(F32)
    channel = lax.broadcasted_iota(jnp.int32, (CP, LANES), 0).astype(F32)

    def estimate(group, carry):
        for u in range(GROUP):
            k = group * GROUP + u
            packet = recv[pl.ds(pl.multiple_of(k * 8, 8), 8), :]
            here, after = column == packet[1:2], column == packet[1:2] + 1.0
            table = jnp.concatenate(
                [
                    jnp.where(here, packet[2:3], jnp.where(after, packet[3:4], 0.0)),
                    jnp.where(here, packet[4:5], jnp.where(after, packet[5:6], 0.0)),
                ],
                axis=0,
            ).astype(BF16)
            bsc[k] = table
            picked = channel == packet[0:1]
            found = dot(sobs[swath_ref[0, k]], table)
            gap = jnp.sum(jnp.where(picked, found, 0.0), axis=0, keepdims=True) - packet[6:7]
            inn[k] = gap
            qsc[k] = jnp.where(picked, packet[7:8] * gap, 0.0).astype(BF16)
        return carry

    lax.fori_loop(0, owners // GROUP, estimate, 0)
    hist[0] = jnp.zeros((CP, WIDE), F32)

    def pull(group, last):
        for u in range(GROUP):
            k = group * GROUP + u
            patch = swath_ref[0, k]
            before = sum(jnp.where(patch == m, last[m], 0) for m in range(chunks))
            share = lax.dot_general(qsc[k], bsc[k], (((1,), (1,)), ((), ())), preferred_element_type=F32)
            hist[k + 1] = hist[before] + share
            last = tuple(jnp.where(patch == m, k + 1, last[m]) for m in range(chunks))
        return last

    last = lax.fori_loop(0, owners // GROUP, pull, (jnp.int32(0),) * chunks)
    inn_recv[me] = inn[me]

    def give_back(other, where):
        pltpu.make_async_remote_copy(
            src_ref=inn.at[other], dst_ref=inn_recv.at[me], send_sem=isend, recv_sem=irecv,
            device_id=where, device_id_type=MESH,
        ).start()

    def tap(i, j, r):
        return ybuf[pl.ds((3 * (i + 1) + j + 1) * CP, CP), pl.ds(r * LANES, LANES)]

    def summed(j, r):
        total = None
        for i in (-1, 0, 1):
            if 0 <= r - i < height:
                part = tap(i, j, r - i)
                total = part if total is None else total + part
        return total

    def rim_sources(t):
        return {
            UP: brow.at[t, 0], UL: brow.at[t, 1], UR: brow.at[t, 2],
            DOWN: brow.at[t, 3], DL: brow.at[t, 4], DR: brow.at[t, 5],
            LEFT: bcol.at[t, 0], RIGHT: bcol.at[t, 1],
        }

    def rim_targets(t):
        table = {UP: rrow.at[t, 0], DOWN: rrow.at[t, 1], LEFT: rcol.at[t, 0], RIGHT: rcol.at[t, 1]}
        for d, slot in diag_slots.items():
            table[d] = rdiag.at[t, slot]
        return table

    pad = jnp.zeros((LANES - CP, WIDE), BF16)

    def backward_step(t, cotangent, slope, meanwhile, finish):
        src, dst = rim_sources(t), rim_targets(t)
        for n in range(chunks):
            rounded = jnp.concatenate([cotangent(n).astype(BF16), pad], axis=0)
            spread = (dot(wot_ref[...], rounded) * slope[:, pl.ds(n * WIDE, WIDE)]).astype(BF16)
            for i in range(3):
                ybuf[pl.ds(3 * i * CP, 3 * CP), pl.ds(n * WIDE, WIDE)] = dot(wk[i, pl.ds(0, 3 * CP), :], spread)

        def inner(t_low, t_mid, t_high):
            return (
                t_mid
                + jnp.where(first_lane, 0.0, pltpu.roll(t_high, 1, 1))
                + jnp.where(last_lane, 0.0, pltpu.roll(t_low, LANES - 1, 1))
            )

        for r, at in ((-1, 0), (height, 3)):
            t_low, t_mid, t_high = (summed(j, r) for j in (-1, 0, 1))
            brow[t, at] = inner(t_low, t_mid, t_high).astype(BF16)
            brow[t, at + 1] = t_low.astype(BF16)
            brow[t, at + 2] = t_high.astype(BF16)
        for d in (UP, DOWN, UL, UR, DL, DR):
            send(src[d], dst[opposite[d]], t, d, bsend, brecv)
        to_left, to_right = column_blocks(height, lambda r: summed(-1, r), lambda r: summed(1, r))
        bcol[t, 0] = to_left
        bcol[t, 1] = to_right
        for d in (LEFT, RIGHT):
            send(src[d], dst[opposite[d]], t, d, bsend, brecv)
        to_all(meanwhile, give_back)
        for r in range(height):
            ubuf[:, pl.ds(r * LANES, LANES)] = inner(summed(-1, r), summed(0, r), summed(1, r)) + cotangent(r // 2)[
                :, (r % 2) * LANES : (r % 2 + 1) * LANES
            ]
        for d in range(8):
            wait_recv(dst[d], t, d, bsend, brecv)
        for r, there, at, a, b in ((0, has_up, 0, UL, UR), (height - 1, has_down, 1, DL, DR)):

            @pl.when(there)
            def _():
                ubuf[:, pl.ds(r * LANES, LANES)] = (
                    ubuf[:, pl.ds(r * LANES, LANES)]
                    + rrow[t, at].astype(F32)
                    + jnp.where(first_lane, pltpu.roll(rdiag[t, diag_slots[a]].astype(F32), 1, 1), 0.0)
                    + jnp.where(last_lane, pltpu.roll(rdiag[t, diag_slots[b]].astype(F32), LANES - 1, 1), 0.0)
                )

        from_left = rcol[t, 0].astype(F32)
        from_right = rcol[t, 1].astype(F32)
        for r in range(height):
            finish(
                r,
                ubuf[:, pl.ds(r * LANES, LANES)]
                + jnp.where(first_lane, pltpu.roll(from_left, (LANES - r) % LANES, 1) if r else from_left, 0.0)
                + jnp.where(last_lane, pltpu.roll(from_right, LANES - 1 - r, 1), 0.0),
            )

    def keep(r, value):
        gbuf[:, pl.ds(r * LANES, LANES)] = value

    def write(r, value):
        here = pl.ds(r, chan, stride=height)
        grad_ref[here, :] = grad_ref[here, :] + value[:chan]

    backward_step(0, lambda n: hist[last[n]], slope2, range(n_lat - 1), keep)
    backward_step(1, lambda n: gbuf[:, pl.ds(n * WIDE, WIDE)], slope1, range(n_lat - 1, n_lat), write)

    rows = pl.ds(0, owners - 1)
    pltpu.make_async_remote_copy(
        src_ref=inn.at[rows], dst_ref=inn_recv.at[rows], send_sem=isend, recv_sem=irecv,
        device_id=ids[RIGHT], device_id_type=MESH,
    ).wait()
    innov_ref[...] = inn_recv[...].reshape(owners, LANES)
    for d in range(8):
        wait_send(state_sources[d], 0, d, fsend, frecv)
    for t in range(2):
        src = rim_sources(t)
        for d in range(8):
            wait_send(src[d], t, d, bsend, brecv)


def hand_over(gradient_in, innov_in, gradient_out, innov_out, sems):
    copies = [
        pltpu.make_async_copy(gradient_in, gradient_out, sems.at[0]),
        pltpu.make_async_copy(innov_in, innov_out, sems.at[1]),
    ]
    for copy in copies:
        copy.start()
    for copy in copies:
        copy.wait()


def local(
    n_lat, n_lon,
    initial_state, background_state, background_precision, conv_weight, conv_bias, out_weight,
    swath_patch, obs_cell, obs_weights, obs_value, obs_precision,
):
    chan, height, breadth = initial_state.shape
    hid = conv_weight.shape[2]
    owners = n_lat * n_lon
    chunks = height // 2
    cells = height * breadth
    vmem = pl.BlockSpec(memory_space=pltpu.VMEM)
    hbm = pl.BlockSpec(memory_space=pltpu.HBM)
    smem = pl.BlockSpec(memory_space=pltpu.SMEM)
    dma = pltpu.SemaphoreType.DMA
    gradient, innov = pl.pallas_call(
        functools.partial(kernel, n_lat, n_lon, hid),
        out_shape=(
            jax.ShapeDtypeStruct((chan * height, LANES), F32),
            jax.ShapeDtypeStruct((owners, LANES), F32),
        ),
        in_specs=[hbm, hbm, smem, vmem, vmem, vmem, smem] + [hbm] * 4,
        out_specs=(vmem, vmem),
        scratch_shapes=[
            pltpu.VMEM((chan, height, breadth), BF16),
            pltpu.VMEM((chan, height, breadth), BF16),
            pltpu.VMEM((owners, LANES), jnp.int32),
            pltpu.VMEM((4, owners, LANES), F32),
            pltpu.VMEM((owners, LANES), F32),
            pltpu.VMEM((owners, LANES), F32),
            pltpu.VMEM((LANES, hid), F32),
            pltpu.VMEM((3, hid, hid), BF16),
            pltpu.VMEM((3, hid, hid), BF16),
            pltpu.VMEM((CP, hid), BF16),
            pltpu.VMEM((hid, LANES), BF16),
            pltpu.VMEM((CP * height, LANES), F32),
            pltpu.VMEM((owners * 8, LANES), F32),
            pltpu.VMEM((owners * 8, LANES), F32),
            pltpu.VMEM((hid, (height + 4) * LANES), BF16),
            pltpu.VMEM((hid, (height + 2) * LANES), BF16),
            pltpu.VMEM((3, hid, LANES), BF16),
            pltpu.VMEM((chunks, CP, WIDE), BF16),
            pltpu.VMEM((hid, cells), F32),
            pltpu.VMEM((hid, cells), F32),
            pltpu.VMEM((2, CP, LANES), BF16),
            pltpu.VMEM((6, CP, LANES), BF16),
            pltpu.VMEM((owners, WIDE, LANES), BF16),
            pltpu.VMEM((owners, CP, LANES), BF16),
            pltpu.VMEM((owners, 1, LANES), F32),
            pltpu.VMEM((owners, 1, LANES), F32),
            pltpu.VMEM((owners + 1, CP, WIDE), F32),
            pltpu.VMEM((9 * CP, cells), F32),
            pltpu.VMEM((CP, cells), F32),
            pltpu.VMEM((CP, cells), F32),
            pltpu.VMEM((2, 6, CP, LANES), BF16),
            pltpu.VMEM((2, 2, CP, LANES), BF16),
            pltpu.VMEM((2, 2, CP, LANES), BF16),
            pltpu.VMEM((2, 4, CP, LANES), BF16),
            pltpu.VMEM((2, 2, CP, LANES), BF16),
            dma((1, 8)), dma((1, 8)), dma((2, 8)), dma((2, 8)),
            dma, dma, dma, dma, dma((6,)),
        ],
        compiler_params=pltpu.CompilerParams(
            collective_id=0, has_side_effects=True, vmem_limit_bytes=56 * 1024 * 1024
        ),
    )(
        initial_state, background_state, background_precision[None], conv_weight, conv_bias[None], out_weight, swath_patch,
        obs_cell[0], obs_weights[:, 0], obs_value[0], obs_precision[0],
    )
    return pl.pallas_call(
        hand_over,
        out_shape=(
            jax.ShapeDtypeStruct((chan, height, breadth), F32),
            jax.ShapeDtypeStruct((1, owners, LANES), F32),
        ),
        in_specs=[hbm, hbm],
        out_specs=(hbm, hbm),
        scratch_shapes=[dma((2,))],
        compiler_params=pltpu.CompilerParams(vmem_limit_bytes=56 * 1024 * 1024),
    )(gradient.reshape(chan, height, breadth), innov[None])


def solution(mesh):
    tile = P(None, "lat", "lon")
    owner = ("lat", "lon")
    in_specs = (
        tile, tile, P(), P(), P(), P(),
        P(owner, None), P(owner, None, None), P(None, owner, None, None), P(owner, None, None), P(owner, None, None),
    )
    return jax.shard_map(
        functools.partial(local, mesh.shape["lat"], mesh.shape["lon"]),
        mesh=mesh, in_specs=in_specs, out_specs=(tile, P(owner, None, None)), check_vma=False,
    )
```

```python
import functools

import jax
import jax.numpy as jnp
from jax import lax
from jax.experimental import pallas as pl
from jax.experimental.pallas import tpu as pltpu
from jax.sharding import PartitionSpec as P

MESH = pl.DeviceIdType.MESH
F32 = jnp.float32
BF16 = jnp.bfloat16
CP = 80
LANES = 128
WIDE = 256
ROOT_HALF = 0.7071067811865476
NORM_DENSITY = 0.3989422804014327
UP, DOWN, LEFT, RIGHT, UL, UR, DL, DR = range(8)
GROUP = 16
PIECES = 3


def dot(a, b):
    return jnp.dot(a, b, preferred_element_type=F32)


def lane_iota(rows):
    return lax.broadcasted_iota(jnp.int32, (rows, LANES), 1)


def kernel(
    n_lat, n_lon, hid,
    x_hbm, xb_hbm, bp_ref, cw_ref, cb_ref, ow_ref, swath_ref, cell_hbm, w_hbm, val_hbm, prec_hbm,
    grad_ref, innov_ref,
    x_ref, xb_ref, cell_ref, w_ref, val_ref, prec_ref, wpad, wk, wt_ref, wo_ref, wot_ref, x32, packed, recv, s1, s2, se, sobs, slope1, slope2, csend, hcol,
    bsc, qsc, inn, inn_recv, hist, ybuf, ubuf, gbuf, brow, bcol, rrow, rdiag, rcol,
    fsend, frecv, bsend, brecv, psend, precv, isend, irecv, loaded,
):
    chan, height = x_ref.shape[0], x_ref.shape[1]
    owners = n_lat * n_lon
    chunks = height // 2
    lat = lax.axis_index("lat")
    lon = lax.axis_index("lon")
    me = lat * n_lon + lon
    has_up = lat > 0
    has_down = lat < n_lat - 1
    left = lax.rem(lon + n_lon - 1, n_lon)
    right = lax.rem(lon + 1, n_lon)
    ids = {
        UP: (lat - 1, lon), DOWN: (lat + 1, lon), LEFT: (lat, left), RIGHT: (lat, right),
        UL: (lat - 1, left), UR: (lat - 1, right), DL: (lat + 1, left), DR: (lat + 1, right),
    }
    opposite = {UP: DOWN, DOWN: UP, LEFT: RIGHT, RIGHT: LEFT, UL: DR, DR: UL, UR: DL, DL: UR}

    barrier = pltpu.get_barrier_semaphore()

    def wrapped(value, count):
        return value - jnp.where(value >= count, count, 0)

    rounds = [(step, ahead) for step in range(n_lat) for ahead in range(n_lon) if step or ahead]

    def to_some(part, parts, act):
        for step, ahead in rounds[len(rounds) * part // parts : len(rounds) * (part + 1) // parts]:
            there, column = wrapped(lat + step, n_lat), wrapped(lon + ahead, n_lon)
            act(there * n_lon + column, (there, column))

    def greet(_, where):
        pl.semaphore_signal(barrier, inc=1, device_id=where, device_id_type=MESH)

    loads = [
        pltpu.make_async_copy(src, dst, loaded.at[k])
        for k, (src, dst) in enumerate(
            (
                (x_hbm, x_ref), (xb_hbm, xb_ref), (cell_hbm, cell_ref),
                (w_hbm, w_ref), (val_hbm, val_ref), (prec_hbm, prec_ref),
            )
        )
    ]
    for load in loads:
        load.start()
    to_some(0, 1, greet)

    x32[pl.ds(chan * height, (CP - chan) * height), :] = jnp.zeros(((CP - chan) * height, LANES), F32)
    loads[0].wait()
    x32[pl.ds(0, chan * height), :] = x_ref[...].astype(F32).reshape(chan * height, LANES)
    lane = lane_iota(CP)
    first_lane = lane == 0
    last_lane = lane == LANES - 1

    def block(rim, r, count=1):
        return pl.ds((r + rim) * LANES, count * LANES)

    def rolled(value, shift):
        return pltpu.roll(value, shift % LANES, 1) if shift % LANES else value

    def spot(r):
        return 2 * (r + 2)

    pair_of = lane // 2
    to_left = jnp.zeros((CP, LANES), F32)
    to_right = jnp.zeros((CP, LANES), F32)
    for r in range(height):
        row = x32[pl.ds(r, CP, stride=height), :]
        s1[pl.ds(CP, CP), block(2, r)] = row.astype(BF16)
        to_left = jnp.where(pair_of == r + 2, rolled(row, spot(r)), to_left)
        to_right = jnp.where(pair_of == r + 2, rolled(row, spot(r) + 2), to_right)
    csend[0] = to_left.astype(BF16)
    csend[1] = to_right.astype(BF16)

    def guarded(d):
        if d in (UP, UL, UR):
            return pl.when(has_up)
        if d in (DOWN, DL, DR):
            return pl.when(has_down)
        return lambda f: f()

    def send(src, dst, t, d, sends, recvs):
        copy = pltpu.make_async_remote_copy(
            src_ref=src, dst_ref=dst, send_sem=sends.at[t, d], recv_sem=recvs.at[t, opposite[d]],
            device_id=ids[d], device_id_type=MESH,
        )
        guarded(d)(copy.start)

    def wait_recv(dst, t, d, sends, recvs):
        copy = pltpu.make_async_remote_copy(
            src_ref=dst, dst_ref=dst, send_sem=sends.at[t, d], recv_sem=recvs.at[t, d],
            device_id=ids[d], device_id_type=MESH,
        )
        guarded(d)(copy.wait_recv)

    def wait_send(src, t, d, sends, recvs):
        copy = pltpu.make_async_remote_copy(
            src_ref=src, dst_ref=src, send_sem=sends.at[t, d], recv_sem=recvs.at[t, d],
            device_id=ids[d], device_id_type=MESH,
        )
        guarded(d)(copy.wait_send)

    def column_blocks(rows, first_of, last_of):
        to_left = jnp.zeros((CP, LANES), F32)
        to_right = jnp.zeros((CP, LANES), F32)
        for r in range(rows):
            to_left = jnp.where(lane == r, pltpu.roll(first_of(r), r, 1) if r else first_of(r), to_left)
            to_right = jnp.where(lane == r, pltpu.roll(last_of(r), r + 1, 1), to_right)
        return to_left.astype(BF16), to_right.astype(BF16)

    diag_slots = {UL: 0, UR: 1, DL: 2, DR: 3}

    def pair(r):
        return s1.at[pl.ds(CP, CP), block(2, r, 2)]

    state_sources = {
        UP: pair(0), DOWN: pair(height - 2),
        LEFT: csend.at[0], UL: csend.at[0], DL: csend.at[0],
        RIGHT: csend.at[1], UR: csend.at[1], DR: csend.at[1],
    }
    state_targets = {UP: pair(-2), DOWN: pair(height)}
    for k, d in enumerate((LEFT, RIGHT, UL, UR, DL, DR)):
        state_targets[d] = hcol.at[k]

    def send_state():
        for d in (UP, DOWN, LEFT, RIGHT, UL, UR, DL, DR):
            send(state_sources[d], state_targets[opposite[d]], 0, d, fsend, frecv)

    def receive_state():
        for d in range(8):
            wait_recv(state_targets[d], 0, d, fsend, frecv)
        for there, r, slots in ((has_up, -2, (2, 3)), (has_down, height, (4, 5))):

            @pl.when(jnp.logical_not(there))
            def _():
                s1[pl.ds(CP, CP), block(2, r, 2)] = jnp.zeros((CP, WIDE), BF16)
                for slot in slots:
                    hcol[slot] = jnp.zeros((CP, LANES), BF16)

    def shift_rows(s, rim, rows, low, low_lane, high, high_lane):
        for r in rows:
            row = s[pl.ds(CP, CP), block(rim, r)].astype(F32)
            lower = jnp.where(first_lane, rolled(low, -low_lane(r)), rolled(row, 1))
            upper = jnp.where(last_lane, rolled(high, LANES - 1 - high_lane(r)), rolled(row, -1))
            s[pl.ds(0, CP), block(rim, r)] = lower.astype(BF16)
            s[pl.ds(2 * CP, CP), block(rim, r)] = upper.astype(BF16)

    def with_corners(side, above, below):
        middle = jnp.logical_and(pair_of >= 2, pair_of < height + 2)
        outer = jnp.where(pair_of < 2, rolled(above, -2 * height), rolled(below, 2 * height))
        return jnp.where(middle, side, outer)

    def spread_columns():
        from_left, from_right, ul, ur, dl, dr = (hcol[k].astype(F32) for k in range(6))
        low = with_corners(from_left, ul, dl)
        high = with_corners(from_right, ur, dr)
        first = csend[0].astype(F32)
        last = rolled(csend[1].astype(F32), -1)
        for r in (-2, -1, height, height + 1):
            row = s1[pl.ds(CP, CP), block(2, r)].astype(F32)
            first = jnp.where(lane == spot(r), rolled(row, spot(r)), first)
            last = jnp.where(lane == spot(r), rolled(row, spot(r) + 1), last)
        on_left = lane < LANES // 2
        taps = (
            jnp.where(on_left, low, rolled(last, LANES // 2)),
            jnp.where(on_left, rolled(low, -1), rolled(high, LANES // 2)),
            jnp.where(on_left, first, rolled(high, LANES // 2 - 1)),
        )
        for i in range(3):
            for j in range(3):
                se[i, pl.ds(j * CP, CP), :] = rolled(taps[j], 2 * (1 - i)).astype(BF16)
        return low, high, taps[1]

    def network(window, centre):
        pre = sum(dot(wt_ref[i], window(i)) for i in range(3))
        cdf = 0.5 * (1.0 + lax.erf(pre * ROOT_HALF))
        update = dot(wo_ref[...], (pre * cdf).astype(BF16))
        return centre.astype(F32) + update, lambda: cdf + pre * jnp.exp(-0.5 * pre * pre) * NORM_DENSITY

    def forward_chunk(s, rim, n, slope):
        state, tangent = network(
            lambda i: s[:, block(rim, 2 * n + i - 1, 2)], s[pl.ds(CP, CP), block(rim, 2 * n, 2)]
        )
        slope[:, pl.ds(n * WIDE, WIDE)] = tangent()
        return state.astype(BF16)

    def first_rim(centre):
        up, down = has_up.astype(F32), has_down.astype(F32)
        rows = (-1, height)
        state, _ = network(
            lambda i: jnp.concatenate([s1[:, block(2, r + i - 1)] for r in rows], axis=1),
            jnp.concatenate([s1[pl.ds(CP, CP), block(2, r)] for r in rows], axis=1),
        )
        s2[pl.ds(CP, CP), block(1, -1)] = (state[:, :LANES] * up).astype(BF16)
        s2[pl.ds(CP, CP), block(1, height)] = (state[:, LANES:] * down).astype(BF16)
        sides, _ = network(lambda i: se[i], centre)
        place = lax.rem(lane, LANES // 2)
        inside = jnp.where(place == spot(-1), up, jnp.where(place == spot(height), down, 1.0))
        return (sides * inside).astype(BF16).astype(F32)

    pl.semaphore_wait(barrier, owners - 1)
    send_state()

    for load in loads[1:]:
        load.wait()
    cell = cell_ref[...]
    packed[pl.ds(0, owners, stride=8), :] = (cell // WIDE).astype(F32)
    packed[pl.ds(1, owners, stride=8), :] = (cell % LANES).astype(F32)
    for k in range(4):
        packed[pl.ds(2 + k, owners, stride=8), :] = w_ref[k]
    packed[pl.ds(6, owners, stride=8), :] = val_ref[...]
    packed[pl.ds(7, owners, stride=8), :] = prec_ref[...]

    def post(other, where):
        pltpu.make_async_remote_copy(
            src_ref=packed.at[pl.ds(pl.multiple_of(other * 8, 8), 8)],
            dst_ref=recv.at[pl.ds(pl.multiple_of(me * 8, 8), 8)],
            send_sem=psend, recv_sem=precv, device_id=where, device_id_type=MESH,
        ).start()

    mine = pl.ds(pl.multiple_of(me * 8, 8), 8)
    recv[mine, :] = packed[mine, :]

    wpad[...] = jnp.zeros((LANES, hid), F32)
    bias = cb_ref[...]
    bias_parts = []
    for _ in range(3):
        part = bias.astype(BF16).astype(F32)
        bias_parts.append(part)
        bias = bias - part
    spare = lax.broadcasted_iota(jnp.int32, (hid - 3 * CP, hid), 0)
    bias_rows = jnp.zeros((hid - 3 * CP, hid), F32)
    for k, part in enumerate(bias_parts):
        bias_rows = jnp.where(spare == k, part, bias_rows)
    for i in range(3):
        for j in range(3):
            wpad[pl.ds(0, chan), :] = cw_ref[3 * i + j].astype(F32)
            wk[i, pl.ds(j * CP, CP), :] = wpad[pl.ds(0, CP), :].astype(BF16)
        wk[i, pl.ds(3 * CP, hid - 3 * CP), :] = (bias_rows if i == 1 else jnp.zeros_like(bias_rows)).astype(BF16)
        wt_ref[i] = jnp.transpose(wk[i].astype(F32)).astype(BF16)
    wpad[pl.ds(0, chan), :] = ow_ref[...].astype(F32)
    wo_ref[...] = wpad[pl.ds(0, CP), :].astype(BF16)
    wot_ref[...] = jnp.transpose(wpad[...]).astype(BF16)
    for c in range(chan):
        grad_ref[pl.ds(c * height, height), :] = bp_ref[0, c] * (x_ref[c].astype(F32) - xb_ref[c].astype(F32))

    def ones(breadth):
        return jnp.ones((hid - 3 * CP, breadth), BF16)

    s1[pl.ds(3 * CP, hid - 3 * CP), :] = ones((height + 4) * LANES)
    s2[pl.ds(3 * CP, hid - 3 * CP), :] = ones((height + 2) * LANES)
    for i in range(3):
        se[i, pl.ds(3 * CP, hid - 3 * CP), :] = ones(LANES)

    receive_state()
    low, high, beside = spread_columns()
    shift_rows(s1, 2, range(-2, height + 2), low, lambda r: spot(r) + 1, high, spot)
    for n in range(chunks):
        to_some(n, chunks, post)
        s2[pl.ds(CP, CP), block(1, 2 * n, 2)] = forward_chunk(s1, 2, n, slope1)
    sides = first_rim(beside)
    shift_rows(s2, 1, range(-1, height + 1), sides, spot, sides, lambda r: LANES // 2 + spot(r))
    for n in range(chunks):
        sobs[n] = forward_chunk(s2, 1, n, slope2)

    others = pl.ds(0, (owners - 1) * 8)
    pltpu.make_async_remote_copy(
        src_ref=packed.at[others], dst_ref=recv.at[others], send_sem=psend, recv_sem=precv,
        device_id=ids[RIGHT], device_id_type=MESH,
    ).wait()
    column = lax.broadcasted_iota(jnp.int32, (LANES, LANES), 0).astype(F32).astype(BF16)
    channel = lax.broadcasted_iota(jnp.int32, (CP, LANES), 0).astype(F32)
    zero = jnp.zeros((LANES, LANES), BF16)

    def estimate(group, carry):
        for u in range(GROUP):
            k = group * GROUP + u
            packet = recv[pl.ds(pl.multiple_of(k * 8, 8), 8), :]
            def row(which):
                return jnp.broadcast_to(packet[which : which + 1].astype(BF16), (LANES, LANES))

            at = row(1)
            here, after = column == at, column == at + 1
            table = jnp.concatenate(
                [
                    jnp.where(here, row(2), jnp.where(after, row(3), zero)),
                    jnp.where(here, row(4), jnp.where(after, row(5), zero)),
                ],
                axis=0,
            )
            bsc[k] = table
            picked = channel == packet[0:1]
            found = dot(sobs[swath_ref[0, k]], table)
            gap = jnp.sum(jnp.where(picked, found, 0.0), axis=0, keepdims=True) - packet[6:7]
            inn[k] = gap
            qsc[k] = jnp.where(picked, packet[7:8] * gap, 0.0).astype(BF16)
        return carry

    lax.fori_loop(0, owners // GROUP, estimate, 0)
    hist[0] = jnp.zeros((CP, WIDE), F32)

    def pull(group, last):
        for u in range(GROUP):
            k = group * GROUP + u
            patch = swath_ref[0, k]
            before = sum(jnp.where(patch == m, last[m], 0) for m in range(chunks))
            share = lax.dot_general(qsc[k], bsc[k], (((1,), (1,)), ((), ())), preferred_element_type=F32)
            hist[k + 1] = hist[before] + share
            last = tuple(jnp.where(patch == m, k + 1, last[m]) for m in range(chunks))
        return last

    last = lax.fori_loop(0, owners // GROUP, pull, (jnp.int32(0),) * chunks)
    inn_recv[me] = inn[me]

    def give_back(other, where):
        pltpu.make_async_remote_copy(
            src_ref=inn.at[other], dst_ref=inn_recv.at[me], send_sem=isend, recv_sem=irecv,
            device_id=where, device_id_type=MESH,
        ).start()

    def tap(i, j, r):
        return ybuf[pl.ds((3 * (i + 1) + j + 1) * CP, CP), pl.ds(r * LANES, LANES)]

    def summed(j, r):
        total = None
        for i in (-1, 0, 1):
            if 0 <= r - i < height:
                part = tap(i, j, r - i)
                total = part if total is None else total + part
        return total

    def rim_sources(t):
        return {
            UP: brow.at[t, 0], UL: brow.at[t, 1], UR: brow.at[t, 2],
            DOWN: brow.at[t, 3], DL: brow.at[t, 4], DR: brow.at[t, 5],
            LEFT: bcol.at[t, 0], RIGHT: bcol.at[t, 1],
        }

    def rim_targets(t):
        table = {UP: rrow.at[t, 0], DOWN: rrow.at[t, 1], LEFT: rcol.at[t, 0], RIGHT: rcol.at[t, 1]}
        for d, slot in diag_slots.items():
            table[d] = rdiag.at[t, slot]
        return table

    pad = jnp.zeros((LANES - CP, WIDE), BF16)

    def backward_step(t, cotangent, slope, finish):
        src, dst = rim_sources(t), rim_targets(t)
        for n in range(chunks):
            rounded = jnp.concatenate([cotangent(n).astype(BF16), pad], axis=0)
            spread = (dot(wot_ref[...], rounded) * slope[:, pl.ds(n * WIDE, WIDE)]).astype(BF16)
            for i in range(3):
                ybuf[pl.ds(3 * i * CP, 3 * CP), pl.ds(n * WIDE, WIDE)] = dot(wk[i, pl.ds(0, 3 * CP), :], spread)

        def inner(t_low, t_mid, t_high):
            return (
                t_mid
                + jnp.where(first_lane, 0.0, pltpu.roll(t_high, 1, 1))
                + jnp.where(last_lane, 0.0, pltpu.roll(t_low, LANES - 1, 1))
            )

        for r, at in ((-1, 0), (height, 3)):
            t_low, t_mid, t_high = (summed(j, r) for j in (-1, 0, 1))
            brow[t, at] = inner(t_low, t_mid, t_high).astype(BF16)
            brow[t, at + 1] = t_low.astype(BF16)
            brow[t, at + 2] = t_high.astype(BF16)
        for d in (UP, DOWN, UL, UR, DL, DR):
            send(src[d], dst[opposite[d]], t, d, bsend, brecv)
        to_left, to_right = column_blocks(height, lambda r: summed(-1, r), lambda r: summed(1, r))
        bcol[t, 0] = to_left
        bcol[t, 1] = to_right
        for d in (LEFT, RIGHT):
            send(src[d], dst[opposite[d]], t, d, bsend, brecv)
        for r in range(height):
            to_some(height * t + r, 2 * height, give_back)
            ubuf[:, pl.ds(r * LANES, LANES)] = inner(summed(-1, r), summed(0, r), summed(1, r)) + cotangent(r // 2)[
                :, (r % 2) * LANES : (r % 2 + 1) * LANES
            ]
        for d in range(8):
            wait_recv(dst[d], t, d, bsend, brecv)
        for r, there, at, a, b in ((0, has_up, 0, UL, UR), (height - 1, has_down, 1, DL, DR)):

            @pl.when(there)
            def _():
                ubuf[:, pl.ds(r * LANES, LANES)] = (
                    ubuf[:, pl.ds(r * LANES, LANES)]
                    + rrow[t, at].astype(F32)
                    + jnp.where(first_lane, pltpu.roll(rdiag[t, diag_slots[a]].astype(F32), 1, 1), 0.0)
                    + jnp.where(last_lane, pltpu.roll(rdiag[t, diag_slots[b]].astype(F32), LANES - 1, 1), 0.0)
                )

        from_left = rcol[t, 0].astype(F32)
        from_right = rcol[t, 1].astype(F32)
        for r in range(height):
            finish(
                r,
                ubuf[:, pl.ds(r * LANES, LANES)]
                + jnp.where(first_lane, pltpu.roll(from_left, (LANES - r) % LANES, 1) if r else from_left, 0.0)
                + jnp.where(last_lane, pltpu.roll(from_right, LANES - 1 - r, 1), 0.0),
            )

    def keep(r, value):
        gbuf[:, pl.ds(r * LANES, LANES)] = value

    def write(r, value):
        here = pl.ds(r, chan, stride=height)
        grad_ref[here, :] = grad_ref[here, :] + value[:chan]

    backward_step(0, lambda n: hist[last[n]], slope2, keep)
    backward_step(1, lambda n: gbuf[:, pl.ds(n * WIDE, WIDE)], slope1, write)

    rows = pl.ds(0, owners - 1)
    pltpu.make_async_remote_copy(
        src_ref=inn.at[rows], dst_ref=inn_recv.at[rows], send_sem=isend, recv_sem=irecv,
        device_id=ids[RIGHT], device_id_type=MESH,
    ).wait()
    innov_ref[...] = inn_recv[...].reshape(owners, LANES)
    for d in range(8):
        wait_send(state_sources[d], 0, d, fsend, frecv)
    for t in range(2):
        src = rim_sources(t)
        for d in range(8):
            wait_send(src[d], t, d, bsend, brecv)


def hand_over(gradient_in, innov_in, gradient_out, innov_out, gradient_held, innov_held, sems):
    chan = gradient_in.shape[0]
    cuts = [chan * k // PIECES for k in range(PIECES + 1)]
    parts = [pl.ds(a, b - a) for a, b in zip(cuts, cuts[1:])]
    routes = [(gradient_in.at[p], gradient_held.at[p], gradient_out.at[p]) for p in parts]
    routes.append((innov_in, innov_held, innov_out))
    reads = [pltpu.make_async_copy(src, held, sems.at[0, k]) for k, (src, held, _) in enumerate(routes)]
    writes = [pltpu.make_async_copy(held, dst, sems.at[1, k]) for k, (_, held, dst) in enumerate(routes)]
    for read in reads:
        read.start()
    for read, write in zip(reads, writes):
        read.wait()
        write.start()
    for write in writes:
        write.wait()


def local(
    n_lat, n_lon,
    initial_state, background_state, background_precision, conv_weight, conv_bias, out_weight,
    swath_patch, obs_cell, obs_weights, obs_value, obs_precision,
):
    chan, height, breadth = initial_state.shape
    hid = conv_weight.shape[2]
    owners = n_lat * n_lon
    chunks = height // 2
    cells = height * breadth
    vmem = pl.BlockSpec(memory_space=pltpu.VMEM)
    hbm = pl.BlockSpec(memory_space=pltpu.HBM)
    smem = pl.BlockSpec(memory_space=pltpu.SMEM)
    dma = pltpu.SemaphoreType.DMA
    gradient, innov = pl.pallas_call(
        functools.partial(kernel, n_lat, n_lon, hid),
        out_shape=(
            jax.ShapeDtypeStruct((chan * height, LANES), F32),
            jax.ShapeDtypeStruct((owners, LANES), F32),
        ),
        in_specs=[hbm, hbm, smem, vmem, vmem, vmem, smem] + [hbm] * 4,
        out_specs=(vmem, vmem),
        scratch_shapes=[
            pltpu.VMEM((chan, height, breadth), BF16),
            pltpu.VMEM((chan, height, breadth), BF16),
            pltpu.VMEM((owners, LANES), jnp.int32),
            pltpu.VMEM((4, owners, LANES), F32),
            pltpu.VMEM((owners, LANES), F32),
            pltpu.VMEM((owners, LANES), F32),
            pltpu.VMEM((LANES, hid), F32),
            pltpu.VMEM((3, hid, hid), BF16),
            pltpu.VMEM((3, hid, hid), BF16),
            pltpu.VMEM((CP, hid), BF16),
            pltpu.VMEM((hid, LANES), BF16),
            pltpu.VMEM((CP * height, LANES), F32),
            pltpu.VMEM((owners * 8, LANES), F32),
            pltpu.VMEM((owners * 8, LANES), F32),
            pltpu.VMEM((hid, (height + 4) * LANES), BF16),
            pltpu.VMEM((hid, (height + 2) * LANES), BF16),
            pltpu.VMEM((3, hid, LANES), BF16),
            pltpu.VMEM((chunks, CP, WIDE), BF16),
            pltpu.VMEM((hid, cells), F32),
            pltpu.VMEM((hid, cells), F32),
            pltpu.VMEM((2, CP, LANES), BF16),
            pltpu.VMEM((6, CP, LANES), BF16),
            pltpu.VMEM((owners, WIDE, LANES), BF16),
            pltpu.VMEM((owners, CP, LANES), BF16),
            pltpu.VMEM((owners, 1, LANES), F32),
            pltpu.VMEM((owners, 1, LANES), F32),
            pltpu.VMEM((owners + 1, CP, WIDE), F32),
            pltpu.VMEM((9 * CP, cells), F32),
            pltpu.VMEM((CP, cells), F32),
            pltpu.VMEM((CP, cells), F32),
            pltpu.VMEM((2, 6, CP, LANES), BF16),
            pltpu.VMEM((2, 2, CP, LANES), BF16),
            pltpu.VMEM((2, 2, CP, LANES), BF16),
            pltpu.VMEM((2, 4, CP, LANES), BF16),
            pltpu.VMEM((2, 2, CP, LANES), BF16),
            dma((1, 8)), dma((1, 8)), dma((2, 8)), dma((2, 8)),
            dma, dma, dma, dma, dma((6,)),
        ],
        compiler_params=pltpu.CompilerParams(
            collective_id=0, has_side_effects=True, vmem_limit_bytes=56 * 1024 * 1024
        ),
    )(
        initial_state, background_state, background_precision[None], conv_weight, conv_bias[None], out_weight, swath_patch,
        obs_cell[0], obs_weights[:, 0], obs_value[0], obs_precision[0],
    )
    return pl.pallas_call(
        hand_over,
        out_shape=(
            jax.ShapeDtypeStruct((chan, height, breadth), F32),
            jax.ShapeDtypeStruct((1, owners, LANES), F32),
        ),
        in_specs=[hbm, hbm],
        out_specs=(hbm, hbm),
        scratch_shapes=[
            pltpu.VMEM((chan, height, breadth), F32),
            pltpu.VMEM((1, owners, LANES), F32),
            dma((2, PIECES + 1)),
        ],
        compiler_params=pltpu.CompilerParams(vmem_limit_bytes=56 * 1024 * 1024),
    )(gradient.reshape(chan, height, breadth), innov[None])


def solution(mesh):
    tile = P(None, "lat", "lon")
    owner = ("lat", "lon")
    in_specs = (
        tile, tile, P(), P(), P(), P(),
        P(owner, None), P(owner, None, None), P(None, owner, None, None), P(owner, None, None), P(owner, None, None),
    )
    return jax.shard_map(
        functools.partial(local, mesh.shape["lat"], mesh.shape["lon"]),
        mesh=mesh, in_specs=in_specs, out_specs=(tile, P(owner, None, None)), check_vma=False,
    )
```

```python
import functools

import jax
import jax.numpy as jnp
from jax import lax
from jax.experimental import pallas as pl
from jax.experimental.pallas import tpu as pltpu
from jax.sharding import PartitionSpec as P

MESH = pl.DeviceIdType.MESH
F32 = jnp.float32
BF16 = jnp.bfloat16
CP = 80
LANES = 128
WIDE = 256
ROOT_HALF = 0.7071067811865476
NORM_DENSITY = 0.3989422804014327
UP, DOWN, LEFT, RIGHT, UL, UR, DL, DR = range(8)
GROUP = 16
PIECES = 3


def dot(a, b):
    return jnp.dot(a, b, preferred_element_type=F32)


def lane_iota(rows):
    return lax.broadcasted_iota(jnp.int32, (rows, LANES), 1)


def kernel(
    n_lat, n_lon, hid,
    x_hbm, xb_hbm, bp_ref, cw_ref, cb_ref, ow_ref, swath_ref, cell_hbm, w_hbm, val_hbm, prec_hbm,
    grad_ref, innov_ref,
    x_ref, xb_ref, cell_ref, w_ref, val_ref, prec_ref, wpad, wk, wt_ref, wo_ref, wot_ref, x32, packed, recv, s1, s2, se, sobs, slope1, slope2, slope_edge, csend, hcol,
    bsc, qsc, inn, inn_recv, hist, ybuf, xbuf, ubuf, brow, bcol, rrow, rcol,
    fsend, frecv, bsend, brecv, psend, precv, isend, irecv, loaded,
):
    chan, height = x_ref.shape[0], x_ref.shape[1]
    owners = n_lat * n_lon
    chunks = height // 2
    lat = lax.axis_index("lat")
    lon = lax.axis_index("lon")
    me = lat * n_lon + lon
    has_up = lat > 0
    has_down = lat < n_lat - 1
    left = lax.rem(lon + n_lon - 1, n_lon)
    right = lax.rem(lon + 1, n_lon)
    ids = {
        UP: (lat - 1, lon), DOWN: (lat + 1, lon), LEFT: (lat, left), RIGHT: (lat, right),
        UL: (lat - 1, left), UR: (lat - 1, right), DL: (lat + 1, left), DR: (lat + 1, right),
    }
    opposite = {UP: DOWN, DOWN: UP, LEFT: RIGHT, RIGHT: LEFT, UL: DR, DR: UL, UR: DL, DL: UR}

    barrier = pltpu.get_barrier_semaphore()

    def wrapped(value, count):
        return value - jnp.where(value >= count, count, 0)

    rounds = [(step, ahead) for step in range(n_lat) for ahead in range(n_lon) if step or ahead]

    def to_some(part, parts, act):
        for step, ahead in rounds[len(rounds) * part // parts : len(rounds) * (part + 1) // parts]:
            there, column = wrapped(lat + step, n_lat), wrapped(lon + ahead, n_lon)
            act(there * n_lon + column, (there, column))

    def greet(_, where):
        pl.semaphore_signal(barrier, inc=1, device_id=where, device_id_type=MESH)

    loads = [
        pltpu.make_async_copy(src, dst, loaded.at[k])
        for k, (src, dst) in enumerate(
            (
                (x_hbm, x_ref), (xb_hbm, xb_ref), (cell_hbm, cell_ref),
                (w_hbm, w_ref), (val_hbm, val_ref), (prec_hbm, prec_ref),
            )
        )
    ]
    for load in loads:
        load.start()
    to_some(0, 1, greet)

    x32[pl.ds(chan * height, (CP - chan) * height), :] = jnp.zeros(((CP - chan) * height, LANES), F32)
    loads[0].wait()
    x32[pl.ds(0, chan * height), :] = x_ref[...].astype(F32).reshape(chan * height, LANES)
    lane = lane_iota(CP)
    first_lane = lane == 0
    last_lane = lane == LANES - 1

    def block(rim, r, count=1):
        return pl.ds((r + rim) * LANES, count * LANES)

    def rolled(value, shift):
        return pltpu.roll(value, shift % LANES, 1) if shift % LANES else value

    def spot(r):
        return 2 * (r + 2)

    even = lax.rem(lane, 2) == 0
    edge = jnp.logical_or(first_lane, last_lane)
    slot_of = (lane + 1) // 2

    def joined(value):
        return jnp.where(even, value, rolled(value, -LANES // 2 - 1))

    def apart(value):
        return jnp.where(lane < LANES // 2, value, rolled(value, LANES // 2 + 1))

    def gathered(total, r, row):
        return jnp.where(slot_of == r + 2, rolled(row, spot(r)), total)

    pair_of = lane // 2
    to_left = jnp.zeros((CP, LANES), F32)
    to_right = jnp.zeros((CP, LANES), F32)
    for r in range(height):
        row = x32[pl.ds(r, CP, stride=height), :]
        s1[pl.ds(CP, CP), block(2, r)] = row.astype(BF16)
        s1[pl.ds(0, CP), block(2, r)] = rolled(row, 1).astype(BF16)
        s1[pl.ds(2 * CP, CP), block(2, r)] = rolled(row, -1).astype(BF16)
        to_left = jnp.where(pair_of == r + 2, rolled(row, spot(r)), to_left)
        to_right = jnp.where(pair_of == r + 2, rolled(row, spot(r) + 2), to_right)
    csend[0] = to_left.astype(BF16)
    csend[1] = to_right.astype(BF16)

    def guarded(d):
        if d in (UP, UL, UR):
            return pl.when(has_up)
        if d in (DOWN, DL, DR):
            return pl.when(has_down)
        return lambda f: f()

    def send(src, dst, t, d, sends, recvs):
        copy = pltpu.make_async_remote_copy(
            src_ref=src, dst_ref=dst, send_sem=sends.at[t, d], recv_sem=recvs.at[t, opposite[d]],
            device_id=ids[d], device_id_type=MESH,
        )
        guarded(d)(copy.start)

    def wait_recv(dst, t, d, sends, recvs):
        copy = pltpu.make_async_remote_copy(
            src_ref=dst, dst_ref=dst, send_sem=sends.at[t, d], recv_sem=recvs.at[t, d],
            device_id=ids[d], device_id_type=MESH,
        )
        guarded(d)(copy.wait_recv)

    def wait_send(src, t, d, sends, recvs):
        copy = pltpu.make_async_remote_copy(
            src_ref=src, dst_ref=src, send_sem=sends.at[t, d], recv_sem=recvs.at[t, d],
            device_id=ids[d], device_id_type=MESH,
        )
        guarded(d)(copy.wait_send)

    def pair(r):
        return s1.at[pl.ds(CP, CP), block(2, r, 2)]

    state_sources = {
        UP: pair(0), DOWN: pair(height - 2),
        LEFT: csend.at[0], UL: csend.at[0], DL: csend.at[0],
        RIGHT: csend.at[1], UR: csend.at[1], DR: csend.at[1],
    }
    state_targets = {UP: pair(-2), DOWN: pair(height)}
    for k, d in enumerate((LEFT, RIGHT, UL, UR, DL, DR)):
        state_targets[d] = hcol.at[k]

    def send_state():
        for d in (UP, DOWN, LEFT, RIGHT, UL, UR, DL, DR):
            send(state_sources[d], state_targets[opposite[d]], 0, d, fsend, frecv)

    def receive_state():
        for d in range(8):
            wait_recv(state_targets[d], 0, d, fsend, frecv)
        for there, r, slots in ((has_up, -2, (2, 3)), (has_down, height, (4, 5))):

            @pl.when(jnp.logical_not(there))
            def _():
                s1[pl.ds(CP, CP), block(2, r, 2)] = jnp.zeros((CP, WIDE), BF16)
                for slot in slots:
                    hcol[slot] = jnp.zeros((CP, LANES), BF16)

    def shift_far_rows():
        for r in (-2, -1, height, height + 1):
            row = s1[pl.ds(CP, CP), block(2, r)].astype(F32)
            s1[pl.ds(0, CP), block(2, r)] = rolled(row, 1).astype(BF16)
            s1[pl.ds(2 * CP, CP), block(2, r)] = rolled(row, -1).astype(BF16)

    def merge_columns(at_edge, beside):
        at_edge, beside = joined(at_edge), joined(beside)
        for r in range(-1, height + 1):
            row = jnp.where(edge, rolled(at_edge, -spot(r)), s2[pl.ds(CP, CP), block(1, r)].astype(F32))
            outer = rolled(beside, -spot(r))
            s2[pl.ds(0, CP), block(1, r)] = jnp.where(first_lane, outer, rolled(row, 1)).astype(BF16)
            s2[pl.ds(CP, CP), block(1, r)] = row.astype(BF16)
            s2[pl.ds(2 * CP, CP), block(1, r)] = jnp.where(last_lane, outer, rolled(row, -1)).astype(BF16)

    def with_corners(side, above, below):
        middle = jnp.logical_and(pair_of >= 2, pair_of < height + 2)
        outer = jnp.where(pair_of < 2, rolled(above, -2 * height), rolled(below, 2 * height))
        return jnp.where(middle, side, outer)

    def spread_columns():
        from_left, from_right, ul, ur, dl, dr = (hcol[k].astype(F32) for k in range(6))
        low = with_corners(from_left, ul, dl)
        high = with_corners(from_right, ur, dr)
        first = csend[0].astype(F32)
        last = csend[1].astype(F32)
        for r in (-2, -1, height, height + 1):
            row = s1[pl.ds(CP, CP), block(2, r)].astype(F32)
            first = jnp.where(pair_of == r + 2, rolled(row, spot(r)), first)
            last = jnp.where(pair_of == r + 2, rolled(row, spot(r) + 2), last)
        on_left = lane < LANES // 2
        lefts = (low, rolled(low, -1), first, rolled(first, -1))
        rights = tuple(rolled(v, LANES // 2 - k) for v in (last, high) for k in (0, 1))
        beside = tuple(jnp.where(on_left, lefts[j], rights[j + 1]) for j in range(3))
        at_edge = tuple(jnp.where(on_left, lefts[j + 1], rights[j]) for j in range(3))
        for i in range(3):
            for j in range(3):
                part = pl.ds(j * CP, CP)
                se[i, part, pl.ds(0, LANES)] = rolled(beside[j], 2 * (1 - i)).astype(BF16)
                se[i, part, pl.ds(LANES, LANES)] = rolled(at_edge[j], 2 * (1 - i)).astype(BF16)
        return jnp.concatenate([beside[1], at_edge[1]], axis=1)

    def network(window, centre):
        pre = sum(dot(wt_ref[i], window(i)) for i in range(3))
        cdf = 0.5 * (1.0 + lax.erf(pre * ROOT_HALF))
        update = dot(wo_ref[...], (pre * cdf).astype(BF16))
        return centre.astype(F32) + update, lambda: cdf + pre * jnp.exp(-0.5 * pre * pre) * NORM_DENSITY

    def forward_chunk(s, rim, n, slope, inner_only):
        state, tangent = network(
            lambda i: s[:, block(rim, 2 * n + i - 1, 2)], s[pl.ds(CP, CP), block(rim, 2 * n, 2)]
        )
        slope[:, pl.ds(n * WIDE, WIDE)] = jnp.where(edge_wide, 0.0, tangent()) if inner_only else tangent()
        return state.astype(BF16)

    def first_rim(centre):
        up, down = has_up.astype(F32), has_down.astype(F32)
        rows = (-1, height)
        state, _ = network(
            lambda i: jnp.concatenate([s1[:, block(2, r + i - 1)] for r in rows], axis=1),
            jnp.concatenate([s1[pl.ds(CP, CP), block(2, r)] for r in rows], axis=1),
        )
        s2[pl.ds(CP, CP), block(1, -1)] = (state[:, :LANES] * up).astype(BF16)
        s2[pl.ds(CP, CP), block(1, height)] = (state[:, LANES:] * down).astype(BF16)
        sides, tangent = network(lambda i: se[i], centre)
        place = lax.rem(lane, LANES // 2)
        inside = jnp.where(place == spot(-1), up, jnp.where(place == spot(height), down, 1.0))
        here = lax.rem(lane_iota(hid), LANES // 2)
        kept = jnp.logical_and(lax.rem(here, 2) == 0, jnp.logical_and(here >= spot(0), here <= spot(height - 1)))
        slope_edge[...] = jnp.where(kept, tangent()[:, LANES:], 0.0)
        return tuple((sides[:, k * LANES : (k + 1) * LANES] * inside).astype(BF16).astype(F32) for k in (0, 1))

    pl.semaphore_wait(barrier, owners - 1)
    send_state()

    for load in loads[1:]:
        load.wait()
    cell = cell_ref[...]
    packed[pl.ds(0, owners, stride=8), :] = (cell // WIDE).astype(F32)
    packed[pl.ds(1, owners, stride=8), :] = (cell % LANES).astype(F32)
    for k in range(4):
        packed[pl.ds(2 + k, owners, stride=8), :] = w_ref[k]
    packed[pl.ds(6, owners, stride=8), :] = val_ref[...]
    packed[pl.ds(7, owners, stride=8), :] = prec_ref[...]

    def post(other, where):
        pltpu.make_async_remote_copy(
            src_ref=packed.at[pl.ds(pl.multiple_of(other * 8, 8), 8)],
            dst_ref=recv.at[pl.ds(pl.multiple_of(me * 8, 8), 8)],
            send_sem=psend, recv_sem=precv, device_id=where, device_id_type=MESH,
        ).start()

    mine = pl.ds(pl.multiple_of(me * 8, 8), 8)
    recv[mine, :] = packed[mine, :]

    wpad[...] = jnp.zeros((LANES, hid), F32)
    bias = cb_ref[...]
    bias_parts = []
    for _ in range(3):
        part = bias.astype(BF16).astype(F32)
        bias_parts.append(part)
        bias = bias - part
    spare = lax.broadcasted_iota(jnp.int32, (hid - 3 * CP, hid), 0)
    bias_rows = jnp.zeros((hid - 3 * CP, hid), F32)
    for k, part in enumerate(bias_parts):
        bias_rows = jnp.where(spare == k, part, bias_rows)
    for i in range(3):
        for j in range(3):
            wpad[pl.ds(0, chan), :] = cw_ref[3 * i + j].astype(F32)
            wk[i, pl.ds(j * CP, CP), :] = wpad[pl.ds(0, CP), :].astype(BF16)
        wk[i, pl.ds(3 * CP, hid - 3 * CP), :] = (bias_rows if i == 1 else jnp.zeros_like(bias_rows)).astype(BF16)
        wt_ref[i] = jnp.transpose(wk[i].astype(F32)).astype(BF16)
    wpad[pl.ds(0, chan), :] = ow_ref[...].astype(F32)
    wo_ref[...] = wpad[pl.ds(0, CP), :].astype(BF16)
    wot_ref[...] = jnp.transpose(wpad[...]).astype(BF16)
    for c in range(chan):
        grad_ref[pl.ds(c * height, height), :] = bp_ref[0, c] * (x_ref[c].astype(F32) - xb_ref[c].astype(F32))

    def ones(breadth):
        return jnp.ones((hid - 3 * CP, breadth), BF16)

    s1[pl.ds(3 * CP, hid - 3 * CP), :] = ones((height + 4) * LANES)
    s2[pl.ds(3 * CP, hid - 3 * CP), :] = ones((height + 2) * LANES)
    for i in range(3):
        se[i, pl.ds(3 * CP, hid - 3 * CP), :] = ones(WIDE)

    column_wide = lax.broadcasted_iota(jnp.int32, (hid, WIDE), 1)
    column_wide = lax.rem(column_wide, LANES)
    edge_wide = jnp.logical_or(column_wide == 0, column_wide == LANES - 1)
    early = range(1, chunks - 1)

    def first_step(n):
        s2[pl.ds(CP, CP), block(1, 2 * n, 2)] = forward_chunk(s1, 2, n, slope1, True)

    for k, n in enumerate(early):
        to_some(k, len(early), post)
        first_step(n)
    receive_state()
    shift_far_rows()
    first_step(0)
    first_step(chunks - 1)
    beside, at_edge = first_rim(spread_columns())
    merge_columns(at_edge, beside)
    for n in range(chunks):
        sobs[n] = forward_chunk(s2, 1, n, slope2, False)

    others = pl.ds(0, (owners - 1) * 8)
    pltpu.make_async_remote_copy(
        src_ref=packed.at[others], dst_ref=recv.at[others], send_sem=psend, recv_sem=precv,
        device_id=ids[RIGHT], device_id_type=MESH,
    ).wait()
    column = lax.broadcasted_iota(jnp.int32, (LANES, LANES), 0).astype(F32).astype(BF16)
    channel = lax.broadcasted_iota(jnp.int32, (CP, LANES), 0).astype(F32)
    zero = jnp.zeros((LANES, LANES), BF16)

    def estimate(group, carry):
        for u in range(GROUP):
            k = group * GROUP + u
            packet = recv[pl.ds(pl.multiple_of(k * 8, 8), 8), :]
            def row(which):
                return jnp.broadcast_to(packet[which : which + 1].astype(BF16), (LANES, LANES))

            at = row(1)
            here, after = column == at, column == at + 1
            table = jnp.concatenate(
                [
                    jnp.where(here, row(2), jnp.where(after, row(3), zero)),
                    jnp.where(here, row(4), jnp.where(after, row(5), zero)),
                ],
                axis=0,
            )
            bsc[k] = table
            picked = channel == packet[0:1]
            found = dot(sobs[swath_ref[0, k]], table)
            gap = jnp.sum(jnp.where(picked, found, 0.0), axis=0, keepdims=True) - packet[6:7]
            inn[k] = gap
            qsc[k] = jnp.where(picked, packet[7:8] * gap, 0.0).astype(BF16)
        return carry

    lax.fori_loop(0, owners // GROUP, estimate, 0)
    hist[0] = jnp.zeros((CP, WIDE), F32)

    def pull(group, last):
        for u in range(GROUP):
            k = group * GROUP + u
            patch = swath_ref[0, k]
            before = sum(jnp.where(patch == m, last[m], 0) for m in range(chunks))
            share = lax.dot_general(qsc[k], bsc[k], (((1,), (1,)), ((), ())), preferred_element_type=F32)
            hist[k + 1] = hist[before] + share
            last = tuple(jnp.where(patch == m, k + 1, last[m]) for m in range(chunks))
        return last

    last = lax.fori_loop(0, owners // GROUP, pull, (jnp.int32(0),) * chunks)
    inn_recv[me] = inn[me]

    def give_back(other, where):
        pltpu.make_async_remote_copy(
            src_ref=inn.at[other], dst_ref=inn_recv.at[me], send_sem=isend, recv_sem=irecv,
            device_id=where, device_id_type=MESH,
        ).start()

    def tap(i, j, r):
        return ybuf[pl.ds((3 * (i + 1) + j + 1) * CP, CP), pl.ds(r * LANES, LANES)]

    def summed(j, r):
        total = None
        for i in (-1, 0, 1):
            if 0 <= r - i < height:
                part = tap(i, j, r - i)
                total = part if total is None else total + part
        return total

    def rim_sources(t):
        table = dict.fromkeys((LEFT, RIGHT, UL, UR, DL, DR), bcol.at[t])
        return table | {UP: brow.at[t, 0], DOWN: brow.at[t, 1]}

    def rim_targets(t):
        table = {d: rcol.at[t, k] for k, d in enumerate((LEFT, RIGHT, UL, UR, DL, DR))}
        return table | {UP: rrow.at[t, 0], DOWN: rrow.at[t, 1]}

    def spread_of(cotangent, slope):
        breadth = cotangent.shape[1]
        rounded = jnp.concatenate([cotangent.astype(BF16), jnp.zeros((LANES - CP, breadth), BF16)], axis=0)
        return (dot(wot_ref[...], rounded) * slope).astype(BF16)

    def products(cotangent, slope):
        for n in range(chunks):
            cells = pl.ds(n * WIDE, WIDE)
            spread = spread_of(cotangent(n), slope[:, cells])
            for i in range(3):
                ybuf[pl.ds(3 * i * CP, 3 * CP), cells] = dot(wk[i, pl.ds(0, 3 * CP), :], spread)

    def inner(t_low, t_mid, t_high):
        return (
            t_mid
            + jnp.where(first_lane, 0.0, rolled(t_high, 1))
            + jnp.where(last_lane, 0.0, rolled(t_low, -1))
        )

    def local_sums(t, own):
        columns = jnp.zeros((CP, LANES), F32)
        for r in range(-1, height + 1):
            t_low, t_mid, t_high = (summed(j, r) for j in (-1, 0, 1))
            total = inner(t_low, t_mid, t_high)
            ubuf[t, :, block(1, r)] = total + own(r) if 0 <= r < height and own else total
            columns = gathered(columns, r, jnp.where(first_lane, t_low, t_high))
        return columns

    def send_rim(t, above, below, columns):
        brow[t, 0] = above.astype(BF16)
        brow[t, 1] = below.astype(BF16)
        bcol[t] = columns.astype(BF16)
        src, dst = rim_sources(t), rim_targets(t)
        for d in (UP, DOWN, LEFT, RIGHT, UL, UR, DL, DR):
            send(src[d], dst[opposite[d]], t, d, bsend, brecv)

    def receive_rim(t):
        dst = rim_targets(t)
        for d in range(8):
            wait_recv(dst[d], t, d, bsend, brecv)
        for there, row, slots in ((has_up, 0, (2, 3)), (has_down, 1, (4, 5))):

            @pl.when(jnp.logical_not(there))
            def _():
                rrow[t, row] = jnp.zeros((CP, LANES), BF16)
                for slot in slots:
                    rcol[t, slot] = jnp.zeros((CP, LANES), BF16)

        from_left, from_right, ul, ur, dl, dr = (rcol[t, k].astype(F32) for k in range(6))
        inside = jnp.logical_and(slot_of >= 2, slot_of < height + 2)
        inflow = jnp.where(inside, jnp.where(even, rolled(from_left, 1), rolled(from_right, -1)), 0.0)
        top, bottom, past, before = spot(0), spot(height - 1), spot(height), spot(-1)
        for value, came, goes in (
            (ul, past - 1, top), (ur, past, top - 1), (dl, before - 1, bottom), (dr, before, bottom - 1),
        ):
            inflow = inflow + jnp.where(lane == goes, rolled(value, goes - came), 0.0)
        return rrow[t, 0].astype(F32), rrow[t, 1].astype(F32), inflow

    products(lambda n: hist[last[n]], slope2)
    columns = local_sums(0, lambda r: hist[last[r // 2]][:, (r % 2) * LANES : (r % 2 + 1) * LANES])
    send_rim(0, ubuf[0, :, block(1, -1)], ubuf[0, :, block(1, height)], columns)

    to_some(0, 2, give_back)
    products(lambda n: ubuf[0, :, block(1, 2 * n, 2)], slope1)
    columns = local_sums(1, None)
    at_edge = jnp.zeros((CP, LANES), F32)
    for r in range(height):
        at_edge = gathered(at_edge, r, ubuf[0, :, block(1, r)])
    to_some(1, 2, give_back)
    above, below, inflow = receive_rim(0)
    far = height - 1
    at_edge = at_edge + inflow
    at_edge = at_edge + gathered(gathered(jnp.zeros((CP, LANES), F32), 0, above), far, below)
    late = spread_of(
        jnp.concatenate([above, below, apart(at_edge)], axis=1),
        jnp.concatenate(
            [slope1[:, pl.ds(0, LANES)], slope1[:, pl.ds(far * LANES, LANES)], slope_edge[...]], axis=1
        ),
    )
    for i in range(3):
        xbuf[pl.ds(3 * i * CP, 3 * CP), :] = dot(wk[i, pl.ds(0, 3 * CP), :], late)

    def late_tap(i, j, part):
        return xbuf[pl.ds((3 * (i + 1) + j + 1) * CP, CP), pl.ds(part * LANES, LANES)]

    def late_row(part, i):
        return tuple(late_tap(i, j, part) for j in (-1, 0, 1))

    to_low, to_same, to_high = (
        sum(rolled(late_tap(i, j, 2), 2 * i) for i in (-1, 0, 1)) for j in (-1, 0, 1)
    )
    outside = slot_of <= height + 2
    columns = columns + jnp.where(outside, jnp.where(even, to_low, rolled(to_high, -LANES // 2 - 1)), 0.0)
    for part, base in ((0, 0), (1, far)):
        for i in (-1, 0, 1):
            t_low, _, t_high = late_row(part, i)
            columns = columns + gathered(
                jnp.zeros((CP, LANES), F32), base + i, jnp.where(first_lane, t_low, t_high)
            )
    same = joined(to_same)
    next_in = jnp.where(even, rolled(to_low, -LANES // 2 - 2), rolled(to_high, 1))
    second = jnp.logical_or(lane == 1, lane == LANES - 2)

    def from_columns(r, outermost):
        return jnp.where(edge, rolled(outermost, -spot(r)), 0.0) + jnp.where(second, rolled(next_in, -spot(r)), 0.0)

    send_rim(
        1,
        ubuf[1, :, block(1, -1)] + inner(*late_row(0, -1)) + from_columns(-1, same),
        ubuf[1, :, block(1, height)] + inner(*late_row(1, 1)) + from_columns(height, same),
        columns,
    )
    outermost = same + inflow
    for r in range(height):
        value = ubuf[0, :, block(1, r)] + ubuf[1, :, block(1, r)] + from_columns(r, outermost)
        if r < 2:
            value = value + inner(*late_row(0, r))
        if r >= far - 1:
            value = value + inner(*late_row(1, r - far))
        if r == 0:
            value = value + above
        if r == far:
            value = value + below
        ubuf[0, :, block(1, r)] = value
    above, below, inflow = receive_rim(1)
    for r in range(height):
        value = ubuf[0, :, block(1, r)] + jnp.where(edge, rolled(inflow, -spot(r)), 0.0)
        if r == 0:
            value = value + above
        if r == far:
            value = value + below
        here = pl.ds(r, chan, stride=height)
        grad_ref[here, :] = grad_ref[here, :] + value[:chan]

    rows = pl.ds(0, owners - 1)
    pltpu.make_async_remote_copy(
        src_ref=inn.at[rows], dst_ref=inn_recv.at[rows], send_sem=isend, recv_sem=irecv,
        device_id=ids[RIGHT], device_id_type=MESH,
    ).wait()
    innov_ref[...] = inn_recv[...].reshape(owners, LANES)
    for d in range(8):
        wait_send(state_sources[d], 0, d, fsend, frecv)
    for t in range(2):
        src = rim_sources(t)
        for d in range(8):
            wait_send(src[d], t, d, bsend, brecv)


def hand_over(gradient_in, innov_in, gradient_out, innov_out, gradient_held, innov_held, sems):
    chan = gradient_in.shape[0]
    cuts = [chan * k // PIECES for k in range(PIECES + 1)]
    parts = [pl.ds(a, b - a) for a, b in zip(cuts, cuts[1:])]
    routes = [(gradient_in.at[p], gradient_held.at[p], gradient_out.at[p]) for p in parts]
    routes.append((innov_in, innov_held, innov_out))
    reads = [pltpu.make_async_copy(src, held, sems.at[0, k]) for k, (src, held, _) in enumerate(routes)]
    writes = [pltpu.make_async_copy(held, dst, sems.at[1, k]) for k, (_, held, dst) in enumerate(routes)]
    for read in reads:
        read.start()
    for read, write in zip(reads, writes):
        read.wait()
        write.start()
    for write in writes:
        write.wait()


def local(
    n_lat, n_lon,
    initial_state, background_state, background_precision, conv_weight, conv_bias, out_weight,
    swath_patch, obs_cell, obs_weights, obs_value, obs_precision,
):
    chan, height, breadth = initial_state.shape
    hid = conv_weight.shape[2]
    owners = n_lat * n_lon
    chunks = height // 2
    cells = height * breadth
    vmem = pl.BlockSpec(memory_space=pltpu.VMEM)
    hbm = pl.BlockSpec(memory_space=pltpu.HBM)
    smem = pl.BlockSpec(memory_space=pltpu.SMEM)
    dma = pltpu.SemaphoreType.DMA
    gradient, innov = pl.pallas_call(
        functools.partial(kernel, n_lat, n_lon, hid),
        out_shape=(
            jax.ShapeDtypeStruct((chan * height, LANES), F32),
            jax.ShapeDtypeStruct((owners, LANES), F32),
        ),
        in_specs=[hbm, hbm, smem, vmem, vmem, vmem, smem] + [hbm] * 4,
        out_specs=(vmem, vmem),
        scratch_shapes=[
            pltpu.VMEM((chan, height, breadth), BF16),
            pltpu.VMEM((chan, height, breadth), BF16),
            pltpu.VMEM((owners, LANES), jnp.int32),
            pltpu.VMEM((4, owners, LANES), F32),
            pltpu.VMEM((owners, LANES), F32),
            pltpu.VMEM((owners, LANES), F32),
            pltpu.VMEM((LANES, hid), F32),
            pltpu.VMEM((3, hid, hid), BF16),
            pltpu.VMEM((3, hid, hid), BF16),
            pltpu.VMEM((CP, hid), BF16),
            pltpu.VMEM((hid, LANES), BF16),
            pltpu.VMEM((CP * height, LANES), F32),
            pltpu.VMEM((owners * 8, LANES), F32),
            pltpu.VMEM((owners * 8, LANES), F32),
            pltpu.VMEM((hid, (height + 4) * LANES), BF16),
            pltpu.VMEM((hid, (height + 2) * LANES), BF16),
            pltpu.VMEM((3, hid, WIDE), BF16),
            pltpu.VMEM((chunks, CP, WIDE), BF16),
            pltpu.VMEM((hid, cells), F32),
            pltpu.VMEM((hid, cells), F32),
            pltpu.VMEM((hid, LANES), F32),
            pltpu.VMEM((2, CP, LANES), BF16),
            pltpu.VMEM((6, CP, LANES), BF16),
            pltpu.VMEM((owners, WIDE, LANES), BF16),
            pltpu.VMEM((owners, CP, LANES), BF16),
            pltpu.VMEM((owners, 1, LANES), F32),
            pltpu.VMEM((owners, 1, LANES), F32),
            pltpu.VMEM((owners + 1, CP, WIDE), F32),
            pltpu.VMEM((9 * CP, cells), F32),
            pltpu.VMEM((9 * CP, 3 * LANES), F32),
            pltpu.VMEM((2, CP, (height + 2) * LANES), F32),
            pltpu.VMEM((2, 2, CP, LANES), BF16),
            pltpu.VMEM((2, CP, LANES), BF16),
            pltpu.VMEM((2, 2, CP, LANES), BF16),
            pltpu.VMEM((2, 6, CP, LANES), BF16),
            dma((1, 8)), dma((1, 8)), dma((2, 8)), dma((2, 8)),
            dma, dma, dma, dma, dma((6,)),
        ],
        compiler_params=pltpu.CompilerParams(
            collective_id=0, has_side_effects=True, vmem_limit_bytes=56 * 1024 * 1024
        ),
    )(
        initial_state, background_state, background_precision[None], conv_weight, conv_bias[None], out_weight, swath_patch,
        obs_cell[0], obs_weights[:, 0], obs_value[0], obs_precision[0],
    )
    return pl.pallas_call(
        hand_over,
        out_shape=(
            jax.ShapeDtypeStruct((chan, height, breadth), F32),
            jax.ShapeDtypeStruct((1, owners, LANES), F32),
        ),
        in_specs=[hbm, hbm],
        out_specs=(hbm, hbm),
        scratch_shapes=[
            pltpu.VMEM((chan, height, breadth), F32),
            pltpu.VMEM((1, owners, LANES), F32),
            dma((2, PIECES + 1)),
        ],
        compiler_params=pltpu.CompilerParams(vmem_limit_bytes=56 * 1024 * 1024),
    )(gradient.reshape(chan, height, breadth), innov[None])


def solution(mesh):
    tile = P(None, "lat", "lon")
    owner = ("lat", "lon")
    in_specs = (
        tile, tile, P(), P(), P(), P(),
        P(owner, None), P(owner, None, None), P(None, owner, None, None), P(owner, None, None), P(owner, None, None),
    )
    return jax.shard_map(
        functools.partial(local, mesh.shape["lat"], mesh.shape["lon"]),
        mesh=mesh, in_specs=in_specs, out_specs=(tile, P(owner, None, None)), check_vma=False,
    )
```

```python
import functools

import jax
import jax.numpy as jnp
from jax import lax
from jax.experimental import pallas as pl
from jax.experimental.pallas import tpu as pltpu
from jax.sharding import PartitionSpec as P

MESH = pl.DeviceIdType.MESH
F32 = jnp.float32
BF16 = jnp.bfloat16
CP = 80
LANES = 128
WIDE = 256
ROOT_HALF = 0.7071067811865476
NORM_DENSITY = 0.3989422804014327
UP, DOWN, LEFT, RIGHT, UL, UR, DL, DR = range(8)
GROUP = 32
LAG = 3
PIECES = 3
WORD = 65536
HALF_WORD = 32768
HALF_WORDS = 65535.0
TOP_PRECISION = 3.0
VALUE_STEPS = 2.0**28


def dot(a, b):
    return jnp.dot(a, b, preferred_element_type=F32)


def lane_iota(rows):
    return lax.broadcasted_iota(jnp.int32, (rows, LANES), 1)


def kernel(
    n_lat, n_lon, hid,
    x_hbm, xb_hbm, bp_ref, cw_ref, cb_ref, ow_ref, swath_ref, cell_hbm, w_hbm, val_hbm, prec_hbm,
    grad_ref, innov_ref,
    x_ref, xb_ref, cell_ref, w_ref, val_ref, prec_ref, wpad, wk, wt_ref, wo_ref, wot_ref, x32, packed, recv, opened, s1, s2, se, sobs, slope1, slope2, slope_edge, csend, hcol,
    bsc, qsc, inn, inn_recv, hist, ybuf, xbuf, ubuf, brow, bcol, rrow, rcol,
    fsend, frecv, bsend, brecv, psend, precv, isend, irecv, loaded,
):
    chan, height = x_ref.shape[0], x_ref.shape[1]
    owners = n_lat * n_lon
    chunks = height // 2
    lat = lax.axis_index("lat")
    lon = lax.axis_index("lon")
    me = lat * n_lon + lon
    has_up = lat > 0
    has_down = lat < n_lat - 1
    left = lax.rem(lon + n_lon - 1, n_lon)
    right = lax.rem(lon + 1, n_lon)
    ids = {
        UP: (lat - 1, lon), DOWN: (lat + 1, lon), LEFT: (lat, left), RIGHT: (lat, right),
        UL: (lat - 1, left), UR: (lat - 1, right), DL: (lat + 1, left), DR: (lat + 1, right),
    }
    opposite = {UP: DOWN, DOWN: UP, LEFT: RIGHT, RIGHT: LEFT, UL: DR, DR: UL, UR: DL, DL: UR}

    barrier = pltpu.get_barrier_semaphore()

    def wrapped(value, count):
        return value - jnp.where(value >= count, count, 0)

    rounds = [(step, ahead) for step in range(n_lat) for ahead in range(n_lon) if step or ahead]

    def to_some(part, parts, act):
        for step, ahead in rounds[len(rounds) * part // parts : len(rounds) * (part + 1) // parts]:
            there, column = wrapped(lat + step, n_lat), wrapped(lon + ahead, n_lon)
            act(there * n_lon + column, (there, column))

    def greet(_, where):
        pl.semaphore_signal(barrier, inc=1, device_id=where, device_id_type=MESH)

    loads = [
        pltpu.make_async_copy(src, dst, loaded.at[k])
        for k, (src, dst) in enumerate(
            (
                (x_hbm, x_ref), (xb_hbm, xb_ref), (cell_hbm, cell_ref),
                (w_hbm, w_ref), (val_hbm, val_ref), (prec_hbm, prec_ref),
            )
        )
    ]
    for load in loads:
        load.start()
    to_some(0, 1, greet)

    x32[pl.ds(chan * height, (CP - chan) * height), :] = jnp.zeros(((CP - chan) * height, LANES), F32)
    loads[0].wait()
    x32[pl.ds(0, chan * height), :] = x_ref[...].astype(F32).reshape(chan * height, LANES)
    lane = lane_iota(CP)
    first_lane = lane == 0
    last_lane = lane == LANES - 1

    def block(rim, r, count=1):
        return pl.ds((r + rim) * LANES, count * LANES)

    def rolled(value, shift):
        return pltpu.roll(value, shift % LANES, 1) if shift % LANES else value

    def spot(r):
        return 2 * (r + 2)

    even = lax.rem(lane, 2) == 0
    edge = jnp.logical_or(first_lane, last_lane)
    slot_of = (lane + 1) // 2

    def joined(value):
        return jnp.where(even, value, rolled(value, -LANES // 2 - 1))

    def apart(value):
        return jnp.where(lane < LANES // 2, value, rolled(value, LANES // 2 + 1))

    def gathered(total, r, row):
        return jnp.where(slot_of == r + 2, rolled(row, spot(r)), total)

    pair_of = lane // 2
    to_left = jnp.zeros((CP, LANES), F32)
    to_right = jnp.zeros((CP, LANES), F32)
    for r in range(height):
        row = x32[pl.ds(r, CP, stride=height), :]
        s1[pl.ds(CP, CP), block(2, r)] = row.astype(BF16)
        s1[pl.ds(0, CP), block(2, r)] = rolled(row, 1).astype(BF16)
        s1[pl.ds(2 * CP, CP), block(2, r)] = rolled(row, -1).astype(BF16)
        to_left = jnp.where(pair_of == r + 2, rolled(row, spot(r)), to_left)
        to_right = jnp.where(pair_of == r + 2, rolled(row, spot(r) + 2), to_right)
    csend[0] = to_left.astype(BF16)
    csend[1] = to_right.astype(BF16)

    def guarded(d):
        if d in (UP, UL, UR):
            return pl.when(has_up)
        if d in (DOWN, DL, DR):
            return pl.when(has_down)
        return lambda f: f()

    def send(src, dst, t, d, sends, recvs):
        copy = pltpu.make_async_remote_copy(
            src_ref=src, dst_ref=dst, send_sem=sends.at[t, d], recv_sem=recvs.at[t, opposite[d]],
            device_id=ids[d], device_id_type=MESH,
        )
        guarded(d)(copy.start)

    def wait_recv(dst, t, d, sends, recvs):
        copy = pltpu.make_async_remote_copy(
            src_ref=dst, dst_ref=dst, send_sem=sends.at[t, d], recv_sem=recvs.at[t, d],
            device_id=ids[d], device_id_type=MESH,
        )
        guarded(d)(copy.wait_recv)

    def wait_send(src, t, d, sends, recvs):
        copy = pltpu.make_async_remote_copy(
            src_ref=src, dst_ref=src, send_sem=sends.at[t, d], recv_sem=recvs.at[t, d],
            device_id=ids[d], device_id_type=MESH,
        )
        guarded(d)(copy.wait_send)

    def pair(r):
        return s1.at[pl.ds(CP, CP), block(2, r, 2)]

    state_sources = {
        UP: pair(0), DOWN: pair(height - 2),
        LEFT: csend.at[0], UL: csend.at[0], DL: csend.at[0],
        RIGHT: csend.at[1], UR: csend.at[1], DR: csend.at[1],
    }
    state_targets = {UP: pair(-2), DOWN: pair(height)}
    for k, d in enumerate((LEFT, RIGHT, UL, UR, DL, DR)):
        state_targets[d] = hcol.at[k]

    def send_state():
        for d in (UP, DOWN, LEFT, RIGHT, UL, UR, DL, DR):
            send(state_sources[d], state_targets[opposite[d]], 0, d, fsend, frecv)

    def receive_state():
        for d in range(8):
            wait_recv(state_targets[d], 0, d, fsend, frecv)
        for there, r, slots in ((has_up, -2, (2, 3)), (has_down, height, (4, 5))):

            @pl.when(jnp.logical_not(there))
            def _():
                s1[pl.ds(CP, CP), block(2, r, 2)] = jnp.zeros((CP, WIDE), BF16)
                for slot in slots:
                    hcol[slot] = jnp.zeros((CP, LANES), BF16)

    def shift_far_rows():
        for r in (-2, -1, height, height + 1):
            row = s1[pl.ds(CP, CP), block(2, r)].astype(F32)
            s1[pl.ds(0, CP), block(2, r)] = rolled(row, 1).astype(BF16)
            s1[pl.ds(2 * CP, CP), block(2, r)] = rolled(row, -1).astype(BF16)

    def merge_columns(at_edge, beside):
        at_edge, beside = joined(at_edge), joined(beside)
        for r in range(-1, height + 1):
            row = jnp.where(edge, rolled(at_edge, -spot(r)), s2[pl.ds(CP, CP), block(1, r)].astype(F32))
            outer = rolled(beside, -spot(r))
            s2[pl.ds(0, CP), block(1, r)] = jnp.where(first_lane, outer, rolled(row, 1)).astype(BF16)
            s2[pl.ds(CP, CP), block(1, r)] = row.astype(BF16)
            s2[pl.ds(2 * CP, CP), block(1, r)] = jnp.where(last_lane, outer, rolled(row, -1)).astype(BF16)

    def with_corners(side, above, below):
        middle = jnp.logical_and(pair_of >= 2, pair_of < height + 2)
        outer = jnp.where(pair_of < 2, rolled(above, -2 * height), rolled(below, 2 * height))
        return jnp.where(middle, side, outer)

    def spread_columns():
        from_left, from_right, ul, ur, dl, dr = (hcol[k].astype(F32) for k in range(6))
        low = with_corners(from_left, ul, dl)
        high = with_corners(from_right, ur, dr)
        first = csend[0].astype(F32)
        last = csend[1].astype(F32)
        for r in (-2, -1, height, height + 1):
            row = s1[pl.ds(CP, CP), block(2, r)].astype(F32)
            first = jnp.where(pair_of == r + 2, rolled(row, spot(r)), first)
            last = jnp.where(pair_of == r + 2, rolled(row, spot(r) + 2), last)
        on_left = lane < LANES // 2
        lefts = (low, rolled(low, -1), first, rolled(first, -1))
        rights = tuple(rolled(v, LANES // 2 - k) for v in (last, high) for k in (0, 1))
        beside = tuple(jnp.where(on_left, lefts[j], rights[j + 1]) for j in range(3))
        at_edge = tuple(jnp.where(on_left, lefts[j + 1], rights[j]) for j in range(3))
        for i in range(3):
            for j in range(3):
                part = pl.ds(j * CP, CP)
                se[i, part, pl.ds(0, LANES)] = rolled(beside[j], 2 * (1 - i)).astype(BF16)
                se[i, part, pl.ds(LANES, LANES)] = rolled(at_edge[j], 2 * (1 - i)).astype(BF16)
        return jnp.concatenate([beside[1], at_edge[1]], axis=1)

    def conv(window):
        return sum(dot(wt_ref[i], window(i)) for i in range(3))

    def network(pre, centre):
        cdf = 0.5 * (1.0 + lax.erf(pre * ROOT_HALF))
        update = dot(wo_ref[...], (pre * cdf).astype(BF16))
        return centre.astype(F32) + update, lambda: cdf + pre * jnp.exp(-0.5 * pre * pre) * NORM_DENSITY

    def conv_chunk(s, rim, n):
        return conv(lambda i: s[:, block(rim, 2 * n + i - 1, 2)])

    def forward_chunk(pre, s, rim, n, slope, inner_only):
        state, tangent = network(pre, s[pl.ds(CP, CP), block(rim, 2 * n, 2)])
        slope[:, pl.ds(n * WIDE, WIDE)] = jnp.where(edge_wide, 0.0, tangent()) if inner_only else tangent()
        return state.astype(BF16)

    def pipelined(order, start, finish, lag=1):
        order = list(order)
        held = [start(n) for n in order[:lag]]
        for k, n in enumerate(order):
            if k + lag < len(order):
                held.append(start(order[k + lag]))
            finish(n, held.pop(0))

    def first_rim(centre):
        up, down = has_up.astype(F32), has_down.astype(F32)
        rows = (-1, height)
        state, _ = network(
            conv(lambda i: jnp.concatenate([s1[:, block(2, r + i - 1)] for r in rows], axis=1)),
            jnp.concatenate([s1[pl.ds(CP, CP), block(2, r)] for r in rows], axis=1),
        )
        s2[pl.ds(CP, CP), block(1, -1)] = (state[:, :LANES] * up).astype(BF16)
        s2[pl.ds(CP, CP), block(1, height)] = (state[:, LANES:] * down).astype(BF16)
        sides, tangent = network(conv(lambda i: se[i]), centre)
        place = lax.rem(lane, LANES // 2)
        inside = jnp.where(place == spot(-1), up, jnp.where(place == spot(height), down, 1.0))
        here = lax.rem(lane_iota(hid), LANES // 2)
        kept = jnp.logical_and(lax.rem(here, 2) == 0, jnp.logical_and(here >= spot(0), here <= spot(height - 1)))
        slope_edge[...] = jnp.where(kept, tangent()[:, LANES:], 0.0)
        return tuple((sides[:, k * LANES : (k + 1) * LANES] * inside).astype(BF16).astype(F32) for k in (0, 1))

    pl.semaphore_wait(barrier, owners - 1)
    send_state()

    for load in loads[1:]:
        load.wait()
    def fixed(value, top):
        return jnp.round(value * (HALF_WORDS / top)).astype(jnp.int32)

    packed[:, 0, :] = (fixed(w_ref[0], 1.0) - HALF_WORD) * WORD + fixed(w_ref[1], 1.0)
    packed[:, 1, :] = (fixed(w_ref[2], 1.0) - HALF_WORD) * WORD + fixed(w_ref[3], 1.0)
    packed[:, 2, :] = cell_ref[...] * WORD + fixed(prec_ref[...], TOP_PRECISION)
    packed[:, 3, :] = jnp.round(val_ref[...] * VALUE_STEPS).astype(jnp.int32)

    def post(other, where):
        pltpu.make_async_remote_copy(
            src_ref=packed.at[other], dst_ref=recv.at[me],
            send_sem=psend, recv_sem=precv, device_id=where, device_id_type=MESH,
        ).start()

    recv[me] = packed[me]

    wpad[...] = jnp.zeros((LANES, hid), F32)
    bias = cb_ref[...]
    bias_parts = []
    for _ in range(3):
        part = bias.astype(BF16).astype(F32)
        bias_parts.append(part)
        bias = bias - part
    spare = lax.broadcasted_iota(jnp.int32, (hid - 3 * CP, hid), 0)
    bias_rows = jnp.zeros((hid - 3 * CP, hid), F32)
    for k, part in enumerate(bias_parts):
        bias_rows = jnp.where(spare == k, part, bias_rows)
    for i in range(3):
        for j in range(3):
            wpad[pl.ds(0, chan), :] = cw_ref[3 * i + j].astype(F32)
            wk[i, pl.ds(j * CP, CP), :] = wpad[pl.ds(0, CP), :].astype(BF16)
        wk[i, pl.ds(3 * CP, hid - 3 * CP), :] = (bias_rows if i == 1 else jnp.zeros_like(bias_rows)).astype(BF16)
        wt_ref[i] = jnp.transpose(wk[i].astype(F32)).astype(BF16)
    wpad[pl.ds(0, chan), :] = ow_ref[...].astype(F32)
    wo_ref[...] = wpad[pl.ds(0, CP), :].astype(BF16)
    wot_ref[...] = jnp.transpose(wpad[...]).astype(BF16)
    for c in range(chan):
        grad_ref[pl.ds(c * height, height), :] = bp_ref[0, c] * (x_ref[c].astype(F32) - xb_ref[c].astype(F32))

    def ones(breadth):
        return jnp.ones((hid - 3 * CP, breadth), BF16)

    s1[pl.ds(3 * CP, hid - 3 * CP), :] = ones((height + 4) * LANES)
    s2[pl.ds(3 * CP, hid - 3 * CP), :] = ones((height + 2) * LANES)
    for i in range(3):
        se[i, pl.ds(3 * CP, hid - 3 * CP), :] = ones(WIDE)

    column_wide = lax.broadcasted_iota(jnp.int32, (hid, WIDE), 1)
    column_wide = lax.rem(column_wide, LANES)
    edge_wide = jnp.logical_or(column_wide == 0, column_wide == LANES - 1)
    early = range(1, chunks - 1)

    def first_conv(n):
        return conv_chunk(s1, 2, n)

    def first_step(n, pre):
        s2[pl.ds(CP, CP), block(1, 2 * n, 2)] = forward_chunk(pre, s1, 2, n, slope1, True)

    def early_step(n, pre):
        to_some(n - 1, len(early), post)
        first_step(n, pre)

    pipelined(early, first_conv, early_step)
    receive_state()
    shift_far_rows()
    pipelined((0, chunks - 1), first_conv, first_step)
    beside, at_edge = first_rim(spread_columns())
    merge_columns(at_edge, beside)

    def second_step(n, pre):
        sobs[n] = forward_chunk(pre, s2, 1, n, slope2, False)

    pipelined(range(chunks), lambda n: conv_chunk(s2, 1, n), second_step)

    others = pl.ds(0, owners - 1)
    pltpu.make_async_remote_copy(
        src_ref=packed.at[others], dst_ref=recv.at[others], send_sem=psend, recv_sem=precv,
        device_id=ids[RIGHT], device_id_type=MESH,
    ).wait()

    def unfixed(value, top):
        return value.astype(F32) * (top / HALF_WORDS)

    def field(k, value):
        opened[pl.ds(k, owners, stride=8), :] = value

    words = recv[:, 2, :]
    field(0, (words >> 24).astype(F32))
    field(1, ((words >> 16) & (LANES - 1)).astype(F32))
    field(7, unfixed(words & (WORD - 1), TOP_PRECISION))
    for k in range(2):
        words = recv[:, k, :]
        field(2 + 2 * k, unfixed((words >> 16) + HALF_WORD, 1.0))
        field(3 + 2 * k, unfixed(words & (WORD - 1), 1.0))
    field(6, recv[:, 3, :].astype(F32) * (1.0 / VALUE_STEPS))
    column = lax.broadcasted_iota(jnp.int32, (LANES, LANES), 0).astype(F32).astype(BF16)
    channel = lax.broadcasted_iota(jnp.int32, (CP, LANES), 0).astype(F32)
    zero = jnp.zeros((LANES, LANES), BF16)

    def estimate(group, carry):
        def start(u):
            k = group * GROUP + u
            packet = opened[pl.ds(pl.multiple_of(k * 8, 8), 8), :]

            def row(which):
                return jnp.broadcast_to(packet[which : which + 1].astype(BF16), (LANES, LANES))

            at = row(1)
            here, after = column == at, column == at + 1
            table = jnp.concatenate(
                [
                    jnp.where(here, row(2), jnp.where(after, row(3), zero)),
                    jnp.where(here, row(4), jnp.where(after, row(5), zero)),
                ],
                axis=0,
            )
            bsc[k] = table
            return packet, dot(sobs[swath_ref[0, k]], table)

        def finish(u, given):
            k = group * GROUP + u
            packet, found = given
            picked = channel == packet[0:1]
            gap = jnp.sum(jnp.where(picked, found, 0.0), axis=0, keepdims=True) - packet[6:7]
            inn[k] = gap
            qsc[k] = jnp.where(picked, packet[7:8] * gap, 0.0).astype(BF16)

        pipelined(range(GROUP), start, finish, LAG)
        return carry

    lax.fori_loop(0, owners // GROUP, estimate, 0)
    hist[0] = jnp.zeros((CP, WIDE), F32)

    def pull(group, last):
        slots = [last]

        def start(u):
            k = group * GROUP + u
            return lax.dot_general(qsc[k], bsc[k], (((1,), (1,)), ((), ())), preferred_element_type=F32)

        def finish(u, share):
            k = group * GROUP + u
            patch = swath_ref[0, k]
            before = sum(jnp.where(patch == m, slots[-1][m], 0) for m in range(chunks))
            hist[k + 1] = hist[before] + share
            slots.append(tuple(jnp.where(patch == m, k + 1, slots[-1][m]) for m in range(chunks)))

        pipelined(range(GROUP), start, finish, LAG)
        return slots[-1]

    last = lax.fori_loop(0, owners // GROUP, pull, (jnp.int32(0),) * chunks)
    inn_recv[me] = inn[me]

    def give_back(other, where):
        pltpu.make_async_remote_copy(
            src_ref=inn.at[other], dst_ref=inn_recv.at[me], send_sem=isend, recv_sem=irecv,
            device_id=where, device_id_type=MESH,
        ).start()

    def tap(i, j, r):
        return ybuf[pl.ds((3 * (i + 1) + j + 1) * CP, CP), pl.ds(r * LANES, LANES)]

    def summed(j, r):
        total = None
        for i in (-1, 0, 1):
            if 0 <= r - i < height:
                part = tap(i, j, r - i)
                total = part if total is None else total + part
        return total

    def rim_sources(t):
        table = dict.fromkeys((LEFT, RIGHT, UL, UR, DL, DR), bcol.at[t])
        return table | {UP: brow.at[t, 0], DOWN: brow.at[t, 1]}

    def rim_targets(t):
        table = {d: rcol.at[t, k] for k, d in enumerate((LEFT, RIGHT, UL, UR, DL, DR))}
        return table | {UP: rrow.at[t, 0], DOWN: rrow.at[t, 1]}

    def spread_of(cotangent, slope):
        breadth = cotangent.shape[1]
        rounded = jnp.concatenate([cotangent.astype(BF16), jnp.zeros((LANES - CP, breadth), BF16)], axis=0)
        return (dot(wot_ref[...], rounded) * slope).astype(BF16)

    def products(cotangent, slope):
        def start(n):
            return spread_of(cotangent(n), slope[:, pl.ds(n * WIDE, WIDE)])

        def finish(n, spread):
            for i in range(3):
                ybuf[pl.ds(3 * i * CP, 3 * CP), pl.ds(n * WIDE, WIDE)] = dot(wk[i, pl.ds(0, 3 * CP), :], spread)

        pipelined(range(chunks), start, finish)

    def inner(t_low, t_mid, t_high):
        return (
            t_mid
            + jnp.where(first_lane, 0.0, rolled(t_high, 1))
            + jnp.where(last_lane, 0.0, rolled(t_low, -1))
        )

    def local_sums(t, own):
        columns = jnp.zeros((CP, LANES), F32)
        for r in range(-1, height + 1):
            t_low, t_mid, t_high = (summed(j, r) for j in (-1, 0, 1))
            total = inner(t_low, t_mid, t_high)
            ubuf[t, :, block(1, r)] = total + own(r) if 0 <= r < height and own else total
            columns = gathered(columns, r, jnp.where(first_lane, t_low, t_high))
        return columns

    def send_rim(t, above, below, columns):
        brow[t, 0] = above.astype(BF16)
        brow[t, 1] = below.astype(BF16)
        bcol[t] = columns.astype(BF16)
        src, dst = rim_sources(t), rim_targets(t)
        for d in (UP, DOWN, LEFT, RIGHT, UL, UR, DL, DR):
            send(src[d], dst[opposite[d]], t, d, bsend, brecv)

    def receive_rim(t):
        dst = rim_targets(t)
        for d in range(8):
            wait_recv(dst[d], t, d, bsend, brecv)
        for there, row, slots in ((has_up, 0, (2, 3)), (has_down, 1, (4, 5))):

            @pl.when(jnp.logical_not(there))
            def _():
                rrow[t, row] = jnp.zeros((CP, LANES), BF16)
                for slot in slots:
                    rcol[t, slot] = jnp.zeros((CP, LANES), BF16)

        from_left, from_right, ul, ur, dl, dr = (rcol[t, k].astype(F32) for k in range(6))
        inside = jnp.logical_and(slot_of >= 2, slot_of < height + 2)
        inflow = jnp.where(inside, jnp.where(even, rolled(from_left, 1), rolled(from_right, -1)), 0.0)
        top, bottom, past, before = spot(0), spot(height - 1), spot(height), spot(-1)
        for value, came, goes in (
            (ul, past - 1, top), (ur, past, top - 1), (dl, before - 1, bottom), (dr, before, bottom - 1),
        ):
            inflow = inflow + jnp.where(lane == goes, rolled(value, goes - came), 0.0)
        return rrow[t, 0].astype(F32), rrow[t, 1].astype(F32), inflow

    products(lambda n: hist[last[n]], slope2)
    columns = local_sums(0, lambda r: hist[last[r // 2]][:, (r % 2) * LANES : (r % 2 + 1) * LANES])
    send_rim(0, ubuf[0, :, block(1, -1)], ubuf[0, :, block(1, height)], columns)

    to_some(0, 2, give_back)
    products(lambda n: ubuf[0, :, block(1, 2 * n, 2)], slope1)
    columns = local_sums(1, None)
    at_edge = jnp.zeros((CP, LANES), F32)
    for r in range(height):
        at_edge = gathered(at_edge, r, ubuf[0, :, block(1, r)])
    to_some(1, 2, give_back)
    above, below, inflow = receive_rim(0)
    far = height - 1
    at_edge = at_edge + inflow
    at_edge = at_edge + gathered(gathered(jnp.zeros((CP, LANES), F32), 0, above), far, below)
    late = spread_of(
        jnp.concatenate([above, below, apart(at_edge)], axis=1),
        jnp.concatenate(
            [slope1[:, pl.ds(0, LANES)], slope1[:, pl.ds(far * LANES, LANES)], slope_edge[...]], axis=1
        ),
    )
    for i in range(3):
        xbuf[pl.ds(3 * i * CP, 3 * CP), :] = dot(wk[i, pl.ds(0, 3 * CP), :], late)

    def late_tap(i, j, part):
        return xbuf[pl.ds((3 * (i + 1) + j + 1) * CP, CP), pl.ds(part * LANES, LANES)]

    def late_row(part, i):
        return tuple(late_tap(i, j, part) for j in (-1, 0, 1))

    to_low, to_same, to_high = (
        sum(rolled(late_tap(i, j, 2), 2 * i) for i in (-1, 0, 1)) for j in (-1, 0, 1)
    )
    outside = slot_of <= height + 2
    columns = columns + jnp.where(outside, jnp.where(even, to_low, rolled(to_high, -LANES // 2 - 1)), 0.0)
    for part, base in ((0, 0), (1, far)):
        for i in (-1, 0, 1):
            t_low, _, t_high = late_row(part, i)
            columns = columns + gathered(
                jnp.zeros((CP, LANES), F32), base + i, jnp.where(first_lane, t_low, t_high)
            )
    same = joined(to_same)
    next_in = jnp.where(even, rolled(to_low, -LANES // 2 - 2), rolled(to_high, 1))
    second = jnp.logical_or(lane == 1, lane == LANES - 2)

    def from_columns(r, outermost):
        return jnp.where(edge, rolled(outermost, -spot(r)), 0.0) + jnp.where(second, rolled(next_in, -spot(r)), 0.0)

    send_rim(
        1,
        ubuf[1, :, block(1, -1)] + inner(*late_row(0, -1)) + from_columns(-1, same),
        ubuf[1, :, block(1, height)] + inner(*late_row(1, 1)) + from_columns(height, same),
        columns,
    )
    outermost = same + inflow
    for r in range(height):
        value = ubuf[0, :, block(1, r)] + ubuf[1, :, block(1, r)] + from_columns(r, outermost)
        if r < 2:
            value = value + inner(*late_row(0, r))
        if r >= far - 1:
            value = value + inner(*late_row(1, r - far))
        if r == 0:
            value = value + above
        if r == far:
            value = value + below
        ubuf[0, :, block(1, r)] = value
    above, below, inflow = receive_rim(1)
    for r in range(height):
        value = ubuf[0, :, block(1, r)] + jnp.where(edge, rolled(inflow, -spot(r)), 0.0)
        if r == 0:
            value = value + above
        if r == far:
            value = value + below
        here = pl.ds(r, chan, stride=height)
        grad_ref[here, :] = grad_ref[here, :] + value[:chan]

    rows = pl.ds(0, owners - 1)
    pltpu.make_async_remote_copy(
        src_ref=inn.at[rows], dst_ref=inn_recv.at[rows], send_sem=isend, recv_sem=irecv,
        device_id=ids[RIGHT], device_id_type=MESH,
    ).wait()
    innov_ref[...] = inn_recv[...].reshape(owners, LANES)
    for d in range(8):
        wait_send(state_sources[d], 0, d, fsend, frecv)
    for t in range(2):
        src = rim_sources(t)
        for d in range(8):
            wait_send(src[d], t, d, bsend, brecv)


def hand_over(gradient_in, innov_in, gradient_out, innov_out, gradient_held, innov_held, sems):
    chan = gradient_in.shape[0]
    cuts = [chan * k // PIECES for k in range(PIECES + 1)]
    parts = [pl.ds(a, b - a) for a, b in zip(cuts, cuts[1:])]
    routes = [(gradient_in.at[p], gradient_held.at[p], gradient_out.at[p]) for p in parts]
    routes.append((innov_in, innov_held, innov_out))
    reads = [pltpu.make_async_copy(src, held, sems.at[0, k]) for k, (src, held, _) in enumerate(routes)]
    writes = [pltpu.make_async_copy(held, dst, sems.at[1, k]) for k, (_, held, dst) in enumerate(routes)]
    for read in reads:
        read.start()
    for read, write in zip(reads, writes):
        read.wait()
        write.start()
    for write in writes:
        write.wait()


def local(
    n_lat, n_lon,
    initial_state, background_state, background_precision, conv_weight, conv_bias, out_weight,
    swath_patch, obs_cell, obs_weights, obs_value, obs_precision,
):
    chan, height, breadth = initial_state.shape
    hid = conv_weight.shape[2]
    owners = n_lat * n_lon
    chunks = height // 2
    cells = height * breadth
    vmem = pl.BlockSpec(memory_space=pltpu.VMEM)
    hbm = pl.BlockSpec(memory_space=pltpu.HBM)
    smem = pl.BlockSpec(memory_space=pltpu.SMEM)
    dma = pltpu.SemaphoreType.DMA
    gradient, innov = pl.pallas_call(
        functools.partial(kernel, n_lat, n_lon, hid),
        out_shape=(
            jax.ShapeDtypeStruct((chan * height, LANES), F32),
            jax.ShapeDtypeStruct((owners, LANES), F32),
        ),
        in_specs=[hbm, hbm, smem, vmem, vmem, vmem, smem] + [hbm] * 4,
        out_specs=(vmem, vmem),
        scratch_shapes=[
            pltpu.VMEM((chan, height, breadth), BF16),
            pltpu.VMEM((chan, height, breadth), BF16),
            pltpu.VMEM((owners, LANES), jnp.int32),
            pltpu.VMEM((4, owners, LANES), F32),
            pltpu.VMEM((owners, LANES), F32),
            pltpu.VMEM((owners, LANES), F32),
            pltpu.VMEM((LANES, hid), F32),
            pltpu.VMEM((3, hid, hid), BF16),
            pltpu.VMEM((3, hid, hid), BF16),
            pltpu.VMEM((CP, hid), BF16),
            pltpu.VMEM((hid, LANES), BF16),
            pltpu.VMEM((CP * height, LANES), F32),
            pltpu.VMEM((owners, 4, LANES), jnp.int32),
            pltpu.VMEM((owners, 4, LANES), jnp.int32),
            pltpu.VMEM((owners * 8, LANES), F32),
            pltpu.VMEM((hid, (height + 4) * LANES), BF16),
            pltpu.VMEM((hid, (height + 2) * LANES), BF16),
            pltpu.VMEM((3, hid, WIDE), BF16),
            pltpu.VMEM((chunks, CP, WIDE), BF16),
            pltpu.VMEM((hid, cells), F32),
            pltpu.VMEM((hid, cells), F32),
            pltpu.VMEM((hid, LANES), F32),
            pltpu.VMEM((2, CP, LANES), BF16),
            pltpu.VMEM((6, CP, LANES), BF16),
            pltpu.VMEM((owners, WIDE, LANES), BF16),
            pltpu.VMEM((owners, CP, LANES), BF16),
            pltpu.VMEM((owners, 1, LANES), F32),
            pltpu.VMEM((owners, 1, LANES), F32),
            pltpu.VMEM((owners + 1, CP, WIDE), F32),
            pltpu.VMEM((9 * CP, cells), F32),
            pltpu.VMEM((9 * CP, 3 * LANES), F32),
            pltpu.VMEM((2, CP, (height + 2) * LANES), F32),
            pltpu.VMEM((2, 2, CP, LANES), BF16),
            pltpu.VMEM((2, CP, LANES), BF16),
            pltpu.VMEM((2, 2, CP, LANES), BF16),
            pltpu.VMEM((2, 6, CP, LANES), BF16),
            dma((1, 8)), dma((1, 8)), dma((2, 8)), dma((2, 8)),
            dma, dma, dma, dma, dma((6,)),
        ],
        compiler_params=pltpu.CompilerParams(
            collective_id=0, has_side_effects=True, vmem_limit_bytes=56 * 1024 * 1024
        ),
    )(
        initial_state, background_state, background_precision[None], conv_weight, conv_bias[None], out_weight, swath_patch,
        obs_cell[0], obs_weights[:, 0], obs_value[0], obs_precision[0],
    )
    return pl.pallas_call(
        hand_over,
        out_shape=(
            jax.ShapeDtypeStruct((chan, height, breadth), F32),
            jax.ShapeDtypeStruct((1, owners, LANES), F32),
        ),
        in_specs=[hbm, hbm],
        out_specs=(hbm, hbm),
        scratch_shapes=[
            pltpu.VMEM((chan, height, breadth), F32),
            pltpu.VMEM((1, owners, LANES), F32),
            dma((2, PIECES + 1)),
        ],
        compiler_params=pltpu.CompilerParams(vmem_limit_bytes=56 * 1024 * 1024),
    )(gradient.reshape(chan, height, breadth), innov[None])


def solution(mesh):
    tile = P(None, "lat", "lon")
    owner = ("lat", "lon")
    in_specs = (
        tile, tile, P(), P(), P(), P(),
        P(owner, None), P(owner, None, None), P(None, owner, None, None), P(owner, None, None), P(owner, None, None),
    )
    return jax.shard_map(
        functools.partial(local, mesh.shape["lat"], mesh.shape["lon"]),
        mesh=mesh, in_specs=in_specs, out_specs=(tile, P(owner, None, None)), check_vma=False,
    )
```

```python
import functools

import jax
import jax.numpy as jnp
from jax import lax
from jax.experimental import pallas as pl
from jax.experimental.pallas import tpu as pltpu
from jax.sharding import PartitionSpec as P

MESH = pl.DeviceIdType.MESH
F32 = jnp.float32
BF16 = jnp.bfloat16
CP = 80
LANES = 128
WIDE = 256
ROOT_HALF = 0.7071067811865476
NORM_DENSITY = 0.3989422804014327
UP, DOWN, LEFT, RIGHT, UL, UR, DL, DR = range(8)
GROUP = 32
LAG = 3
PIECES = 3
WORD = 65536
HALF_WORD = 32768
HALF_WORDS = 65535.0
TOP_PRECISION = 3.0
VALUE_STEPS = 2.0**28


def dot(a, b):
    return jnp.dot(a, b, preferred_element_type=F32)


def lane_iota(rows):
    return lax.broadcasted_iota(jnp.int32, (rows, LANES), 1)


def kernel(
    n_lat, n_lon, hid,
    x_hbm, xb_hbm, bp_ref, cw_ref, cb_ref, ow_ref, swath_ref, cell_hbm, w_hbm, val_hbm, prec_hbm,
    grad_ref, innov_ref,
    x_ref, xb_ref, cell_ref, w_ref, val_ref, prec_ref, wpad, wk, wt_ref, wo_ref, wot_ref, x32, given, packed, recv, opened, s1, s2, se, sobs, slope1, slope2, slope_edge, csend, hcol,
    bsc, qsc, inn, inn_recv, inn_mate, hist, ybuf, xbuf, ubuf, brow, bcol, rrow, rcol,
    fsend, frecv, bsend, brecv, psend, precv, isend, irecv, gsend, grecv, loaded,
):
    chan, height = x_ref.shape[0], x_ref.shape[1]
    owners = n_lat * n_lon
    chunks = height // 2
    lat = lax.axis_index("lat")
    lon = lax.axis_index("lon")
    has_up = lat > 0
    has_down = lat < n_lat - 1
    left = lax.rem(lon + n_lon - 1, n_lon)
    right = lax.rem(lon + 1, n_lon)
    ids = {
        UP: (lat - 1, lon), DOWN: (lat + 1, lon), LEFT: (lat, left), RIGHT: (lat, right),
        UL: (lat - 1, left), UR: (lat - 1, right), DL: (lat + 1, left), DR: (lat + 1, right),
    }
    opposite = {UP: DOWN, DOWN: UP, LEFT: RIGHT, RIGHT: LEFT, UL: DR, DR: UL, UR: DL, DL: UR}

    barrier = pltpu.get_barrier_semaphore()

    def wrapped(value, count):
        return value - jnp.where(value >= count, count, 0)

    side, half = lax.rem(lat, 2), lat // 2
    halves = n_lat // 2
    pairs = halves * n_lon
    mate = {"lat": lat + 1 - 2 * side}
    my_pair = half * n_lon + lon
    rounds = [(step, ahead) for step in range(halves) for ahead in range(n_lon) if step or ahead]

    def to_some(part, parts, act):
        for step, ahead in rounds[len(rounds) * part // parts : len(rounds) * (part + 1) // parts]:
            there, column = wrapped(half + step, halves), wrapped(lon + ahead, n_lon)
            act(there * n_lon + column, (2 * there + side, column))

    def rows_of(which, ref):
        return jnp.concatenate(
            [ref[pl.ds(pl.multiple_of((2 * h + which) * n_lon, n_lon), n_lon), :] for h in range(halves)], axis=0
        )

    def greet(_, where):
        pl.semaphore_signal(barrier, inc=1, device_id=where, device_id_type=MESH)

    across = {UP: has_up, UL: has_up, UR: has_up, DOWN: has_down, DL: has_down, DR: has_down}

    loads = [
        pltpu.make_async_copy(src, dst, loaded.at[k])
        for k, (src, dst) in enumerate(
            (
                (x_hbm, x_ref), (xb_hbm, xb_ref), (cell_hbm, cell_ref),
                (w_hbm, w_ref), (val_hbm, val_ref), (prec_hbm, prec_ref),
            )
        )
    ]
    for load in loads:
        load.start()
    to_some(0, 1, greet)
    for d, there in across.items():
        pl.when(there)(functools.partial(greet, None, ids[d]))

    x32[pl.ds(chan * height, (CP - chan) * height), :] = jnp.zeros(((CP - chan) * height, LANES), F32)
    loads[0].wait()
    x32[pl.ds(0, chan * height), :] = x_ref[...].astype(F32).reshape(chan * height, LANES)
    lane = lane_iota(CP)
    first_lane = lane == 0
    last_lane = lane == LANES - 1

    def block(rim, r, count=1):
        return pl.ds((r + rim) * LANES, count * LANES)

    def rolled(value, shift):
        return pltpu.roll(value, shift % LANES, 1) if shift % LANES else value

    def spot(r):
        return 2 * (r + 2)

    even = lax.rem(lane, 2) == 0
    edge = jnp.logical_or(first_lane, last_lane)
    slot_of = (lane + 1) // 2

    def joined(value):
        return jnp.where(even, value, rolled(value, -LANES // 2 - 1))

    def apart(value):
        return jnp.where(lane < LANES // 2, value, rolled(value, LANES // 2 + 1))

    def gathered(total, r, row):
        return jnp.where(slot_of == r + 2, rolled(row, spot(r)), total)

    pair_of = lane // 2
    to_left = jnp.zeros((CP, LANES), F32)
    to_right = jnp.zeros((CP, LANES), F32)
    for r in range(height):
        row = x32[pl.ds(r, CP, stride=height), :]
        s1[pl.ds(CP, CP), block(2, r)] = row.astype(BF16)
        s1[pl.ds(0, CP), block(2, r)] = rolled(row, 1).astype(BF16)
        s1[pl.ds(2 * CP, CP), block(2, r)] = rolled(row, -1).astype(BF16)
        to_left = jnp.where(pair_of == r + 2, rolled(row, spot(r)), to_left)
        to_right = jnp.where(pair_of == r + 2, rolled(row, spot(r) + 2), to_right)
    csend[0] = to_left.astype(BF16)
    csend[1] = to_right.astype(BF16)

    def guarded(d):
        if d in (UP, UL, UR):
            return pl.when(has_up)
        if d in (DOWN, DL, DR):
            return pl.when(has_down)
        return lambda f: f()

    def send(src, dst, t, d, sends, recvs):
        copy = pltpu.make_async_remote_copy(
            src_ref=src, dst_ref=dst, send_sem=sends.at[t, d], recv_sem=recvs.at[t, opposite[d]],
            device_id=ids[d], device_id_type=MESH,
        )
        guarded(d)(copy.start)

    def wait_recv(dst, t, d, sends, recvs):
        copy = pltpu.make_async_remote_copy(
            src_ref=dst, dst_ref=dst, send_sem=sends.at[t, d], recv_sem=recvs.at[t, d],
            device_id=ids[d], device_id_type=MESH,
        )
        guarded(d)(copy.wait_recv)

    def wait_send(src, t, d, sends, recvs):
        copy = pltpu.make_async_remote_copy(
            src_ref=src, dst_ref=src, send_sem=sends.at[t, d], recv_sem=recvs.at[t, d],
            device_id=ids[d], device_id_type=MESH,
        )
        guarded(d)(copy.wait_send)

    def pair(r):
        return s1.at[pl.ds(CP, CP), block(2, r, 2)]

    state_sources = {
        UP: pair(0), DOWN: pair(height - 2),
        LEFT: csend.at[0], UL: csend.at[0], DL: csend.at[0],
        RIGHT: csend.at[1], UR: csend.at[1], DR: csend.at[1],
    }
    state_targets = {UP: pair(-2), DOWN: pair(height)}
    for k, d in enumerate((LEFT, RIGHT, UL, UR, DL, DR)):
        state_targets[d] = hcol.at[k]

    def send_state():
        for d in (UP, DOWN, LEFT, RIGHT, UL, UR, DL, DR):
            send(state_sources[d], state_targets[opposite[d]], 0, d, fsend, frecv)

    def receive_state():
        for d in range(8):
            wait_recv(state_targets[d], 0, d, fsend, frecv)
        for there, r, slots in ((has_up, -2, (2, 3)), (has_down, height, (4, 5))):

            @pl.when(jnp.logical_not(there))
            def _():
                s1[pl.ds(CP, CP), block(2, r, 2)] = jnp.zeros((CP, WIDE), BF16)
                for slot in slots:
                    hcol[slot] = jnp.zeros((CP, LANES), BF16)

    def shift_far_rows():
        for r in (-2, -1, height, height + 1):
            row = s1[pl.ds(CP, CP), block(2, r)].astype(F32)
            s1[pl.ds(0, CP), block(2, r)] = rolled(row, 1).astype(BF16)
            s1[pl.ds(2 * CP, CP), block(2, r)] = rolled(row, -1).astype(BF16)

    def merge_columns(at_edge, beside):
        at_edge, beside = joined(at_edge), joined(beside)
        for r in range(-1, height + 1):
            row = jnp.where(edge, rolled(at_edge, -spot(r)), s2[pl.ds(CP, CP), block(1, r)].astype(F32))
            outer = rolled(beside, -spot(r))
            s2[pl.ds(0, CP), block(1, r)] = jnp.where(first_lane, outer, rolled(row, 1)).astype(BF16)
            s2[pl.ds(CP, CP), block(1, r)] = row.astype(BF16)
            s2[pl.ds(2 * CP, CP), block(1, r)] = jnp.where(last_lane, outer, rolled(row, -1)).astype(BF16)

    def with_corners(side, above, below):
        middle = jnp.logical_and(pair_of >= 2, pair_of < height + 2)
        outer = jnp.where(pair_of < 2, rolled(above, -2 * height), rolled(below, 2 * height))
        return jnp.where(middle, side, outer)

    def spread_columns():
        from_left, from_right, ul, ur, dl, dr = (hcol[k].astype(F32) for k in range(6))
        low = with_corners(from_left, ul, dl)
        high = with_corners(from_right, ur, dr)
        first = csend[0].astype(F32)
        last = csend[1].astype(F32)
        for r in (-2, -1, height, height + 1):
            row = s1[pl.ds(CP, CP), block(2, r)].astype(F32)
            first = jnp.where(pair_of == r + 2, rolled(row, spot(r)), first)
            last = jnp.where(pair_of == r + 2, rolled(row, spot(r) + 2), last)
        on_left = lane < LANES // 2
        lefts = (low, rolled(low, -1), first, rolled(first, -1))
        rights = tuple(rolled(v, LANES // 2 - k) for v in (last, high) for k in (0, 1))
        beside = tuple(jnp.where(on_left, lefts[j], rights[j + 1]) for j in range(3))
        at_edge = tuple(jnp.where(on_left, lefts[j + 1], rights[j]) for j in range(3))
        for i in range(3):
            for j in range(3):
                part = pl.ds(j * CP, CP)
                se[i, part, pl.ds(0, LANES)] = rolled(beside[j], 2 * (1 - i)).astype(BF16)
                se[i, part, pl.ds(LANES, LANES)] = rolled(at_edge[j], 2 * (1 - i)).astype(BF16)
        return jnp.concatenate([beside[1], at_edge[1]], axis=1)

    def conv(window):
        return sum(dot(wt_ref[i], window(i)) for i in range(3))

    def network(pre, centre):
        cdf = 0.5 * (1.0 + lax.erf(pre * ROOT_HALF))
        update = dot(wo_ref[...], (pre * cdf).astype(BF16))
        return centre.astype(F32) + update, lambda: cdf + pre * jnp.exp(-0.5 * pre * pre) * NORM_DENSITY

    def conv_chunk(s, rim, n):
        return conv(lambda i: s[:, block(rim, 2 * n + i - 1, 2)])

    def forward_chunk(pre, s, rim, n, slope, inner_only):
        state, tangent = network(pre, s[pl.ds(CP, CP), block(rim, 2 * n, 2)])
        slope[:, pl.ds(n * WIDE, WIDE)] = jnp.where(edge_wide, 0.0, tangent()) if inner_only else tangent()
        return state.astype(BF16)

    def pipelined(order, start, finish, lag=1):
        order = list(order)
        held = [start(n) for n in order[:lag]]
        for k, n in enumerate(order):
            if k + lag < len(order):
                held.append(start(order[k + lag]))
            finish(n, held.pop(0))

    def first_rim(centre):
        up, down = has_up.astype(F32), has_down.astype(F32)
        rows = (-1, height)
        state, _ = network(
            conv(lambda i: jnp.concatenate([s1[:, block(2, r + i - 1)] for r in rows], axis=1)),
            jnp.concatenate([s1[pl.ds(CP, CP), block(2, r)] for r in rows], axis=1),
        )
        s2[pl.ds(CP, CP), block(1, -1)] = (state[:, :LANES] * up).astype(BF16)
        s2[pl.ds(CP, CP), block(1, height)] = (state[:, LANES:] * down).astype(BF16)
        sides, tangent = network(conv(lambda i: se[i]), centre)
        place = lax.rem(lane, LANES // 2)
        inside = jnp.where(place == spot(-1), up, jnp.where(place == spot(height), down, 1.0))
        here = lax.rem(lane_iota(hid), LANES // 2)
        kept = jnp.logical_and(lax.rem(here, 2) == 0, jnp.logical_and(here >= spot(0), here <= spot(height - 1)))
        slope_edge[...] = jnp.where(kept, tangent()[:, LANES:], 0.0)
        return tuple((sides[:, k * LANES : (k + 1) * LANES] * inside).astype(BF16).astype(F32) for k in (0, 1))

    pl.semaphore_wait(barrier, pairs - 1 + 3 * (has_up.astype(jnp.int32) + has_down.astype(jnp.int32)))
    send_state()

    for load in loads[1:]:
        load.wait()
    def fixed(value, top):
        return jnp.round(value * (HALF_WORDS / top)).astype(jnp.int32)

    def packet_words(which):
        first, second, third, fourth = (fixed(rows_of(which, w_ref.at[k]), 1.0) for k in range(4))
        return (
            (first - HALF_WORD) * WORD + second,
            (third - HALF_WORD) * WORD + fourth,
            rows_of(which, cell_ref) * WORD + fixed(rows_of(which, prec_ref), TOP_PRECISION),
            jnp.round(rows_of(which, val_ref) * VALUE_STEPS).astype(jnp.int32),
        )

    for k, word in enumerate(packet_words(1 - side)):
        given[:, k, :] = word
    to_mate = pltpu.make_async_remote_copy(
        src_ref=given, dst_ref=packed.at[1], send_sem=gsend.at[0], recv_sem=grecv.at[0],
        device_id=mate, device_id_type=MESH,
    )
    to_mate.start()
    for k, word in enumerate(packet_words(side)):
        packed[0, :, k, :] = word

    def post(other, where):
        pltpu.make_async_remote_copy(
            src_ref=packed.at[:, other], dst_ref=recv.at[:, my_pair],
            send_sem=psend, recv_sem=precv, device_id=where, device_id_type=MESH,
        ).start()

    wpad[...] = jnp.zeros((LANES, hid), F32)
    bias = cb_ref[...]
    bias_parts = []
    for _ in range(3):
        part = bias.astype(BF16).astype(F32)
        bias_parts.append(part)
        bias = bias - part
    spare = lax.broadcasted_iota(jnp.int32, (hid - 3 * CP, hid), 0)
    bias_rows = jnp.zeros((hid - 3 * CP, hid), F32)
    for k, part in enumerate(bias_parts):
        bias_rows = jnp.where(spare == k, part, bias_rows)
    for i in range(3):
        for j in range(3):
            wpad[pl.ds(0, chan), :] = cw_ref[3 * i + j].astype(F32)
            wk[i, pl.ds(j * CP, CP), :] = wpad[pl.ds(0, CP), :].astype(BF16)
        wk[i, pl.ds(3 * CP, hid - 3 * CP), :] = (bias_rows if i == 1 else jnp.zeros_like(bias_rows)).astype(BF16)
        wt_ref[i] = jnp.transpose(wk[i].astype(F32)).astype(BF16)
    wpad[pl.ds(0, chan), :] = ow_ref[...].astype(F32)
    wo_ref[...] = wpad[pl.ds(0, CP), :].astype(BF16)
    wot_ref[...] = jnp.transpose(wpad[...]).astype(BF16)
    for c in range(chan):
        grad_ref[pl.ds(c * height, height), :] = bp_ref[0, c] * (x_ref[c].astype(F32) - xb_ref[c].astype(F32))

    def ones(breadth):
        return jnp.ones((hid - 3 * CP, breadth), BF16)

    s1[pl.ds(3 * CP, hid - 3 * CP), :] = ones((height + 4) * LANES)
    s2[pl.ds(3 * CP, hid - 3 * CP), :] = ones((height + 2) * LANES)
    for i in range(3):
        se[i, pl.ds(3 * CP, hid - 3 * CP), :] = ones(WIDE)

    column_wide = lax.broadcasted_iota(jnp.int32, (hid, WIDE), 1)
    column_wide = lax.rem(column_wide, LANES)
    edge_wide = jnp.logical_or(column_wide == 0, column_wide == LANES - 1)
    early = range(1, chunks - 1)

    def first_conv(n):
        return conv_chunk(s1, 2, n)

    def first_step(n, pre):
        s2[pl.ds(CP, CP), block(1, 2 * n, 2)] = forward_chunk(pre, s1, 2, n, slope1, True)

    def early_step(n, pre):
        to_some(n - 1, len(early), post)
        first_step(n, pre)

    to_mate.wait_recv()
    recv[:, my_pair] = packed[:, my_pair]
    pipelined(early, first_conv, early_step)
    receive_state()
    shift_far_rows()
    pipelined((0, chunks - 1), first_conv, first_step)
    beside, at_edge = first_rim(spread_columns())
    merge_columns(at_edge, beside)

    def second_step(n, pre):
        sobs[n] = forward_chunk(pre, s2, 1, n, slope2, False)

    pipelined(range(chunks), lambda n: conv_chunk(s2, 1, n), second_step)

    others = pl.ds(0, pairs - 1)
    pltpu.make_async_remote_copy(
        src_ref=packed.at[:, others], dst_ref=recv.at[:, others], send_sem=psend, recv_sem=precv,
        device_id=ids[RIGHT], device_id_type=MESH,
    ).wait()

    def unfixed(value, top):
        return value.astype(F32) * (top / HALF_WORDS)

    for which in range(2):

        def field(k, value, which=which):
            opened[pl.ds(which * pairs * 8 + k, pairs, stride=8), :] = value

        words = recv[which, :, 2, :]
        field(0, (words >> 24).astype(F32))
        field(1, ((words >> 16) & (LANES - 1)).astype(F32))
        field(7, unfixed(words & (WORD - 1), TOP_PRECISION))
        for k in range(2):
            words = recv[which, :, k, :]
            field(2 + 2 * k, unfixed((words >> 16) + HALF_WORD, 1.0))
            field(3 + 2 * k, unfixed(words & (WORD - 1), 1.0))
        field(6, recv[which, :, 3, :].astype(F32) * (1.0 / VALUE_STEPS))

    def patch_of(group, u):
        k = group * GROUP + u
        which, pair_id = k // pairs, lax.rem(k, pairs)
        at_side = jnp.where(which == 0, side, 1 - side)
        owner = (2 * (pair_id // n_lon) + at_side) * n_lon + lax.rem(pair_id, n_lon)
        return swath_ref[0, owner]

    column = lax.broadcasted_iota(jnp.int32, (LANES, LANES), 0).astype(F32).astype(BF16)
    channel = lax.broadcasted_iota(jnp.int32, (CP, LANES), 0).astype(F32)
    zero = jnp.zeros((LANES, LANES), BF16)

    def estimate(group, carry):
        def start(u):
            k = group * GROUP + u
            packet = opened[pl.ds(pl.multiple_of(k * 8, 8), 8), :]

            def row(which):
                return jnp.broadcast_to(packet[which : which + 1].astype(BF16), (LANES, LANES))

            at = row(1)
            here, after = column == at, column == at + 1
            table = jnp.concatenate(
                [
                    jnp.where(here, row(2), jnp.where(after, row(3), zero)),
                    jnp.where(here, row(4), jnp.where(after, row(5), zero)),
                ],
                axis=0,
            )
            bsc[k] = table
            return packet, dot(sobs[patch_of(group, u)], table)

        def finish(u, given):
            k = group * GROUP + u
            packet, found = given
            picked = channel == packet[0:1]
            gap = jnp.sum(jnp.where(picked, found, 0.0), axis=0, keepdims=True) - packet[6:7]
            inn[k // pairs, lax.rem(k, pairs)] = gap
            qsc[k] = jnp.where(picked, packet[7:8] * gap, 0.0).astype(BF16)

        pipelined(range(GROUP), start, finish, LAG)
        return carry

    lax.fori_loop(0, owners // GROUP, estimate, 0)
    hist[0] = jnp.zeros((CP, WIDE), F32)

    def pull(group, last):
        slots = [last]

        def start(u):
            k = group * GROUP + u
            return lax.dot_general(qsc[k], bsc[k], (((1,), (1,)), ((), ())), preferred_element_type=F32)

        def finish(u, share):
            k = group * GROUP + u
            patch = patch_of(group, u)
            before = sum(jnp.where(patch == m, slots[-1][m], 0) for m in range(chunks))
            hist[k + 1] = hist[before] + share
            slots.append(tuple(jnp.where(patch == m, k + 1, slots[-1][m]) for m in range(chunks)))

        pipelined(range(GROUP), start, finish, LAG)
        return slots[-1]

    last = lax.fori_loop(0, owners // GROUP, pull, (jnp.int32(0),) * chunks)
    inn_recv[:, my_pair] = inn[:, my_pair]

    def give_back(other, where):
        pltpu.make_async_remote_copy(
            src_ref=inn.at[:, other], dst_ref=inn_recv.at[:, my_pair],
            send_sem=isend, recv_sem=irecv, device_id=where, device_id_type=MESH,
        ).start()

    def tap(i, j, r):
        return ybuf[pl.ds((3 * (i + 1) + j + 1) * CP, CP), pl.ds(r * LANES, LANES)]

    def summed(j, r):
        total = None
        for i in (-1, 0, 1):
            if 0 <= r - i < height:
                part = tap(i, j, r - i)
                total = part if total is None else total + part
        return total

    def rim_sources(t):
        table = dict.fromkeys((LEFT, RIGHT, UL, UR, DL, DR), bcol.at[t])
        return table | {UP: brow.at[t, 0], DOWN: brow.at[t, 1]}

    def rim_targets(t):
        table = {d: rcol.at[t, k] for k, d in enumerate((LEFT, RIGHT, UL, UR, DL, DR))}
        return table | {UP: rrow.at[t, 0], DOWN: rrow.at[t, 1]}

    def spread_of(cotangent, slope):
        breadth = cotangent.shape[1]
        rounded = jnp.concatenate([cotangent.astype(BF16), jnp.zeros((LANES - CP, breadth), BF16)], axis=0)
        return (dot(wot_ref[...], rounded) * slope).astype(BF16)

    def products(cotangent, slope, beside=None):
        def start(n):
            return spread_of(cotangent(n), slope[:, pl.ds(n * WIDE, WIDE)])

        def finish(n, spread):
            if beside:
                to_some(n, chunks, beside)
            for i in range(3):
                ybuf[pl.ds(3 * i * CP, 3 * CP), pl.ds(n * WIDE, WIDE)] = dot(wk[i, pl.ds(0, 3 * CP), :], spread)

        pipelined(range(chunks), start, finish)

    def inner(t_low, t_mid, t_high):
        return (
            t_mid
            + jnp.where(first_lane, 0.0, rolled(t_high, 1))
            + jnp.where(last_lane, 0.0, rolled(t_low, -1))
        )

    def local_sums(t, own):
        columns = jnp.zeros((CP, LANES), F32)
        for r in range(-1, height + 1):
            t_low, t_mid, t_high = (summed(j, r) for j in (-1, 0, 1))
            total = inner(t_low, t_mid, t_high)
            ubuf[t, :, block(1, r)] = total + own(r) if 0 <= r < height and own else total
            columns = gathered(columns, r, jnp.where(first_lane, t_low, t_high))
        return columns

    def send_rim(t, above, below, columns):
        brow[t, 0] = above.astype(BF16)
        brow[t, 1] = below.astype(BF16)
        bcol[t] = columns.astype(BF16)
        src, dst = rim_sources(t), rim_targets(t)
        for d in (UP, DOWN, LEFT, RIGHT, UL, UR, DL, DR):
            send(src[d], dst[opposite[d]], t, d, bsend, brecv)

    def receive_rim(t):
        dst = rim_targets(t)
        for d in range(8):
            wait_recv(dst[d], t, d, bsend, brecv)
        for there, row, slots in ((has_up, 0, (2, 3)), (has_down, 1, (4, 5))):

            @pl.when(jnp.logical_not(there))
            def _():
                rrow[t, row] = jnp.zeros((CP, LANES), BF16)
                for slot in slots:
                    rcol[t, slot] = jnp.zeros((CP, LANES), BF16)

        from_left, from_right, ul, ur, dl, dr = (rcol[t, k].astype(F32) for k in range(6))
        inside = jnp.logical_and(slot_of >= 2, slot_of < height + 2)
        inflow = jnp.where(inside, jnp.where(even, rolled(from_left, 1), rolled(from_right, -1)), 0.0)
        top, bottom, past, before = spot(0), spot(height - 1), spot(height), spot(-1)
        for value, came, goes in (
            (ul, past - 1, top), (ur, past, top - 1), (dl, before - 1, bottom), (dr, before, bottom - 1),
        ):
            inflow = inflow + jnp.where(lane == goes, rolled(value, goes - came), 0.0)
        return rrow[t, 0].astype(F32), rrow[t, 1].astype(F32), inflow

    products(lambda n: hist[last[n]], slope2, give_back)
    columns = local_sums(0, lambda r: hist[last[r // 2]][:, (r % 2) * LANES : (r % 2 + 1) * LANES])
    send_rim(0, ubuf[0, :, block(1, -1)], ubuf[0, :, block(1, height)], columns)

    products(lambda n: ubuf[0, :, block(1, 2 * n, 2)], slope1)
    columns = local_sums(1, None)
    at_edge = jnp.zeros((CP, LANES), F32)
    for r in range(height):
        at_edge = gathered(at_edge, r, ubuf[0, :, block(1, r)])
    above, below, inflow = receive_rim(0)
    far = height - 1
    at_edge = at_edge + inflow
    at_edge = at_edge + gathered(gathered(jnp.zeros((CP, LANES), F32), 0, above), far, below)
    late = spread_of(
        jnp.concatenate([above, below, apart(at_edge)], axis=1),
        jnp.concatenate(
            [slope1[:, pl.ds(0, LANES)], slope1[:, pl.ds(far * LANES, LANES)], slope_edge[...]], axis=1
        ),
    )
    for i in range(3):
        xbuf[pl.ds(3 * i * CP, 3 * CP), :] = dot(wk[i, pl.ds(0, 3 * CP), :], late)

    def late_tap(i, j, part):
        return xbuf[pl.ds((3 * (i + 1) + j + 1) * CP, CP), pl.ds(part * LANES, LANES)]

    def late_row(part, i):
        return tuple(late_tap(i, j, part) for j in (-1, 0, 1))

    to_low, to_same, to_high = (
        sum(rolled(late_tap(i, j, 2), 2 * i) for i in (-1, 0, 1)) for j in (-1, 0, 1)
    )
    outside = slot_of <= height + 2
    columns = columns + jnp.where(outside, jnp.where(even, to_low, rolled(to_high, -LANES // 2 - 1)), 0.0)
    for part, base in ((0, 0), (1, far)):
        for i in (-1, 0, 1):
            t_low, _, t_high = late_row(part, i)
            columns = columns + gathered(
                jnp.zeros((CP, LANES), F32), base + i, jnp.where(first_lane, t_low, t_high)
            )
    same = joined(to_same)
    next_in = jnp.where(even, rolled(to_low, -LANES // 2 - 2), rolled(to_high, 1))
    second = jnp.logical_or(lane == 1, lane == LANES - 2)

    def from_columns(r, outermost):
        return jnp.where(edge, rolled(outermost, -spot(r)), 0.0) + jnp.where(second, rolled(next_in, -spot(r)), 0.0)

    send_rim(
        1,
        ubuf[1, :, block(1, -1)] + inner(*late_row(0, -1)) + from_columns(-1, same),
        ubuf[1, :, block(1, height)] + inner(*late_row(1, 1)) + from_columns(height, same),
        columns,
    )
    pltpu.make_async_remote_copy(
        src_ref=inn.at[:, others], dst_ref=inn_recv.at[:, others], send_sem=isend, recv_sem=irecv,
        device_id=ids[RIGHT], device_id_type=MESH,
    ).wait()
    innov_to_mate = pltpu.make_async_remote_copy(
        src_ref=inn_recv.at[1], dst_ref=inn_mate, send_sem=gsend.at[1], recv_sem=grecv.at[1],
        device_id=mate, device_id_type=MESH,
    )
    innov_to_mate.start()
    outermost = same + inflow
    for r in range(height):
        value = ubuf[0, :, block(1, r)] + ubuf[1, :, block(1, r)] + from_columns(r, outermost)
        if r < 2:
            value = value + inner(*late_row(0, r))
        if r >= far - 1:
            value = value + inner(*late_row(1, r - far))
        if r == 0:
            value = value + above
        if r == far:
            value = value + below
        ubuf[0, :, block(1, r)] = value
    above, below, inflow = receive_rim(1)
    for r in range(height):
        value = ubuf[0, :, block(1, r)] + jnp.where(edge, rolled(inflow, -spot(r)), 0.0)
        if r == 0:
            value = value + above
        if r == far:
            value = value + below
        here = pl.ds(r, chan, stride=height)
        grad_ref[here, :] = grad_ref[here, :] + value[:chan]

    innov_to_mate.wait()
    to_mate.wait_send()
    for h in range(halves):
        part = pl.ds(h * n_lon, n_lon)
        for which, ref in ((side, inn_recv.at[0]), (1 - side, inn_mate)):
            rows = pl.ds(pl.multiple_of((2 * h + which) * n_lon, n_lon), n_lon)
            innov_ref[rows, :] = ref[part].reshape(n_lon, LANES)
    for d in range(8):
        wait_send(state_sources[d], 0, d, fsend, frecv)
    for t in range(2):
        src = rim_sources(t)
        for d in range(8):
            wait_send(src[d], t, d, bsend, brecv)


def hand_over(gradient_in, innov_in, gradient_out, innov_out, gradient_held, innov_held, sems):
    chan = gradient_in.shape[0]
    cuts = [chan * k // PIECES for k in range(PIECES + 1)]
    parts = [pl.ds(a, b - a) for a, b in zip(cuts, cuts[1:])]
    routes = [(gradient_in.at[p], gradient_held.at[p], gradient_out.at[p]) for p in parts]
    routes.append((innov_in, innov_held, innov_out))
    reads = [pltpu.make_async_copy(src, held, sems.at[0, k]) for k, (src, held, _) in enumerate(routes)]
    writes = [pltpu.make_async_copy(held, dst, sems.at[1, k]) for k, (_, held, dst) in enumerate(routes)]
    for read in reads:
        read.start()
    for read, write in zip(reads, writes):
        read.wait()
        write.start()
    for write in writes:
        write.wait()


def local(
    n_lat, n_lon,
    initial_state, background_state, background_precision, conv_weight, conv_bias, out_weight,
    swath_patch, obs_cell, obs_weights, obs_value, obs_precision,
):
    chan, height, breadth = initial_state.shape
    hid = conv_weight.shape[2]
    owners = n_lat * n_lon
    chunks = height // 2
    cells = height * breadth
    vmem = pl.BlockSpec(memory_space=pltpu.VMEM)
    hbm = pl.BlockSpec(memory_space=pltpu.HBM)
    smem = pl.BlockSpec(memory_space=pltpu.SMEM)
    dma = pltpu.SemaphoreType.DMA
    gradient, innov = pl.pallas_call(
        functools.partial(kernel, n_lat, n_lon, hid),
        out_shape=(
            jax.ShapeDtypeStruct((chan * height, LANES), F32),
            jax.ShapeDtypeStruct((owners, LANES), F32),
        ),
        in_specs=[hbm, hbm, smem, vmem, vmem, vmem, smem] + [hbm] * 4,
        out_specs=(vmem, vmem),
        scratch_shapes=[
            pltpu.VMEM((chan, height, breadth), BF16),
            pltpu.VMEM((chan, height, breadth), BF16),
            pltpu.VMEM((owners, LANES), jnp.int32),
            pltpu.VMEM((4, owners, LANES), F32),
            pltpu.VMEM((owners, LANES), F32),
            pltpu.VMEM((owners, LANES), F32),
            pltpu.VMEM((LANES, hid), F32),
            pltpu.VMEM((3, hid, hid), BF16),
            pltpu.VMEM((3, hid, hid), BF16),
            pltpu.VMEM((CP, hid), BF16),
            pltpu.VMEM((hid, LANES), BF16),
            pltpu.VMEM((CP * height, LANES), F32),
            pltpu.VMEM((owners // 2, 4, LANES), jnp.int32),
            pltpu.VMEM((2, owners // 2, 4, LANES), jnp.int32),
            pltpu.VMEM((2, owners // 2, 4, LANES), jnp.int32),
            pltpu.VMEM((owners * 8, LANES), F32),
            pltpu.VMEM((hid, (height + 4) * LANES), BF16),
            pltpu.VMEM((hid, (height + 2) * LANES), BF16),
            pltpu.VMEM((3, hid, WIDE), BF16),
            pltpu.VMEM((chunks, CP, WIDE), BF16),
            pltpu.VMEM((hid, cells), F32),
            pltpu.VMEM((hid, cells), F32),
            pltpu.VMEM((hid, LANES), F32),
            pltpu.VMEM((2, CP, LANES), BF16),
            pltpu.VMEM((6, CP, LANES), BF16),
            pltpu.VMEM((owners, WIDE, LANES), BF16),
            pltpu.VMEM((owners, CP, LANES), BF16),
            pltpu.VMEM((2, owners // 2, 1, LANES), F32),
            pltpu.VMEM((2, owners // 2, 1, LANES), F32),
            pltpu.VMEM((owners // 2, 1, LANES), F32),
            pltpu.VMEM((owners + 1, CP, WIDE), F32),
            pltpu.VMEM((9 * CP, cells), F32),
            pltpu.VMEM((9 * CP, 3 * LANES), F32),
            pltpu.VMEM((2, CP, (height + 2) * LANES), F32),
            pltpu.VMEM((2, 2, CP, LANES), BF16),
            pltpu.VMEM((2, CP, LANES), BF16),
            pltpu.VMEM((2, 2, CP, LANES), BF16),
            pltpu.VMEM((2, 6, CP, LANES), BF16),
            dma((1, 8)), dma((1, 8)), dma((2, 8)), dma((2, 8)),
            dma, dma, dma, dma, dma((2,)), dma((2,)), dma((6,)),
        ],
        compiler_params=pltpu.CompilerParams(
            collective_id=0, has_side_effects=True, vmem_limit_bytes=56 * 1024 * 1024
        ),
    )(
        initial_state, background_state, background_precision[None], conv_weight, conv_bias[None], out_weight, swath_patch,
        obs_cell[0], obs_weights[:, 0], obs_value[0], obs_precision[0],
    )
    return pl.pallas_call(
        hand_over,
        out_shape=(
            jax.ShapeDtypeStruct((chan, height, breadth), F32),
            jax.ShapeDtypeStruct((1, owners, LANES), F32),
        ),
        in_specs=[hbm, hbm],
        out_specs=(hbm, hbm),
        scratch_shapes=[
            pltpu.VMEM((chan, height, breadth), F32),
            pltpu.VMEM((1, owners, LANES), F32),
            dma((2, PIECES + 1)),
        ],
        compiler_params=pltpu.CompilerParams(vmem_limit_bytes=56 * 1024 * 1024),
    )(gradient.reshape(chan, height, breadth), innov[None])


def solution(mesh):
    tile = P(None, "lat", "lon")
    owner = ("lat", "lon")
    in_specs = (
        tile, tile, P(), P(), P(), P(),
        P(owner, None), P(owner, None, None), P(None, owner, None, None), P(owner, None, None), P(owner, None, None),
    )
    return jax.shard_map(
        functools.partial(local, mesh.shape["lat"], mesh.shape["lon"]),
        mesh=mesh, in_specs=in_specs, out_specs=(tile, P(owner, None, None)), check_vma=False,
    )
```

```python
import functools

import jax
import jax.numpy as jnp
from jax import lax
from jax.experimental import pallas as pl
from jax.experimental.pallas import tpu as pltpu
from jax.sharding import PartitionSpec as P

MESH = pl.DeviceIdType.MESH
F32 = jnp.float32
BF16 = jnp.bfloat16
CP = 80
LANES = 128
WIDE = 256
ROOT_HALF = 0.7071067811865476
NORM_DENSITY = 0.3989422804014327
UP, DOWN, LEFT, RIGHT, UL, UR, DL, DR = range(8)
GROUP = 32
LAG = 3
PIECES = 3
WORD = 65536
HALF_WORD = 32768
HALF_WORDS = 65535.0
TOP_PRECISION = 3.0
VALUE_STEPS = 2.0**28


def dot(a, b):
    return jnp.dot(a, b, preferred_element_type=F32)


def lane_iota(rows):
    return lax.broadcasted_iota(jnp.int32, (rows, LANES), 1)


def kernel(
    n_lat, n_lon, hid,
    x_hbm, xb_hbm, bp_ref, cw_ref, cb_ref, ow_ref, swath_ref, cell_hbm, w_hbm, val_hbm, prec_hbm,
    grad_ref, innov_ref,
    x_ref, xb_ref, cell_ref, w_ref, val_ref, prec_ref, wpad, wk, wt_ref, wo_ref, wot_ref, x32, given, packed, recv, opened, s1, s2, se, sobs, slope1, slope2, slope_edge, csend, hcol,
    bsc, qsc, inn, inn_recv, inn_mate, hist, ybuf, xbuf, ubuf, brow, bcol, rrow, rcol,
    fsend, frecv, bsend, brecv, psend, precv, isend, irecv, gsend, grecv, loaded,
):
    chan, height = x_ref.shape[0], x_ref.shape[1]
    owners = n_lat * n_lon
    chunks = height // 2
    lat = lax.axis_index("lat")
    lon = lax.axis_index("lon")
    has_up = lat > 0
    has_down = lat < n_lat - 1
    left = lax.rem(lon + n_lon - 1, n_lon)
    right = lax.rem(lon + 1, n_lon)
    ids = {
        UP: (lat - 1, lon), DOWN: (lat + 1, lon), LEFT: (lat, left), RIGHT: (lat, right),
        UL: (lat - 1, left), UR: (lat - 1, right), DL: (lat + 1, left), DR: (lat + 1, right),
    }
    opposite = {UP: DOWN, DOWN: UP, LEFT: RIGHT, RIGHT: LEFT, UL: DR, DR: UL, UR: DL, DL: UR}

    barrier = pltpu.get_barrier_semaphore()

    def wrapped(value, count):
        return value - jnp.where(value >= count, count, 0)

    side, half = lax.rem(lat, 2), lat // 2
    halves = n_lat // 2
    pairs = halves * n_lon
    mate = {"lat": lat + 1 - 2 * side}
    my_pair = half * n_lon + lon
    rounds = [(step, ahead) for step in range(halves) for ahead in range(n_lon) if step or ahead]

    def to_some(part, parts, act):
        for step, ahead in rounds[len(rounds) * part // parts : len(rounds) * (part + 1) // parts]:
            there, column = wrapped(half + step, halves), wrapped(lon + ahead, n_lon)
            act(there * n_lon + column, (2 * there + side, column))

    def rows_of(which, ref):
        return jnp.concatenate(
            [ref[pl.ds(pl.multiple_of((2 * h + which) * n_lon, n_lon), n_lon), :] for h in range(halves)], axis=0
        )

    def greet(_, where):
        pl.semaphore_signal(barrier, inc=1, device_id=where, device_id_type=MESH)

    across = {UP: has_up, UL: has_up, UR: has_up, DOWN: has_down, DL: has_down, DR: has_down}

    loads = [
        pltpu.make_async_copy(src, dst, loaded.at[k])
        for k, (src, dst) in enumerate(
            (
                (x_hbm, x_ref), (xb_hbm, xb_ref), (cell_hbm, cell_ref),
                (w_hbm, w_ref), (val_hbm, val_ref), (prec_hbm, prec_ref),
            )
        )
    ]
    for load in loads:
        load.start()
    to_some(0, 1, greet)
    for d, there in across.items():
        pl.when(there)(functools.partial(greet, None, ids[d]))

    x32[pl.ds(chan * height, (CP - chan) * height), :] = jnp.zeros(((CP - chan) * height, LANES), F32)
    loads[0].wait()
    x32[pl.ds(0, chan * height), :] = x_ref[...].astype(F32).reshape(chan * height, LANES)
    lane = lane_iota(CP)
    first_lane = lane == 0
    last_lane = lane == LANES - 1

    def block(rim, r, count=1):
        return pl.ds((r + rim) * LANES, count * LANES)

    def rolled(value, shift):
        return pltpu.roll(value, shift % LANES, 1) if shift % LANES else value

    def spot(r):
        return 2 * (r + 2)

    even = lax.rem(lane, 2) == 0
    edge = jnp.logical_or(first_lane, last_lane)
    slot_of = (lane + 1) // 2

    def joined(value):
        return jnp.where(even, value, rolled(value, -LANES // 2 - 1))

    def apart(value):
        return jnp.where(lane < LANES // 2, value, rolled(value, LANES // 2 + 1))

    def gathered(total, r, row):
        return jnp.where(slot_of == r + 2, rolled(row, spot(r)), total)

    pair_of = lane // 2
    to_left = jnp.zeros((CP, LANES), F32)
    to_right = jnp.zeros((CP, LANES), F32)
    for r in range(height):
        row = x32[pl.ds(r, CP, stride=height), :]
        s1[pl.ds(CP, CP), block(2, r)] = row.astype(BF16)
        s1[pl.ds(0, CP), block(2, r)] = rolled(row, 1).astype(BF16)
        s1[pl.ds(2 * CP, CP), block(2, r)] = rolled(row, -1).astype(BF16)
        to_left = jnp.where(pair_of == r + 2, rolled(row, spot(r)), to_left)
        to_right = jnp.where(pair_of == r + 2, rolled(row, spot(r) + 2), to_right)
    csend[0] = to_left.astype(BF16)
    csend[1] = to_right.astype(BF16)

    def guarded(d):
        if d in (UP, UL, UR):
            return pl.when(has_up)
        if d in (DOWN, DL, DR):
            return pl.when(has_down)
        return lambda f: f()

    def send(src, dst, t, d, sends, recvs):
        copy = pltpu.make_async_remote_copy(
            src_ref=src, dst_ref=dst, send_sem=sends.at[t, d], recv_sem=recvs.at[t, opposite[d]],
            device_id=ids[d], device_id_type=MESH,
        )
        guarded(d)(copy.start)

    def wait_recv(dst, t, d, sends, recvs):
        copy = pltpu.make_async_remote_copy(
            src_ref=dst, dst_ref=dst, send_sem=sends.at[t, d], recv_sem=recvs.at[t, d],
            device_id=ids[d], device_id_type=MESH,
        )
        guarded(d)(copy.wait_recv)

    def wait_send(src, t, d, sends, recvs):
        copy = pltpu.make_async_remote_copy(
            src_ref=src, dst_ref=src, send_sem=sends.at[t, d], recv_sem=recvs.at[t, d],
            device_id=ids[d], device_id_type=MESH,
        )
        guarded(d)(copy.wait_send)

    def pair(r):
        return s1.at[pl.ds(CP, CP), block(2, r, 2)]

    state_sources = {
        UP: pair(0), DOWN: pair(height - 2),
        LEFT: csend.at[0], UL: csend.at[0], DL: csend.at[0],
        RIGHT: csend.at[1], UR: csend.at[1], DR: csend.at[1],
    }
    state_targets = {UP: pair(-2), DOWN: pair(height)}
    for k, d in enumerate((LEFT, RIGHT, UL, UR, DL, DR)):
        state_targets[d] = hcol.at[k]

    def send_state():
        for d in (UP, DOWN, LEFT, RIGHT, UL, UR, DL, DR):
            send(state_sources[d], state_targets[opposite[d]], 0, d, fsend, frecv)

    def receive_state():
        for d in range(8):
            wait_recv(state_targets[d], 0, d, fsend, frecv)
        for there, r, slots in ((has_up, -2, (2, 3)), (has_down, height, (4, 5))):

            @pl.when(jnp.logical_not(there))
            def _():
                s1[pl.ds(CP, CP), block(2, r, 2)] = jnp.zeros((CP, WIDE), BF16)
                for slot in slots:
                    hcol[slot] = jnp.zeros((CP, LANES), BF16)

    def shift_far_rows():
        for r in (-2, -1, height, height + 1):
            row = s1[pl.ds(CP, CP), block(2, r)].astype(F32)
            s1[pl.ds(0, CP), block(2, r)] = rolled(row, 1).astype(BF16)
            s1[pl.ds(2 * CP, CP), block(2, r)] = rolled(row, -1).astype(BF16)

    def merge_columns(at_edge, beside):
        at_edge, beside = joined(at_edge), joined(beside)
        for r in range(-1, height + 1):
            row = jnp.where(edge, rolled(at_edge, -spot(r)), s2[pl.ds(CP, CP), block(1, r)].astype(F32))
            outer = rolled(beside, -spot(r))
            s2[pl.ds(0, CP), block(1, r)] = jnp.where(first_lane, outer, rolled(row, 1)).astype(BF16)
            s2[pl.ds(CP, CP), block(1, r)] = row.astype(BF16)
            s2[pl.ds(2 * CP, CP), block(1, r)] = jnp.where(last_lane, outer, rolled(row, -1)).astype(BF16)

    def with_corners(side, above, below):
        middle = jnp.logical_and(pair_of >= 2, pair_of < height + 2)
        outer = jnp.where(pair_of < 2, rolled(above, -2 * height), rolled(below, 2 * height))
        return jnp.where(middle, side, outer)

    def spread_columns():
        from_left, from_right, ul, ur, dl, dr = (hcol[k].astype(F32) for k in range(6))
        low = with_corners(from_left, ul, dl)
        high = with_corners(from_right, ur, dr)
        first = csend[0].astype(F32)
        last = csend[1].astype(F32)
        for r in (-2, -1, height, height + 1):
            row = s1[pl.ds(CP, CP), block(2, r)].astype(F32)
            first = jnp.where(pair_of == r + 2, rolled(row, spot(r)), first)
            last = jnp.where(pair_of == r + 2, rolled(row, spot(r) + 2), last)
        on_left = lane < LANES // 2
        lefts = (low, rolled(low, -1), first, rolled(first, -1))
        rights = tuple(rolled(v, LANES // 2 - k) for v in (last, high) for k in (0, 1))
        beside = tuple(jnp.where(on_left, lefts[j], rights[j + 1]) for j in range(3))
        at_edge = tuple(jnp.where(on_left, lefts[j + 1], rights[j]) for j in range(3))
        for i in range(3):
            for j in range(3):
                part = pl.ds(j * CP, CP)
                se[i, part, pl.ds(0, LANES)] = rolled(beside[j], 2 * (1 - i)).astype(BF16)
                se[i, part, pl.ds(LANES, LANES)] = rolled(at_edge[j], 2 * (1 - i)).astype(BF16)
        return jnp.concatenate([beside[1], at_edge[1]], axis=1)

    def conv(window):
        return sum(dot(wt_ref[i], window(i)) for i in range(3))

    def network(pre, centre):
        cdf = 0.5 * (1.0 + lax.erf(pre * ROOT_HALF))
        update = dot(wo_ref[...], (pre * cdf).astype(BF16))
        return centre.astype(F32) + update, lambda: cdf + pre * jnp.exp(-0.5 * pre * pre) * NORM_DENSITY

    def conv_chunk(s, rim, n):
        return conv(lambda i: s[:, block(rim, 2 * n + i - 1, 2)])

    def forward_chunk(pre, s, rim, n, slope, inner_only):
        state, tangent = network(pre, s[pl.ds(CP, CP), block(rim, 2 * n, 2)])
        slope[:, pl.ds(n * WIDE, WIDE)] = jnp.where(edge_wide, 0.0, tangent()) if inner_only else tangent()
        return state.astype(BF16)

    def pipelined(order, start, finish, lag=1):
        order = list(order)
        held = [start(n) for n in order[:lag]]
        for k, n in enumerate(order):
            if k + lag < len(order):
                held.append(start(order[k + lag]))
            finish(n, held.pop(0))

    def first_rim(centre):
        up, down = has_up.astype(F32), has_down.astype(F32)
        rows = (-1, height)
        state, _ = network(
            conv(lambda i: jnp.concatenate([s1[:, block(2, r + i - 1)] for r in rows], axis=1)),
            jnp.concatenate([s1[pl.ds(CP, CP), block(2, r)] for r in rows], axis=1),
        )
        s2[pl.ds(CP, CP), block(1, -1)] = (state[:, :LANES] * up).astype(BF16)
        s2[pl.ds(CP, CP), block(1, height)] = (state[:, LANES:] * down).astype(BF16)
        sides, tangent = network(conv(lambda i: se[i]), centre)
        place = lax.rem(lane, LANES // 2)
        inside = jnp.where(place == spot(-1), up, jnp.where(place == spot(height), down, 1.0))
        here = lax.rem(lane_iota(hid), LANES // 2)
        kept = jnp.logical_and(lax.rem(here, 2) == 0, jnp.logical_and(here >= spot(0), here <= spot(height - 1)))
        slope_edge[...] = jnp.where(kept, tangent()[:, LANES:], 0.0)
        return tuple((sides[:, k * LANES : (k + 1) * LANES] * inside).astype(BF16).astype(F32) for k in (0, 1))

    pl.semaphore_wait(barrier, pairs - 1 + 3 * (has_up.astype(jnp.int32) + has_down.astype(jnp.int32)))
    send_state()

    for load in loads[1:]:
        load.wait()
    def fixed(value, top):
        return jnp.round(value * (HALF_WORDS / top)).astype(jnp.int32)

    def packet_words(which):
        first, second, third, fourth = (fixed(rows_of(which, w_ref.at[k]), 1.0) for k in range(4))
        return (
            (first - HALF_WORD) * WORD + second,
            (third - HALF_WORD) * WORD + fourth,
            rows_of(which, cell_ref) * WORD + fixed(rows_of(which, prec_ref), TOP_PRECISION),
            jnp.round(rows_of(which, val_ref) * VALUE_STEPS).astype(jnp.int32),
        )

    for k, word in enumerate(packet_words(1 - side)):
        given[:, k, :] = word
    to_mate = pltpu.make_async_remote_copy(
        src_ref=given, dst_ref=packed.at[1], send_sem=gsend.at[0], recv_sem=grecv.at[0],
        device_id=mate, device_id_type=MESH,
    )
    to_mate.start()
    for k, word in enumerate(packet_words(side)):
        packed[0, :, k, :] = word

    def post(other, where):
        pltpu.make_async_remote_copy(
            src_ref=packed.at[:, other], dst_ref=recv.at[:, my_pair],
            send_sem=psend, recv_sem=precv, device_id=where, device_id_type=MESH,
        ).start()

    wpad[...] = jnp.zeros((LANES, hid), F32)
    bias = cb_ref[...]
    bias_parts = []
    for _ in range(3):
        part = bias.astype(BF16).astype(F32)
        bias_parts.append(part)
        bias = bias - part
    spare = lax.broadcasted_iota(jnp.int32, (hid - 3 * CP, hid), 0)
    bias_rows = jnp.zeros((hid - 3 * CP, hid), F32)
    for k, part in enumerate(bias_parts):
        bias_rows = jnp.where(spare == k, part, bias_rows)
    for i in range(3):
        for j in range(3):
            wpad[pl.ds(0, chan), :] = cw_ref[3 * i + j].astype(F32)
            wk[i, pl.ds(j * CP, CP), :] = wpad[pl.ds(0, CP), :].astype(BF16)
        wk[i, pl.ds(3 * CP, hid - 3 * CP), :] = (bias_rows if i == 1 else jnp.zeros_like(bias_rows)).astype(BF16)
        wt_ref[i] = jnp.transpose(wk[i].astype(F32)).astype(BF16)
    wpad[pl.ds(0, chan), :] = ow_ref[...].astype(F32)
    wo_ref[...] = wpad[pl.ds(0, CP), :].astype(BF16)
    wot_ref[...] = jnp.transpose(wpad[...]).astype(BF16)
    for c in range(chan):
        grad_ref[pl.ds(c * height, height), :] = bp_ref[0, c] * (x_ref[c].astype(F32) - xb_ref[c].astype(F32))

    def ones(breadth):
        return jnp.ones((hid - 3 * CP, breadth), BF16)

    s1[pl.ds(3 * CP, hid - 3 * CP), :] = ones((height + 4) * LANES)
    s2[pl.ds(3 * CP, hid - 3 * CP), :] = ones((height + 2) * LANES)
    for i in range(3):
        se[i, pl.ds(3 * CP, hid - 3 * CP), :] = ones(WIDE)

    column_wide = lax.broadcasted_iota(jnp.int32, (hid, WIDE), 1)
    column_wide = lax.rem(column_wide, LANES)
    edge_wide = jnp.logical_or(column_wide == 0, column_wide == LANES - 1)
    early = range(1, chunks - 1)

    def first_conv(n):
        return conv_chunk(s1, 2, n)

    def first_step(n, pre):
        s2[pl.ds(CP, CP), block(1, 2 * n, 2)] = forward_chunk(pre, s1, 2, n, slope1, True)

    def early_step(n, pre):
        to_some(n - 1, len(early), post)
        first_step(n, pre)

    to_mate.wait_recv()
    recv[:, my_pair] = packed[:, my_pair]
    pipelined(early, first_conv, early_step)
    receive_state()
    shift_far_rows()
    pipelined((0, chunks - 1), first_conv, first_step)
    beside, at_edge = first_rim(spread_columns())
    merge_columns(at_edge, beside)

    def second_step(n, pre):
        sobs[n] = forward_chunk(pre, s2, 1, n, slope2, False)

    pipelined(range(chunks), lambda n: conv_chunk(s2, 1, n), second_step)

    others = pl.ds(0, pairs - 1)
    pltpu.make_async_remote_copy(
        src_ref=packed.at[:, others], dst_ref=recv.at[:, others], send_sem=psend, recv_sem=precv,
        device_id=ids[RIGHT], device_id_type=MESH,
    ).wait()

    def unfixed(value, top):
        return value.astype(F32) * (top / HALF_WORDS)

    for which in range(2):

        def field(k, value, which=which):
            opened[pl.ds(which * pairs * 8 + k, pairs, stride=8), :] = value

        words = recv[which, :, 2, :]
        field(0, (words >> 24).astype(F32))
        field(1, ((words >> 16) & (LANES - 1)).astype(F32))
        field(7, unfixed(words & (WORD - 1), TOP_PRECISION))
        for k in range(2):
            words = recv[which, :, k, :]
            field(2 + 2 * k, unfixed((words >> 16) + HALF_WORD, 1.0))
            field(3 + 2 * k, unfixed(words & (WORD - 1), 1.0))
        field(6, recv[which, :, 3, :].astype(F32) * (1.0 / VALUE_STEPS))

    def patch_of(group, u):
        k = group * GROUP + u
        which, pair_id = k // pairs, lax.rem(k, pairs)
        at_side = jnp.where(which == 0, side, 1 - side)
        owner = (2 * (pair_id // n_lon) + at_side) * n_lon + lax.rem(pair_id, n_lon)
        return swath_ref[0, owner]

    column = lax.broadcasted_iota(jnp.int32, (LANES, LANES), 0).astype(F32).astype(BF16)
    channel = lax.broadcasted_iota(jnp.int32, (CP, LANES), 0).astype(F32)
    zero = jnp.zeros((LANES, LANES), BF16)

    def estimate(group, carry):
        def start(u):
            k = group * GROUP + u
            packet = opened[pl.ds(pl.multiple_of(k * 8, 8), 8), :]

            def row(which):
                return jnp.broadcast_to(packet[which : which + 1].astype(BF16), (LANES, LANES))

            at = row(1)
            here, after = column == at, column == at + 1
            table = jnp.concatenate(
                [
                    jnp.where(here, row(2), jnp.where(after, row(3), zero)),
                    jnp.where(here, row(4), jnp.where(after, row(5), zero)),
                ],
                axis=0,
            )
            bsc[k] = table
            return packet, dot(sobs[patch_of(group, u)], table)

        def finish(u, given):
            k = group * GROUP + u
            packet, found = given
            picked = channel == packet[0:1]
            gap = jnp.sum(jnp.where(picked, found, 0.0), axis=0, keepdims=True) - packet[6:7]
            inn[k // pairs, lax.rem(k, pairs)] = gap
            qsc[k] = jnp.where(picked, packet[7:8] * gap, 0.0).astype(BF16)

        pipelined(range(GROUP), start, finish, LAG)
        return carry

    lax.fori_loop(0, owners // GROUP, estimate, 0)
    hist[0] = jnp.zeros((CP, WIDE), F32)

    def pull(group, last):
        slots = [last]

        def start(u):
            k = group * GROUP + u
            return lax.dot_general(qsc[k], bsc[k], (((1,), (1,)), ((), ())), preferred_element_type=F32)

        def finish(u, share):
            k = group * GROUP + u
            patch = patch_of(group, u)
            before = sum(jnp.where(patch == m, slots[-1][m], 0) for m in range(chunks))
            hist[k + 1] = hist[before] + share
            slots.append(tuple(jnp.where(patch == m, k + 1, slots[-1][m]) for m in range(chunks)))

        pipelined(range(GROUP), start, finish, LAG)
        return slots[-1]

    last = lax.fori_loop(0, owners // GROUP, pull, (jnp.int32(0),) * chunks)
    inn_recv[:, my_pair] = inn[:, my_pair]

    def give_back(other, where):
        pltpu.make_async_remote_copy(
            src_ref=inn.at[:, other], dst_ref=inn_recv.at[:, my_pair],
            send_sem=isend, recv_sem=irecv, device_id=where, device_id_type=MESH,
        ).start()

    def tap(i, j, r):
        return ybuf[pl.ds((3 * (i + 1) + j + 1) * CP, CP), pl.ds(r * LANES, LANES)]

    def summed(j, r):
        total = None
        for i in (-1, 0, 1):
            if 0 <= r - i < height:
                part = tap(i, j, r - i)
                total = part if total is None else total + part
        return total

    def rim_sources(t):
        table = dict.fromkeys((LEFT, RIGHT, UL, UR, DL, DR), bcol.at[t])
        return table | {UP: brow.at[t, 0], DOWN: brow.at[t, 1]}

    def rim_targets(t):
        table = {d: rcol.at[t, k] for k, d in enumerate((LEFT, RIGHT, UL, UR, DL, DR))}
        return table | {UP: rrow.at[t, 0], DOWN: rrow.at[t, 1]}

    def spread_of(cotangent, slope):
        breadth = cotangent.shape[1]
        rounded = jnp.concatenate([cotangent.astype(BF16), jnp.zeros((LANES - CP, breadth), BF16)], axis=0)
        return (dot(wot_ref[...], rounded) * slope).astype(BF16)

    def products(cotangent, slope):
        def start(n):
            return spread_of(cotangent(n), slope[:, pl.ds(n * WIDE, WIDE)])

        def finish(n, spread):
            for i in range(3):
                ybuf[pl.ds(3 * i * CP, 3 * CP), pl.ds(n * WIDE, WIDE)] = dot(wk[i, pl.ds(0, 3 * CP), :], spread)

        pipelined(range(chunks), start, finish)

    def inner(t_low, t_mid, t_high):
        return (
            t_mid
            + jnp.where(first_lane, 0.0, rolled(t_high, 1))
            + jnp.where(last_lane, 0.0, rolled(t_low, -1))
        )

    def local_sums(t, own):
        columns = jnp.zeros((CP, LANES), F32)
        for r in range(-1, height + 1):
            t_low, t_mid, t_high = (summed(j, r) for j in (-1, 0, 1))
            total = inner(t_low, t_mid, t_high)
            ubuf[t, :, block(1, r)] = total + own(r) if 0 <= r < height and own else total
            columns = gathered(columns, r, jnp.where(first_lane, t_low, t_high))
        return columns

    def send_rim(t, above, below, columns):
        brow[t, 0] = above.astype(BF16)
        brow[t, 1] = below.astype(BF16)
        bcol[t] = columns.astype(BF16)
        src, dst = rim_sources(t), rim_targets(t)
        for d in (UP, DOWN, LEFT, RIGHT, UL, UR, DL, DR):
            send(src[d], dst[opposite[d]], t, d, bsend, brecv)

    def receive_rim(t):
        dst = rim_targets(t)
        for d in range(8):
            wait_recv(dst[d], t, d, bsend, brecv)
        for there, row, slots in ((has_up, 0, (2, 3)), (has_down, 1, (4, 5))):

            @pl.when(jnp.logical_not(there))
            def _():
                rrow[t, row] = jnp.zeros((CP, LANES), BF16)
                for slot in slots:
                    rcol[t, slot] = jnp.zeros((CP, LANES), BF16)

        from_left, from_right, ul, ur, dl, dr = (rcol[t, k].astype(F32) for k in range(6))
        inside = jnp.logical_and(slot_of >= 2, slot_of < height + 2)
        inflow = jnp.where(inside, jnp.where(even, rolled(from_left, 1), rolled(from_right, -1)), 0.0)
        top, bottom, past, before = spot(0), spot(height - 1), spot(height), spot(-1)
        for value, came, goes in (
            (ul, past - 1, top), (ur, past, top - 1), (dl, before - 1, bottom), (dr, before, bottom - 1),
        ):
            inflow = inflow + jnp.where(lane == goes, rolled(value, goes - came), 0.0)
        return rrow[t, 0].astype(F32), rrow[t, 1].astype(F32), inflow

    products(lambda n: hist[last[n]], slope2)
    columns = local_sums(0, lambda r: hist[last[r // 2]][:, (r % 2) * LANES : (r % 2 + 1) * LANES])
    send_rim(0, ubuf[0, :, block(1, -1)], ubuf[0, :, block(1, height)], columns)

    to_some(0, 1, give_back)
    products(lambda n: ubuf[0, :, block(1, 2 * n, 2)], slope1)
    columns = local_sums(1, None)
    at_edge = jnp.zeros((CP, LANES), F32)
    for r in range(height):
        at_edge = gathered(at_edge, r, ubuf[0, :, block(1, r)])
    above, below, inflow = receive_rim(0)
    far = height - 1
    at_edge = at_edge + inflow
    at_edge = at_edge + gathered(gathered(jnp.zeros((CP, LANES), F32), 0, above), far, below)
    late = spread_of(
        jnp.concatenate([above, below, apart(at_edge)], axis=1),
        jnp.concatenate(
            [slope1[:, pl.ds(0, LANES)], slope1[:, pl.ds(far * LANES, LANES)], slope_edge[...]], axis=1
        ),
    )
    for i in range(3):
        xbuf[pl.ds(3 * i * CP, 3 * CP), :] = dot(wk[i, pl.ds(0, 3 * CP), :], late)

    def late_tap(i, j, part):
        return xbuf[pl.ds((3 * (i + 1) + j + 1) * CP, CP), pl.ds(part * LANES, LANES)]

    def late_row(part, i):
        return tuple(late_tap(i, j, part) for j in (-1, 0, 1))

    to_low, to_same, to_high = (
        sum(rolled(late_tap(i, j, 2), 2 * i) for i in (-1, 0, 1)) for j in (-1, 0, 1)
    )
    outside = slot_of <= height + 2
    columns = columns + jnp.where(outside, jnp.where(even, to_low, rolled(to_high, -LANES // 2 - 1)), 0.0)
    for part, base in ((0, 0), (1, far)):
        for i in (-1, 0, 1):
            t_low, _, t_high = late_row(part, i)
            columns = columns + gathered(
                jnp.zeros((CP, LANES), F32), base + i, jnp.where(first_lane, t_low, t_high)
            )
    same = joined(to_same)
    next_in = jnp.where(even, rolled(to_low, -LANES // 2 - 2), rolled(to_high, 1))
    second = jnp.logical_or(lane == 1, lane == LANES - 2)

    def from_columns(r, outermost):
        return jnp.where(edge, rolled(outermost, -spot(r)), 0.0) + jnp.where(second, rolled(next_in, -spot(r)), 0.0)

    send_rim(
        1,
        ubuf[1, :, block(1, -1)] + inner(*late_row(0, -1)) + from_columns(-1, same),
        ubuf[1, :, block(1, height)] + inner(*late_row(1, 1)) + from_columns(height, same),
        columns,
    )
    pltpu.make_async_remote_copy(
        src_ref=inn.at[:, others], dst_ref=inn_recv.at[:, others], send_sem=isend, recv_sem=irecv,
        device_id=ids[RIGHT], device_id_type=MESH,
    ).wait()
    innov_to_mate = pltpu.make_async_remote_copy(
        src_ref=inn_recv.at[1], dst_ref=inn_mate, send_sem=gsend.at[1], recv_sem=grecv.at[1],
        device_id=mate, device_id_type=MESH,
    )
    innov_to_mate.start()
    outermost = same + inflow
    for r in range(height):
        value = ubuf[0, :, block(1, r)] + ubuf[1, :, block(1, r)] + from_columns(r, outermost)
        if r < 2:
            value = value + inner(*late_row(0, r))
        if r >= far - 1:
            value = value + inner(*late_row(1, r - far))
        if r == 0:
            value = value + above
        if r == far:
            value = value + below
        ubuf[0, :, block(1, r)] = value
    above, below, inflow = receive_rim(1)
    for r in range(height):
        value = ubuf[0, :, block(1, r)] + jnp.where(edge, rolled(inflow, -spot(r)), 0.0)
        if r == 0:
            value = value + above
        if r == far:
            value = value + below
        here = pl.ds(r, chan, stride=height)
        grad_ref[here, :] = grad_ref[here, :] + value[:chan]

    innov_to_mate.wait()
    to_mate.wait_send()
    for h in range(halves):
        part = pl.ds(h * n_lon, n_lon)
        for which, ref in ((side, inn_recv.at[0]), (1 - side, inn_mate)):
            rows = pl.ds(pl.multiple_of((2 * h + which) * n_lon, n_lon), n_lon)
            innov_ref[rows, :] = ref[part].reshape(n_lon, LANES)
    for d in range(8):
        wait_send(state_sources[d], 0, d, fsend, frecv)
    for t in range(2):
        src = rim_sources(t)
        for d in range(8):
            wait_send(src[d], t, d, bsend, brecv)


def hand_over(gradient_in, innov_in, gradient_out, innov_out, gradient_held, innov_held, sems):
    chan = gradient_in.shape[0]
    cuts = [chan * k // PIECES for k in range(PIECES + 1)]
    parts = [pl.ds(a, b - a) for a, b in zip(cuts, cuts[1:])]
    routes = [(gradient_in.at[p], gradient_held.at[p], gradient_out.at[p]) for p in parts]
    routes.append((innov_in, innov_held, innov_out))
    reads = [pltpu.make_async_copy(src, held, sems.at[0, k]) for k, (src, held, _) in enumerate(routes)]
    writes = [pltpu.make_async_copy(held, dst, sems.at[1, k]) for k, (_, held, dst) in enumerate(routes)]
    for read in reads:
        read.start()
    for read, write in zip(reads, writes):
        read.wait()
        write.start()
    for write in writes:
        write.wait()


def local(
    n_lat, n_lon,
    initial_state, background_state, background_precision, conv_weight, conv_bias, out_weight,
    swath_patch, obs_cell, obs_weights, obs_value, obs_precision,
):
    chan, height, breadth = initial_state.shape
    hid = conv_weight.shape[2]
    owners = n_lat * n_lon
    chunks = height // 2
    cells = height * breadth
    vmem = pl.BlockSpec(memory_space=pltpu.VMEM)
    hbm = pl.BlockSpec(memory_space=pltpu.HBM)
    smem = pl.BlockSpec(memory_space=pltpu.SMEM)
    dma = pltpu.SemaphoreType.DMA
    gradient, innov = pl.pallas_call(
        functools.partial(kernel, n_lat, n_lon, hid),
        out_shape=(
            jax.ShapeDtypeStruct((chan * height, LANES), F32),
            jax.ShapeDtypeStruct((owners, LANES), F32),
        ),
        in_specs=[hbm, hbm, smem, vmem, vmem, vmem, smem] + [hbm] * 4,
        out_specs=(vmem, vmem),
        scratch_shapes=[
            pltpu.VMEM((chan, height, breadth), BF16),
            pltpu.VMEM((chan, height, breadth), BF16),
            pltpu.VMEM((owners, LANES), jnp.int32),
            pltpu.VMEM((4, owners, LANES), F32),
            pltpu.VMEM((owners, LANES), F32),
            pltpu.VMEM((owners, LANES), F32),
            pltpu.VMEM((LANES, hid), F32),
            pltpu.VMEM((3, hid, hid), BF16),
            pltpu.VMEM((3, hid, hid), BF16),
            pltpu.VMEM((CP, hid), BF16),
            pltpu.VMEM((hid, LANES), BF16),
            pltpu.VMEM((CP * height, LANES), F32),
            pltpu.VMEM((owners // 2, 4, LANES), jnp.int32),
            pltpu.VMEM((2, owners // 2, 4, LANES), jnp.int32),
            pltpu.VMEM((2, owners // 2, 4, LANES), jnp.int32),
            pltpu.VMEM((owners * 8, LANES), F32),
            pltpu.VMEM((hid, (height + 4) * LANES), BF16),
            pltpu.VMEM((hid, (height + 2) * LANES), BF16),
            pltpu.VMEM((3, hid, WIDE), BF16),
            pltpu.VMEM((chunks, CP, WIDE), BF16),
            pltpu.VMEM((hid, cells), F32),
            pltpu.VMEM((hid, cells), F32),
            pltpu.VMEM((hid, LANES), F32),
            pltpu.VMEM((2, CP, LANES), BF16),
            pltpu.VMEM((6, CP, LANES), BF16),
            pltpu.VMEM((owners, WIDE, LANES), BF16),
            pltpu.VMEM((owners, CP, LANES), BF16),
            pltpu.VMEM((2, owners // 2, 1, LANES), F32),
            pltpu.VMEM((2, owners // 2, 1, LANES), F32),
            pltpu.VMEM((owners // 2, 1, LANES), F32),
            pltpu.VMEM((owners + 1, CP, WIDE), F32),
            pltpu.VMEM((9 * CP, cells), F32),
            pltpu.VMEM((9 * CP, 3 * LANES), F32),
            pltpu.VMEM((2, CP, (height + 2) * LANES), F32),
            pltpu.VMEM((2, 2, CP, LANES), BF16),
            pltpu.VMEM((2, CP, LANES), BF16),
            pltpu.VMEM((2, 2, CP, LANES), BF16),
            pltpu.VMEM((2, 6, CP, LANES), BF16),
            dma((1, 8)), dma((1, 8)), dma((2, 8)), dma((2, 8)),
            dma, dma, dma, dma, dma((2,)), dma((2,)), dma((6,)),
        ],
        compiler_params=pltpu.CompilerParams(
            collective_id=0, has_side_effects=True, vmem_limit_bytes=56 * 1024 * 1024
        ),
    )(
        initial_state, background_state, background_precision[None], conv_weight, conv_bias[None], out_weight, swath_patch,
        obs_cell[0], obs_weights[:, 0], obs_value[0], obs_precision[0],
    )
    return pl.pallas_call(
        hand_over,
        out_shape=(
            jax.ShapeDtypeStruct((chan, height, breadth), F32),
            jax.ShapeDtypeStruct((1, owners, LANES), F32),
        ),
        in_specs=[hbm, hbm],
        out_specs=(hbm, hbm),
        scratch_shapes=[
            pltpu.VMEM((chan, height, breadth), F32),
            pltpu.VMEM((1, owners, LANES), F32),
            dma((2, PIECES + 1)),
        ],
        compiler_params=pltpu.CompilerParams(vmem_limit_bytes=56 * 1024 * 1024),
    )(gradient.reshape(chan, height, breadth), innov[None])


def solution(mesh):
    tile = P(None, "lat", "lon")
    owner = ("lat", "lon")
    in_specs = (
        tile, tile, P(), P(), P(), P(),
        P(owner, None), P(owner, None, None), P(None, owner, None, None), P(owner, None, None), P(owner, None, None),
    )
    return jax.shard_map(
        functools.partial(local, mesh.shape["lat"], mesh.shape["lon"]),
        mesh=mesh, in_specs=in_specs, out_specs=(tile, P(owner, None, None)), check_vma=False,
    )
```

```python
import functools

import jax
import jax.numpy as jnp
from jax import lax
from jax.experimental import pallas as pl
from jax.experimental.pallas import tpu as pltpu
from jax.sharding import PartitionSpec as P

MESH = pl.DeviceIdType.MESH
F32 = jnp.float32
BF16 = jnp.bfloat16
CP = 80
LANES = 128
WIDE = 256
ROOT_HALF = 0.7071067811865476
NORM_DENSITY = 0.3989422804014327
UP, DOWN, LEFT, RIGHT, UL, UR, DL, DR = range(8)
GROUP = 32
LAG = 3
PIECES = 3
WORD = 65536
HALF_WORD = 32768
HALF_WORDS = 65535.0
TOP_PRECISION = 3.0
VALUE_STEPS = 2.0**28


def dot(a, b):
    return jnp.dot(a, b, preferred_element_type=F32)


def lane_iota(rows):
    return lax.broadcasted_iota(jnp.int32, (rows, LANES), 1)


def kernel(
    n_lat, n_lon, hid,
    x_hbm, xb_hbm, bp_ref, cw_ref, cb_ref, ow_ref, swath_ref, cell_hbm, w_hbm, val_hbm, prec_hbm,
    grad_ref, innov_ref,
    x_ref, xb_ref, cell_ref, w_ref, val_ref, prec_ref, wpad, wk, wt_ref, wo_ref, wot_ref, x32, given, packed, recv, opened, s1, s2, se, sobs, slope1, slope2, slope_edge, slope_edge2, csend, hcol,
    bsc, qsc, inn, inn_recv, inn_mate, hist, ybuf, xbuf, ubuf, brow, bcol, rrow, rcol,
    fsend, frecv, bsend, brecv, psend, precv, isend, irecv, gsend, grecv, loaded,
):
    chan, height = x_ref.shape[0], x_ref.shape[1]
    owners = n_lat * n_lon
    chunks = height // 2
    lat = lax.axis_index("lat")
    lon = lax.axis_index("lon")
    has_up = lat > 0
    has_down = lat < n_lat - 1
    left = lax.rem(lon + n_lon - 1, n_lon)
    right = lax.rem(lon + 1, n_lon)
    ids = {
        UP: (lat - 1, lon), DOWN: (lat + 1, lon), LEFT: (lat, left), RIGHT: (lat, right),
        UL: (lat - 1, left), UR: (lat - 1, right), DL: (lat + 1, left), DR: (lat + 1, right),
    }
    opposite = {UP: DOWN, DOWN: UP, LEFT: RIGHT, RIGHT: LEFT, UL: DR, DR: UL, UR: DL, DL: UR}

    barrier = pltpu.get_barrier_semaphore()

    def wrapped(value, count):
        return value - jnp.where(value >= count, count, 0)

    side, half = lax.rem(lat, 2), lat // 2
    halves = n_lat // 2
    pairs = halves * n_lon
    mate = {"lat": lat + 1 - 2 * side}
    my_pair = half * n_lon + lon
    rounds = [(step, ahead) for step in range(halves) for ahead in range(n_lon) if step or ahead]

    def to_some(part, parts, act):
        for step, ahead in rounds[len(rounds) * part // parts : len(rounds) * (part + 1) // parts]:
            there, column = wrapped(half + step, halves), wrapped(lon + ahead, n_lon)
            act(there * n_lon + column, (2 * there + side, column))

    def rows_of(which, ref):
        return jnp.concatenate(
            [ref[pl.ds(pl.multiple_of((2 * h + which) * n_lon, n_lon), n_lon), :] for h in range(halves)], axis=0
        )

    def greet(_, where):
        pl.semaphore_signal(barrier, inc=1, device_id=where, device_id_type=MESH)

    across = {UP: has_up, UL: has_up, UR: has_up, DOWN: has_down, DL: has_down, DR: has_down}

    loads = [
        pltpu.make_async_copy(src, dst, loaded.at[k])
        for k, (src, dst) in enumerate(
            (
                (x_hbm, x_ref), (xb_hbm, xb_ref), (cell_hbm, cell_ref),
                (w_hbm, w_ref), (val_hbm, val_ref), (prec_hbm, prec_ref),
            )
        )
    ]
    for load in loads:
        load.start()
    to_some(0, 1, greet)
    for d, there in across.items():
        pl.when(there)(functools.partial(greet, None, ids[d]))

    x32[pl.ds(chan * height, (CP - chan) * height), :] = jnp.zeros(((CP - chan) * height, LANES), F32)
    loads[0].wait()
    x32[pl.ds(0, chan * height), :] = x_ref[...].astype(F32).reshape(chan * height, LANES)
    lane = lane_iota(CP)
    first_lane = lane == 0
    last_lane = lane == LANES - 1

    def block(rim, r, count=1):
        return pl.ds((r + rim) * LANES, count * LANES)

    def rolled(value, shift):
        return pltpu.roll(value, shift % LANES, 1) if shift % LANES else value

    def spot(r):
        return 2 * (r + 2)

    even = lax.rem(lane, 2) == 0
    edge = jnp.logical_or(first_lane, last_lane)
    slot_of = (lane + 1) // 2

    def joined(value):
        return jnp.where(even, value, rolled(value, -LANES // 2 - 1))

    def apart(value):
        return jnp.where(lane < LANES // 2, value, rolled(value, LANES // 2 + 1))

    def gathered(total, r, row):
        return jnp.where(slot_of == r + 2, rolled(row, spot(r)), total)

    pair_of = lane // 2
    to_left = jnp.zeros((CP, LANES), F32)
    to_right = jnp.zeros((CP, LANES), F32)
    for r in range(height):
        row = x32[pl.ds(r, CP, stride=height), :]
        s1[pl.ds(CP, CP), block(2, r)] = row.astype(BF16)
        s1[pl.ds(0, CP), block(2, r)] = rolled(row, 1).astype(BF16)
        s1[pl.ds(2 * CP, CP), block(2, r)] = rolled(row, -1).astype(BF16)
        to_left = jnp.where(pair_of == r + 2, rolled(row, spot(r)), to_left)
        to_right = jnp.where(pair_of == r + 2, rolled(row, spot(r) + 2), to_right)
    csend[0] = to_left.astype(BF16)
    csend[1] = to_right.astype(BF16)

    def guarded(d):
        if d in (UP, UL, UR):
            return pl.when(has_up)
        if d in (DOWN, DL, DR):
            return pl.when(has_down)
        return lambda f: f()

    def send(src, dst, t, d, sends, recvs):
        copy = pltpu.make_async_remote_copy(
            src_ref=src, dst_ref=dst, send_sem=sends.at[t, d], recv_sem=recvs.at[t, opposite[d]],
            device_id=ids[d], device_id_type=MESH,
        )
        guarded(d)(copy.start)

    def wait_recv(dst, t, d, sends, recvs):
        copy = pltpu.make_async_remote_copy(
            src_ref=dst, dst_ref=dst, send_sem=sends.at[t, d], recv_sem=recvs.at[t, d],
            device_id=ids[d], device_id_type=MESH,
        )
        guarded(d)(copy.wait_recv)

    def wait_send(src, t, d, sends, recvs):
        copy = pltpu.make_async_remote_copy(
            src_ref=src, dst_ref=src, send_sem=sends.at[t, d], recv_sem=recvs.at[t, d],
            device_id=ids[d], device_id_type=MESH,
        )
        guarded(d)(copy.wait_send)

    def pair(r):
        return s1.at[pl.ds(CP, CP), block(2, r, 2)]

    state_sources = {
        UP: pair(0), DOWN: pair(height - 2),
        LEFT: csend.at[0], UL: csend.at[0], DL: csend.at[0],
        RIGHT: csend.at[1], UR: csend.at[1], DR: csend.at[1],
    }
    state_targets = {UP: pair(-2), DOWN: pair(height)}
    for k, d in enumerate((LEFT, RIGHT, UL, UR, DL, DR)):
        state_targets[d] = hcol.at[k]

    def send_state():
        for d in (UP, DOWN, LEFT, RIGHT, UL, UR, DL, DR):
            send(state_sources[d], state_targets[opposite[d]], 0, d, fsend, frecv)

    def receive_state():
        for d in range(8):
            wait_recv(state_targets[d], 0, d, fsend, frecv)
        for there, r, slots in ((has_up, -2, (2, 3)), (has_down, height, (4, 5))):

            @pl.when(jnp.logical_not(there))
            def _():
                s1[pl.ds(CP, CP), block(2, r, 2)] = jnp.zeros((CP, WIDE), BF16)
                for slot in slots:
                    hcol[slot] = jnp.zeros((CP, LANES), BF16)

    def shift_far_rows():
        for r in (-2, -1, height, height + 1):
            row = s1[pl.ds(CP, CP), block(2, r)].astype(F32)
            s1[pl.ds(0, CP), block(2, r)] = rolled(row, 1).astype(BF16)
            s1[pl.ds(2 * CP, CP), block(2, r)] = rolled(row, -1).astype(BF16)

    def merge_columns(at_edge, beside):
        at_edge, beside = joined(at_edge), joined(beside)
        for r in range(-1, height + 1):
            row = jnp.where(edge, rolled(at_edge, -spot(r)), s2[pl.ds(CP, CP), block(1, r)].astype(F32))
            outer = rolled(beside, -spot(r))
            s2[pl.ds(0, CP), block(1, r)] = jnp.where(first_lane, outer, rolled(row, 1)).astype(BF16)
            s2[pl.ds(CP, CP), block(1, r)] = row.astype(BF16)
            s2[pl.ds(2 * CP, CP), block(1, r)] = jnp.where(last_lane, outer, rolled(row, -1)).astype(BF16)

    def with_corners(side, above, below):
        middle = jnp.logical_and(pair_of >= 2, pair_of < height + 2)
        outer = jnp.where(pair_of < 2, rolled(above, -2 * height), rolled(below, 2 * height))
        return jnp.where(middle, side, outer)

    def spread_columns():
        from_left, from_right, ul, ur, dl, dr = (hcol[k].astype(F32) for k in range(6))
        low = with_corners(from_left, ul, dl)
        high = with_corners(from_right, ur, dr)
        first = csend[0].astype(F32)
        last = csend[1].astype(F32)
        for r in (-2, -1, height, height + 1):
            row = s1[pl.ds(CP, CP), block(2, r)].astype(F32)
            first = jnp.where(pair_of == r + 2, rolled(row, spot(r)), first)
            last = jnp.where(pair_of == r + 2, rolled(row, spot(r) + 2), last)
        on_left = lane < LANES // 2
        lefts = (low, rolled(low, -1), first, rolled(first, -1))
        rights = tuple(rolled(v, LANES // 2 - k) for v in (last, high) for k in (0, 1))
        beside = tuple(jnp.where(on_left, lefts[j], rights[j + 1]) for j in range(3))
        at_edge = tuple(jnp.where(on_left, lefts[j + 1], rights[j]) for j in range(3))
        for i in range(3):
            for j in range(3):
                part = pl.ds(j * CP, CP)
                se[i, part, pl.ds(0, LANES)] = rolled(beside[j], 2 * (1 - i)).astype(BF16)
                se[i, part, pl.ds(LANES, LANES)] = rolled(at_edge[j], 2 * (1 - i)).astype(BF16)
        return jnp.concatenate([beside[1], at_edge[1]], axis=1)

    def conv(window):
        return sum(dot(wt_ref[i], window(i)) for i in range(3))

    def network(pre, centre):
        cdf = 0.5 * (1.0 + lax.erf(pre * ROOT_HALF))
        update = dot(wo_ref[...], (pre * cdf).astype(BF16))
        return centre.astype(F32) + update, lambda: cdf + pre * jnp.exp(-0.5 * pre * pre) * NORM_DENSITY

    def conv_chunk(s, rim, n):
        return conv(lambda i: s[:, block(rim, 2 * n + i - 1, 2)])

    def forward_chunk(pre, s, rim, n, slope, inner_only):
        state, tangent = network(pre, s[pl.ds(CP, CP), block(rim, 2 * n, 2)])
        slope[:, pl.ds(n * WIDE, WIDE)] = jnp.where(edge_wide, 0.0, tangent()) if inner_only else tangent()
        return state.astype(BF16)

    def pipelined(order, start, finish, lag=1):
        order = list(order)
        held = [start(n) for n in order[:lag]]
        for k, n in enumerate(order):
            if k + lag < len(order):
                held.append(start(order[k + lag]))
            finish(n, held.pop(0))

    def kept_cells():
        here = lax.rem(lane_iota(hid), LANES // 2)
        return jnp.logical_and(lax.rem(here, 2) == 0, jnp.logical_and(here >= spot(0), here <= spot(height - 1)))

    def first_rim(centre):
        up, down = has_up.astype(F32), has_down.astype(F32)
        rows = (-1, height)
        state, _ = network(
            conv(lambda i: jnp.concatenate([s1[:, block(2, r + i - 1)] for r in rows], axis=1)),
            jnp.concatenate([s1[pl.ds(CP, CP), block(2, r)] for r in rows], axis=1),
        )
        s2[pl.ds(CP, CP), block(1, -1)] = (state[:, :LANES] * up).astype(BF16)
        s2[pl.ds(CP, CP), block(1, height)] = (state[:, LANES:] * down).astype(BF16)
        sides, tangent = network(conv(lambda i: se[i]), centre)
        place = lax.rem(lane, LANES // 2)
        inside = jnp.where(place == spot(-1), up, jnp.where(place == spot(height), down, 1.0))
        slope_edge[...] = jnp.where(kept_cells(), tangent()[:, LANES:], 0.0)
        return tuple((sides[:, k * LANES : (k + 1) * LANES] * inside).astype(BF16).astype(F32) for k in (0, 1))

    pl.semaphore_wait(barrier, pairs - 1 + 3 * (has_up.astype(jnp.int32) + has_down.astype(jnp.int32)))
    send_state()

    for load in loads[1:]:
        load.wait()
    def fixed(value, top):
        return jnp.round(value * (HALF_WORDS / top)).astype(jnp.int32)

    def packet_words(which):
        first, second, third, fourth = (fixed(rows_of(which, w_ref.at[k]), 1.0) for k in range(4))
        return (
            (first - HALF_WORD) * WORD + second,
            (third - HALF_WORD) * WORD + fourth,
            rows_of(which, cell_ref) * WORD + fixed(rows_of(which, prec_ref), TOP_PRECISION),
            jnp.round(rows_of(which, val_ref) * VALUE_STEPS).astype(jnp.int32),
        )

    for k, word in enumerate(packet_words(1 - side)):
        given[:, k, :] = word
    to_mate = pltpu.make_async_remote_copy(
        src_ref=given, dst_ref=packed.at[1], send_sem=gsend.at[0], recv_sem=grecv.at[0],
        device_id=mate, device_id_type=MESH,
    )
    to_mate.start()
    for k, word in enumerate(packet_words(side)):
        packed[0, :, k, :] = word

    def post(other, where):
        pltpu.make_async_remote_copy(
            src_ref=packed.at[:, other], dst_ref=recv.at[:, my_pair],
            send_sem=psend, recv_sem=precv, device_id=where, device_id_type=MESH,
        ).start()

    wpad[...] = jnp.zeros((LANES, hid), F32)
    bias = cb_ref[...]
    bias_parts = []
    for _ in range(3):
        part = bias.astype(BF16).astype(F32)
        bias_parts.append(part)
        bias = bias - part
    spare = lax.broadcasted_iota(jnp.int32, (hid - 3 * CP, hid), 0)
    bias_rows = jnp.zeros((hid - 3 * CP, hid), F32)
    for k, part in enumerate(bias_parts):
        bias_rows = jnp.where(spare == k, part, bias_rows)
    for i in range(3):
        for j in range(3):
            wpad[pl.ds(0, chan), :] = cw_ref[3 * i + j].astype(F32)
            wk[i, pl.ds(j * CP, CP), :] = wpad[pl.ds(0, CP), :].astype(BF16)
        wk[i, pl.ds(3 * CP, hid - 3 * CP), :] = (bias_rows if i == 1 else jnp.zeros_like(bias_rows)).astype(BF16)
        wt_ref[i] = jnp.transpose(wk[i].astype(F32)).astype(BF16)
    wpad[pl.ds(0, chan), :] = ow_ref[...].astype(F32)
    wo_ref[...] = wpad[pl.ds(0, CP), :].astype(BF16)
    wot_ref[...] = jnp.transpose(wpad[...]).astype(BF16)
    for c in range(chan):
        grad_ref[pl.ds(c * height, height), :] = bp_ref[0, c] * (x_ref[c].astype(F32) - xb_ref[c].astype(F32))

    def ones(breadth):
        return jnp.ones((hid - 3 * CP, breadth), BF16)

    s1[pl.ds(3 * CP, hid - 3 * CP), :] = ones((height + 4) * LANES)
    s2[pl.ds(3 * CP, hid - 3 * CP), :] = ones((height + 2) * LANES)
    for i in range(3):
        se[i, pl.ds(3 * CP, hid - 3 * CP), :] = ones(WIDE)

    column_wide = lax.broadcasted_iota(jnp.int32, (hid, WIDE), 1)
    column_wide = lax.rem(column_wide, LANES)
    edge_wide = jnp.logical_or(column_wide == 0, column_wide == LANES - 1)
    early = range(1, chunks - 1)

    def first_conv(n):
        return conv_chunk(s1, 2, n)

    def first_step(n, pre):
        s2[pl.ds(CP, CP), block(1, 2 * n, 2)] = forward_chunk(pre, s1, 2, n, slope1, True)

    def early_step(n, pre):
        to_some(n - 1, len(early), post)
        first_step(n, pre)

    to_mate.wait_recv()
    recv[:, my_pair] = packed[:, my_pair]
    pipelined(early, first_conv, early_step)
    receive_state()
    shift_far_rows()
    pipelined((0, chunks - 1), first_conv, first_step)
    beside, at_edge = first_rim(spread_columns())
    merge_columns(at_edge, beside)

    def second_step(n, pre):
        sobs[n] = forward_chunk(pre, s2, 1, n, slope2, False)

    pipelined(range(chunks), lambda n: conv_chunk(s2, 1, n), second_step)
    hid_lane = lane_iota(hid)
    tangents = jnp.zeros((hid, LANES), F32)
    for r in range(height):
        tangents = jnp.where((hid_lane + 1) // 2 == r + 2, rolled(slope2[:, block(0, r)], spot(r)), tangents)
    tangents = jnp.where(hid_lane < LANES // 2, tangents, rolled(tangents, LANES // 2 + 1))
    slope_edge2[...] = jnp.where(kept_cells(), tangents, 0.0)

    others = pl.ds(0, pairs - 1)
    pltpu.make_async_remote_copy(
        src_ref=packed.at[:, others], dst_ref=recv.at[:, others], send_sem=psend, recv_sem=precv,
        device_id=ids[RIGHT], device_id_type=MESH,
    ).wait()

    def unfixed(value, top):
        return value.astype(F32) * (top / HALF_WORDS)

    for which in range(2):

        def field(k, value, which=which):
            opened[pl.ds(which * pairs * 8 + k, pairs, stride=8), :] = value

        words = recv[which, :, 2, :]
        field(0, (words >> 24).astype(F32))
        field(1, ((words >> 16) & (LANES - 1)).astype(F32))
        field(7, unfixed(words & (WORD - 1), TOP_PRECISION))
        for k in range(2):
            words = recv[which, :, k, :]
            field(2 + 2 * k, unfixed((words >> 16) + HALF_WORD, 1.0))
            field(3 + 2 * k, unfixed(words & (WORD - 1), 1.0))
        field(6, recv[which, :, 3, :].astype(F32) * (1.0 / VALUE_STEPS))

    def patch_of(group, u):
        k = group * GROUP + u
        which, pair_id = k // pairs, lax.rem(k, pairs)
        at_side = jnp.where(which == 0, side, 1 - side)
        owner = (2 * (pair_id // n_lon) + at_side) * n_lon + lax.rem(pair_id, n_lon)
        return swath_ref[0, owner]

    column = lax.broadcasted_iota(jnp.int32, (LANES, LANES), 0).astype(F32).astype(BF16)
    channel = lax.broadcasted_iota(jnp.int32, (CP, LANES), 0).astype(F32)
    zero = jnp.zeros((LANES, LANES), BF16)

    def estimate(group, carry):
        def start(u):
            k = group * GROUP + u
            packet = opened[pl.ds(pl.multiple_of(k * 8, 8), 8), :]

            def row(which):
                return jnp.broadcast_to(packet[which : which + 1].astype(BF16), (LANES, LANES))

            at = row(1)
            here, after = column == at, column == at + 1
            table = jnp.concatenate(
                [
                    jnp.where(here, row(2), jnp.where(after, row(3), zero)),
                    jnp.where(here, row(4), jnp.where(after, row(5), zero)),
                ],
                axis=0,
            )
            bsc[k] = table
            return packet, dot(sobs[patch_of(group, u)], table)

        def finish(u, given):
            k = group * GROUP + u
            packet, found = given
            picked = channel == packet[0:1]
            gap = jnp.sum(jnp.where(picked, found, 0.0), axis=0, keepdims=True) - packet[6:7]
            inn[k // pairs, lax.rem(k, pairs)] = gap
            qsc[k] = jnp.where(picked, packet[7:8] * gap, 0.0).astype(BF16)

        pipelined(range(GROUP), start, finish, LAG)
        return carry

    lax.fori_loop(0, owners // GROUP, estimate, 0)
    hist[0] = jnp.zeros((CP, WIDE), F32)

    def pull(group, last):
        slots = [last]

        def start(u):
            k = group * GROUP + u
            return lax.dot_general(qsc[k], bsc[k], (((1,), (1,)), ((), ())), preferred_element_type=F32)

        def finish(u, share):
            k = group * GROUP + u
            patch = patch_of(group, u)
            before = sum(jnp.where(patch == m, slots[-1][m], 0) for m in range(chunks))
            hist[k + 1] = hist[before] + share
            slots.append(tuple(jnp.where(patch == m, k + 1, slots[-1][m]) for m in range(chunks)))

        pipelined(range(GROUP), start, finish, LAG)
        return slots[-1]

    last = lax.fori_loop(0, owners // GROUP, pull, (jnp.int32(0),) * chunks)
    inn_recv[:, my_pair] = inn[:, my_pair]

    def give_back(other, where):
        pltpu.make_async_remote_copy(
            src_ref=inn.at[:, other], dst_ref=inn_recv.at[:, my_pair],
            send_sem=isend, recv_sem=irecv, device_id=where, device_id_type=MESH,
        ).start()

    def tap(i, j, r):
        return ybuf[pl.ds((3 * (i + 1) + j + 1) * CP, CP), pl.ds(r * LANES, LANES)]

    def summed(j, r):
        total = None
        for i in (-1, 0, 1):
            if 0 <= r - i < height:
                part = tap(i, j, r - i)
                total = part if total is None else total + part
        return total

    def rim_sources(t):
        table = dict.fromkeys((LEFT, RIGHT, UL, UR, DL, DR), bcol.at[t])
        return table | {UP: brow.at[t, 0], DOWN: brow.at[t, 1]}

    def rim_targets(t):
        table = {d: rcol.at[t, k] for k, d in enumerate((LEFT, RIGHT, UL, UR, DL, DR))}
        return table | {UP: rrow.at[t, 0], DOWN: rrow.at[t, 1]}

    def spread_of(cotangent, slope):
        breadth = cotangent.shape[1]
        rounded = jnp.concatenate([cotangent.astype(BF16), jnp.zeros((LANES - CP, breadth), BF16)], axis=0)
        return (dot(wot_ref[...], rounded) * slope).astype(BF16)

    def products(cotangent, slope):
        def start(n):
            return spread_of(cotangent(n), slope[:, pl.ds(n * WIDE, WIDE)])

        def finish(n, spread):
            for i in range(3):
                ybuf[pl.ds(3 * i * CP, 3 * CP), pl.ds(n * WIDE, WIDE)] = dot(wk[i, pl.ds(0, 3 * CP), :], spread)

        pipelined(range(chunks), start, finish)

    def inner(t_low, t_mid, t_high):
        return (
            t_mid
            + jnp.where(first_lane, 0.0, rolled(t_high, 1))
            + jnp.where(last_lane, 0.0, rolled(t_low, -1))
        )

    def own_sums(own):
        for r in range(height):
            ubuf[0, :, block(1, r)] = inner(*(summed(j, r) for j in (-1, 0, 1))) + own(r)

    def local_sums(t):
        columns = jnp.zeros((CP, LANES), F32)
        for r in range(-1, height + 1):
            t_low, t_mid, t_high = (summed(j, r) for j in (-1, 0, 1))
            ubuf[t, :, block(1, r)] = inner(t_low, t_mid, t_high)
            columns = gathered(columns, r, jnp.where(first_lane, t_low, t_high))
        return columns

    def send_rim(t, above, below, columns):
        brow[t, 0] = above.astype(BF16)
        brow[t, 1] = below.astype(BF16)
        bcol[t] = columns.astype(BF16)
        src, dst = rim_sources(t), rim_targets(t)
        for d in (UP, DOWN, LEFT, RIGHT, UL, UR, DL, DR):
            send(src[d], dst[opposite[d]], t, d, bsend, brecv)

    def receive_rim(t):
        dst = rim_targets(t)
        for d in range(8):
            wait_recv(dst[d], t, d, bsend, brecv)
        for there, row, slots in ((has_up, 0, (2, 3)), (has_down, 1, (4, 5))):

            @pl.when(jnp.logical_not(there))
            def _():
                rrow[t, row] = jnp.zeros((CP, LANES), BF16)
                for slot in slots:
                    rcol[t, slot] = jnp.zeros((CP, LANES), BF16)

        from_left, from_right, ul, ur, dl, dr = (rcol[t, k].astype(F32) for k in range(6))
        inside = jnp.logical_and(slot_of >= 2, slot_of < height + 2)
        inflow = jnp.where(inside, jnp.where(even, rolled(from_left, 1), rolled(from_right, -1)), 0.0)
        top, bottom, past, before = spot(0), spot(height - 1), spot(height), spot(-1)
        for value, came, goes in (
            (ul, past - 1, top), (ur, past, top - 1), (dl, before - 1, bottom), (dr, before, bottom - 1),
        ):
            inflow = inflow + jnp.where(lane == goes, rolled(value, goes - came), 0.0)
        return rrow[t, 0].astype(F32), rrow[t, 1].astype(F32), inflow

    far = height - 1
    outside = slot_of <= height + 2

    def rim_products(top_row, bottom_row, at_edge, slopes):
        late = spread_of(
            jnp.concatenate([top_row, bottom_row, apart(at_edge)], axis=1), jnp.concatenate(slopes, axis=1)
        )
        for i in range(3):
            xbuf[pl.ds(3 * i * CP, 3 * CP), :] = dot(wk[i, pl.ds(0, 3 * CP), :], late)

    def late_tap(i, j, part):
        return xbuf[pl.ds((3 * (i + 1) + j + 1) * CP, CP), pl.ds(part * LANES, LANES)]

    def late_row(part, i):
        return tuple(late_tap(i, j, part) for j in (-1, 0, 1))

    def late_columns(j):
        return sum(rolled(late_tap(i, j, 2), 2 * i) for i in (-1, 0, 1))

    def outward(to_low, to_high):
        return jnp.where(outside, jnp.where(even, to_low, rolled(to_high, -LANES // 2 - 1)), 0.0)

    def pull_row(r):
        return hist[last[r // 2]][:, (r % 2) * LANES : (r % 2 + 1) * LANES]

    at_edge = jnp.zeros((CP, LANES), F32)
    for r in range(height):
        at_edge = gathered(at_edge, r, pull_row(r))
    rim_products(
        pull_row(0), pull_row(far), at_edge,
        [slope2[:, pl.ds(0, LANES)], slope2[:, pl.ds(far * LANES, LANES)], slope_edge2[...]],
    )
    send_rim(
        0, inner(*late_row(0, -1)), inner(*late_row(1, 1)), outward(late_columns(-1), late_columns(1))
    )
    products(lambda n: hist[last[n]], slope2)
    own_sums(pull_row)

    to_some(0, 1, give_back)
    products(lambda n: ubuf[0, :, block(1, 2 * n, 2)], slope1)
    columns = local_sums(1)
    at_edge = jnp.zeros((CP, LANES), F32)
    for r in range(height):
        at_edge = gathered(at_edge, r, ubuf[0, :, block(1, r)])
    above, below, inflow = receive_rim(0)
    at_edge = at_edge + inflow
    at_edge = at_edge + gathered(gathered(jnp.zeros((CP, LANES), F32), 0, above), far, below)
    rim_products(
        above, below, at_edge,
        [slope1[:, pl.ds(0, LANES)], slope1[:, pl.ds(far * LANES, LANES)], slope_edge[...]],
    )
    to_low, to_same, to_high = (late_columns(j) for j in (-1, 0, 1))
    columns = columns + outward(to_low, to_high)
    for part, base in ((0, 0), (1, far)):
        for i in (-1, 0, 1):
            t_low, _, t_high = late_row(part, i)
            columns = columns + gathered(
                jnp.zeros((CP, LANES), F32), base + i, jnp.where(first_lane, t_low, t_high)
            )
    same = joined(to_same)
    next_in = jnp.where(even, rolled(to_low, -LANES // 2 - 2), rolled(to_high, 1))
    second = jnp.logical_or(lane == 1, lane == LANES - 2)

    def from_columns(r, outermost):
        return jnp.where(edge, rolled(outermost, -spot(r)), 0.0) + jnp.where(second, rolled(next_in, -spot(r)), 0.0)

    send_rim(
        1,
        ubuf[1, :, block(1, -1)] + inner(*late_row(0, -1)) + from_columns(-1, same),
        ubuf[1, :, block(1, height)] + inner(*late_row(1, 1)) + from_columns(height, same),
        columns,
    )
    pltpu.make_async_remote_copy(
        src_ref=inn.at[:, others], dst_ref=inn_recv.at[:, others], send_sem=isend, recv_sem=irecv,
        device_id=ids[RIGHT], device_id_type=MESH,
    ).wait()
    innov_to_mate = pltpu.make_async_remote_copy(
        src_ref=inn_recv.at[1], dst_ref=inn_mate, send_sem=gsend.at[1], recv_sem=grecv.at[1],
        device_id=mate, device_id_type=MESH,
    )
    innov_to_mate.start()
    outermost = same + inflow
    for r in range(height):
        value = ubuf[0, :, block(1, r)] + ubuf[1, :, block(1, r)] + from_columns(r, outermost)
        if r < 2:
            value = value + inner(*late_row(0, r))
        if r >= far - 1:
            value = value + inner(*late_row(1, r - far))
        if r == 0:
            value = value + above
        if r == far:
            value = value + below
        ubuf[0, :, block(1, r)] = value
    above, below, inflow = receive_rim(1)
    for r in range(height):
        value = ubuf[0, :, block(1, r)] + jnp.where(edge, rolled(inflow, -spot(r)), 0.0)
        if r == 0:
            value = value + above
        if r == far:
            value = value + below
        here = pl.ds(r, chan, stride=height)
        grad_ref[here, :] = grad_ref[here, :] + value[:chan]

    innov_to_mate.wait()
    to_mate.wait_send()
    for h in range(halves):
        part = pl.ds(h * n_lon, n_lon)
        for which, ref in ((side, inn_recv.at[0]), (1 - side, inn_mate)):
            rows = pl.ds(pl.multiple_of((2 * h + which) * n_lon, n_lon), n_lon)
            innov_ref[rows, :] = ref[part].reshape(n_lon, LANES)
    for d in range(8):
        wait_send(state_sources[d], 0, d, fsend, frecv)
    for t in range(2):
        src = rim_sources(t)
        for d in range(8):
            wait_send(src[d], t, d, bsend, brecv)


def hand_over(gradient_in, innov_in, gradient_out, innov_out, gradient_held, innov_held, sems):
    chan = gradient_in.shape[0]
    cuts = [chan * k // PIECES for k in range(PIECES + 1)]
    parts = [pl.ds(a, b - a) for a, b in zip(cuts, cuts[1:])]
    routes = [(gradient_in.at[p], gradient_held.at[p], gradient_out.at[p]) for p in parts]
    routes.append((innov_in, innov_held, innov_out))
    reads = [pltpu.make_async_copy(src, held, sems.at[0, k]) for k, (src, held, _) in enumerate(routes)]
    writes = [pltpu.make_async_copy(held, dst, sems.at[1, k]) for k, (_, held, dst) in enumerate(routes)]
    for read in reads:
        read.start()
    for read, write in zip(reads, writes):
        read.wait()
        write.start()
    for write in writes:
        write.wait()


def local(
    n_lat, n_lon,
    initial_state, background_state, background_precision, conv_weight, conv_bias, out_weight,
    swath_patch, obs_cell, obs_weights, obs_value, obs_precision,
):
    chan, height, breadth = initial_state.shape
    hid = conv_weight.shape[2]
    owners = n_lat * n_lon
    chunks = height // 2
    cells = height * breadth
    vmem = pl.BlockSpec(memory_space=pltpu.VMEM)
    hbm = pl.BlockSpec(memory_space=pltpu.HBM)
    smem = pl.BlockSpec(memory_space=pltpu.SMEM)
    dma = pltpu.SemaphoreType.DMA
    gradient, innov = pl.pallas_call(
        functools.partial(kernel, n_lat, n_lon, hid),
        out_shape=(
            jax.ShapeDtypeStruct((chan * height, LANES), F32),
            jax.ShapeDtypeStruct((owners, LANES), F32),
        ),
        in_specs=[hbm, hbm, smem, vmem, vmem, vmem, smem] + [hbm] * 4,
        out_specs=(vmem, vmem),
        scratch_shapes=[
            pltpu.VMEM((chan, height, breadth), BF16),
            pltpu.VMEM((chan, height, breadth), BF16),
            pltpu.VMEM((owners, LANES), jnp.int32),
            pltpu.VMEM((4, owners, LANES), F32),
            pltpu.VMEM((owners, LANES), F32),
            pltpu.VMEM((owners, LANES), F32),
            pltpu.VMEM((LANES, hid), F32),
            pltpu.VMEM((3, hid, hid), BF16),
            pltpu.VMEM((3, hid, hid), BF16),
            pltpu.VMEM((CP, hid), BF16),
            pltpu.VMEM((hid, LANES), BF16),
            pltpu.VMEM((CP * height, LANES), F32),
            pltpu.VMEM((owners // 2, 4, LANES), jnp.int32),
            pltpu.VMEM((2, owners // 2, 4, LANES), jnp.int32),
            pltpu.VMEM((2, owners // 2, 4, LANES), jnp.int32),
            pltpu.VMEM((owners * 8, LANES), F32),
            pltpu.VMEM((hid, (height + 4) * LANES), BF16),
            pltpu.VMEM((hid, (height + 2) * LANES), BF16),
            pltpu.VMEM((3, hid, WIDE), BF16),
            pltpu.VMEM((chunks, CP, WIDE), BF16),
            pltpu.VMEM((hid, cells), F32),
            pltpu.VMEM((hid, cells), F32),
            pltpu.VMEM((hid, LANES), F32),
            pltpu.VMEM((hid, LANES), F32),
            pltpu.VMEM((2, CP, LANES), BF16),
            pltpu.VMEM((6, CP, LANES), BF16),
            pltpu.VMEM((owners, WIDE, LANES), BF16),
            pltpu.VMEM((owners, CP, LANES), BF16),
            pltpu.VMEM((2, owners // 2, 1, LANES), F32),
            pltpu.VMEM((2, owners // 2, 1, LANES), F32),
            pltpu.VMEM((owners // 2, 1, LANES), F32),
            pltpu.VMEM((owners + 1, CP, WIDE), F32),
            pltpu.VMEM((9 * CP, cells), F32),
            pltpu.VMEM((9 * CP, 3 * LANES), F32),
            pltpu.VMEM((2, CP, (height + 2) * LANES), F32),
            pltpu.VMEM((2, 2, CP, LANES), BF16),
            pltpu.VMEM((2, CP, LANES), BF16),
            pltpu.VMEM((2, 2, CP, LANES), BF16),
            pltpu.VMEM((2, 6, CP, LANES), BF16),
            dma((1, 8)), dma((1, 8)), dma((2, 8)), dma((2, 8)),
            dma, dma, dma, dma, dma((2,)), dma((2,)), dma((6,)),
        ],
        compiler_params=pltpu.CompilerParams(
            collective_id=0, has_side_effects=True, vmem_limit_bytes=56 * 1024 * 1024
        ),
    )(
        initial_state, background_state, background_precision[None], conv_weight, conv_bias[None], out_weight, swath_patch,
        obs_cell[0], obs_weights[:, 0], obs_value[0], obs_precision[0],
    )
    return pl.pallas_call(
        hand_over,
        out_shape=(
            jax.ShapeDtypeStruct((chan, height, breadth), F32),
            jax.ShapeDtypeStruct((1, owners, LANES), F32),
        ),
        in_specs=[hbm, hbm],
        out_specs=(hbm, hbm),
        scratch_shapes=[
            pltpu.VMEM((chan, height, breadth), F32),
            pltpu.VMEM((1, owners, LANES), F32),
            dma((2, PIECES + 1)),
        ],
        compiler_params=pltpu.CompilerParams(vmem_limit_bytes=56 * 1024 * 1024),
    )(gradient.reshape(chan, height, breadth), innov[None])


def solution(mesh):
    tile = P(None, "lat", "lon")
    owner = ("lat", "lon")
    in_specs = (
        tile, tile, P(), P(), P(), P(),
        P(owner, None), P(owner, None, None), P(None, owner, None, None), P(owner, None, None), P(owner, None, None),
    )
    return jax.shard_map(
        functools.partial(local, mesh.shape["lat"], mesh.shape["lon"]),
        mesh=mesh, in_specs=in_specs, out_specs=(tile, P(owner, None, None)), check_vma=False,
    )
```

```python
import functools

import jax
import jax.numpy as jnp
from jax import lax
from jax.experimental import pallas as pl
from jax.experimental.pallas import tpu as pltpu
from jax.sharding import PartitionSpec as P

MESH = pl.DeviceIdType.MESH
F32 = jnp.float32
BF16 = jnp.bfloat16
CP = 80
LANES = 128
WIDE = 256
ROOT_HALF = 0.7071067811865476
NORM_DENSITY = 0.3989422804014327
UP, DOWN, LEFT, RIGHT, UL, UR, DL, DR = range(8)
GROUP = 32
LAG = 3
PIECES = 2
WORD = 65536
HALF_WORD = 32768
HALF_WORDS = 65535.0
TOP_PRECISION = 3.0
VALUE_STEPS = 2.0**28


def dot(a, b):
    return jnp.dot(a, b, preferred_element_type=F32)


def lane_iota(rows):
    return lax.broadcasted_iota(jnp.int32, (rows, LANES), 1)


def kernel(
    n_lat, n_lon, hid,
    x_hbm, xb_hbm, bp_ref, cw_ref, cb_ref, ow_ref, swath_ref, cell_hbm, w_hbm, val_hbm, prec_hbm,
    grad_ref, innov_ref,
    x_ref, xb_ref, cell_ref, w_ref, val_ref, prec_ref, wpad, wk, wt_ref, wo_ref, wot_ref, x32, given, packed, recv, opened, s1, s2, se, sobs, slope1, slope2, slope_edge, slope_edge2, csend, hcol,
    bsc, qsc, inn, inn_recv, inn_mate, hist, ybuf, xbuf, ubuf, brow, bcol, rrow, rcol,
    fsend, frecv, bsend, brecv, psend, precv, isend, irecv, gsend, grecv, loaded,
):
    chan, height = x_ref.shape[0], x_ref.shape[1]
    owners = n_lat * n_lon
    chunks = height // 2
    lat = lax.axis_index("lat")
    lon = lax.axis_index("lon")
    has_up = lat > 0
    has_down = lat < n_lat - 1
    left = lax.rem(lon + n_lon - 1, n_lon)
    right = lax.rem(lon + 1, n_lon)
    ids = {
        UP: (lat - 1, lon), DOWN: (lat + 1, lon), LEFT: (lat, left), RIGHT: (lat, right),
        UL: (lat - 1, left), UR: (lat - 1, right), DL: (lat + 1, left), DR: (lat + 1, right),
    }
    opposite = {UP: DOWN, DOWN: UP, LEFT: RIGHT, RIGHT: LEFT, UL: DR, DR: UL, UR: DL, DL: UR}

    barrier = pltpu.get_barrier_semaphore()

    def wrapped(value, count):
        return value - jnp.where(value >= count, count, 0)

    side, half = lax.rem(lat, 2), lat // 2
    halves = n_lat // 2
    pairs = halves * n_lon
    mate = {"lat": lat + 1 - 2 * side}
    my_pair = half * n_lon + lon
    rounds = [(step, ahead) for step in range(halves) for ahead in range(n_lon) if step or ahead]

    def to_some(part, parts, act):
        for step, ahead in rounds[len(rounds) * part // parts : len(rounds) * (part + 1) // parts]:
            there, column = wrapped(half + step, halves), wrapped(lon + ahead, n_lon)
            act(there * n_lon + column, (2 * there + side, column))

    def rows_of(which, ref):
        return jnp.concatenate(
            [ref[pl.ds(pl.multiple_of((2 * h + which) * n_lon, n_lon), n_lon), :] for h in range(halves)], axis=0
        )

    def greet(_, where):
        pl.semaphore_signal(barrier, inc=1, device_id=where, device_id_type=MESH)

    across = {UP: has_up, UL: has_up, UR: has_up, DOWN: has_down, DL: has_down, DR: has_down}

    loads = [
        pltpu.make_async_copy(src, dst, loaded.at[k])
        for k, (src, dst) in enumerate(
            (
                (x_hbm, x_ref), (xb_hbm, xb_ref), (cell_hbm, cell_ref),
                (w_hbm, w_ref), (val_hbm, val_ref), (prec_hbm, prec_ref),
            )
        )
    ]
    for load in loads:
        load.start()
    to_some(0, 1, greet)
    for d, there in across.items():
        pl.when(there)(functools.partial(greet, None, ids[d]))

    x32[pl.ds(chan * height, (CP - chan) * height), :] = jnp.zeros(((CP - chan) * height, LANES), F32)
    loads[0].wait()
    x32[pl.ds(0, chan * height), :] = x_ref[...].astype(F32).reshape(chan * height, LANES)
    lane = lane_iota(CP)
    first_lane = lane == 0
    last_lane = lane == LANES - 1

    def block(rim, r, count=1):
        return pl.ds((r + rim) * LANES, count * LANES)

    def rolled(value, shift):
        return pltpu.roll(value, shift % LANES, 1) if shift % LANES else value

    def spot(r):
        return 2 * (r + 2)

    even = lax.rem(lane, 2) == 0
    edge = jnp.logical_or(first_lane, last_lane)
    slot_of = (lane + 1) // 2

    def joined(value):
        return jnp.where(even, value, rolled(value, -LANES // 2 - 1))

    def apart(value):
        return jnp.where(lane < LANES // 2, value, rolled(value, LANES // 2 + 1))

    def gathered(total, r, row):
        return jnp.where(slot_of == r + 2, rolled(row, spot(r)), total)

    pair_of = lane // 2
    to_left = jnp.zeros((CP, LANES), F32)
    to_right = jnp.zeros((CP, LANES), F32)
    for r in range(height):
        row = x32[pl.ds(r, CP, stride=height), :]
        s1[pl.ds(CP, CP), block(2, r)] = row.astype(BF16)
        s1[pl.ds(0, CP), block(2, r)] = rolled(row, 1).astype(BF16)
        s1[pl.ds(2 * CP, CP), block(2, r)] = rolled(row, -1).astype(BF16)
        to_left = jnp.where(pair_of == r + 2, rolled(row, spot(r)), to_left)
        to_right = jnp.where(pair_of == r + 2, rolled(row, spot(r) + 2), to_right)
    csend[0] = to_left.astype(BF16)
    csend[1] = to_right.astype(BF16)

    def guarded(d):
        if d in (UP, UL, UR):
            return pl.when(has_up)
        if d in (DOWN, DL, DR):
            return pl.when(has_down)
        return lambda f: f()

    def send(src, dst, t, d, sends, recvs):
        copy = pltpu.make_async_remote_copy(
            src_ref=src, dst_ref=dst, send_sem=sends.at[t, d], recv_sem=recvs.at[t, opposite[d]],
            device_id=ids[d], device_id_type=MESH,
        )
        guarded(d)(copy.start)

    def wait_recv(dst, t, d, sends, recvs):
        copy = pltpu.make_async_remote_copy(
            src_ref=dst, dst_ref=dst, send_sem=sends.at[t, d], recv_sem=recvs.at[t, d],
            device_id=ids[d], device_id_type=MESH,
        )
        guarded(d)(copy.wait_recv)

    def wait_send(src, t, d, sends, recvs):
        copy = pltpu.make_async_remote_copy(
            src_ref=src, dst_ref=src, send_sem=sends.at[t, d], recv_sem=recvs.at[t, d],
            device_id=ids[d], device_id_type=MESH,
        )
        guarded(d)(copy.wait_send)

    def pair(r):
        return s1.at[pl.ds(CP, CP), block(2, r, 2)]

    state_sources = {
        UP: pair(0), DOWN: pair(height - 2),
        LEFT: csend.at[0], UL: csend.at[0], DL: csend.at[0],
        RIGHT: csend.at[1], UR: csend.at[1], DR: csend.at[1],
    }
    state_targets = {UP: pair(-2), DOWN: pair(height)}
    for k, d in enumerate((LEFT, RIGHT, UL, UR, DL, DR)):
        state_targets[d] = hcol.at[k]

    def send_state():
        for d in (UP, DOWN, LEFT, RIGHT, UL, UR, DL, DR):
            send(state_sources[d], state_targets[opposite[d]], 0, d, fsend, frecv)

    def receive_state():
        for d in range(8):
            wait_recv(state_targets[d], 0, d, fsend, frecv)
        for there, r, slots in ((has_up, -2, (2, 3)), (has_down, height, (4, 5))):

            @pl.when(jnp.logical_not(there))
            def _():
                s1[pl.ds(CP, CP), block(2, r, 2)] = jnp.zeros((CP, WIDE), BF16)
                for slot in slots:
                    hcol[slot] = jnp.zeros((CP, LANES), BF16)

    def shift_far_rows():
        for r in (-2, -1, height, height + 1):
            row = s1[pl.ds(CP, CP), block(2, r)].astype(F32)
            s1[pl.ds(0, CP), block(2, r)] = rolled(row, 1).astype(BF16)
            s1[pl.ds(2 * CP, CP), block(2, r)] = rolled(row, -1).astype(BF16)

    def merge_columns(at_edge, beside):
        at_edge, beside = joined(at_edge), joined(beside)
        for r in range(-1, height + 1):
            row = jnp.where(edge, rolled(at_edge, -spot(r)), s2[pl.ds(CP, CP), block(1, r)].astype(F32))
            outer = rolled(beside, -spot(r))
            s2[pl.ds(0, CP), block(1, r)] = jnp.where(first_lane, outer, rolled(row, 1)).astype(BF16)
            s2[pl.ds(CP, CP), block(1, r)] = row.astype(BF16)
            s2[pl.ds(2 * CP, CP), block(1, r)] = jnp.where(last_lane, outer, rolled(row, -1)).astype(BF16)

    def with_corners(side, above, below):
        middle = jnp.logical_and(pair_of >= 2, pair_of < height + 2)
        outer = jnp.where(pair_of < 2, rolled(above, -2 * height), rolled(below, 2 * height))
        return jnp.where(middle, side, outer)

    def spread_columns():
        from_left, from_right, ul, ur, dl, dr = (hcol[k].astype(F32) for k in range(6))
        low = with_corners(from_left, ul, dl)
        high = with_corners(from_right, ur, dr)
        first = csend[0].astype(F32)
        last = csend[1].astype(F32)
        for r in (-2, -1, height, height + 1):
            row = s1[pl.ds(CP, CP), block(2, r)].astype(F32)
            first = jnp.where(pair_of == r + 2, rolled(row, spot(r)), first)
            last = jnp.where(pair_of == r + 2, rolled(row, spot(r) + 2), last)
        on_left = lane < LANES // 2
        lefts = (low, rolled(low, -1), first, rolled(first, -1))
        rights = tuple(rolled(v, LANES // 2 - k) for v in (last, high) for k in (0, 1))
        beside = tuple(jnp.where(on_left, lefts[j], rights[j + 1]) for j in range(3))
        at_edge = tuple(jnp.where(on_left, lefts[j + 1], rights[j]) for j in range(3))
        for i in range(3):
            for j in range(3):
                part = pl.ds(j * CP, CP)
                se[i, part, pl.ds(0, LANES)] = rolled(beside[j], 2 * (1 - i)).astype(BF16)
                se[i, part, pl.ds(LANES, LANES)] = rolled(at_edge[j], 2 * (1 - i)).astype(BF16)
        return jnp.concatenate([beside[1], at_edge[1]], axis=1)

    def conv(window):
        return sum(dot(wt_ref[i], window(i)) for i in range(3))

    def network(pre, centre):
        cdf = 0.5 * (1.0 + lax.erf(pre * ROOT_HALF))
        update = dot(wo_ref[...], (pre * cdf).astype(BF16))
        return centre.astype(F32) + update, lambda: cdf + pre * jnp.exp(-0.5 * pre * pre) * NORM_DENSITY

    def conv_chunk(s, rim, n):
        return conv(lambda i: s[:, block(rim, 2 * n + i - 1, 2)])

    def forward_chunk(pre, s, rim, n, slope, inner_only):
        state, tangent = network(pre, s[pl.ds(CP, CP), block(rim, 2 * n, 2)])
        slope[:, pl.ds(n * WIDE, WIDE)] = jnp.where(edge_wide, 0.0, tangent()) if inner_only else tangent()
        return state.astype(BF16)

    def pipelined(order, start, finish, lag=1):
        order = list(order)
        held = [start(n) for n in order[:lag]]
        for k, n in enumerate(order):
            if k + lag < len(order):
                held.append(start(order[k + lag]))
            finish(n, held.pop(0))

    def kept_cells():
        here = lax.rem(lane_iota(hid), LANES // 2)
        return jnp.logical_and(lax.rem(here, 2) == 0, jnp.logical_and(here >= spot(0), here <= spot(height - 1)))

    def first_rim(centre):
        up, down = has_up.astype(F32), has_down.astype(F32)
        rows = (-1, height)
        state, _ = network(
            conv(lambda i: jnp.concatenate([s1[:, block(2, r + i - 1)] for r in rows], axis=1)),
            jnp.concatenate([s1[pl.ds(CP, CP), block(2, r)] for r in rows], axis=1),
        )
        s2[pl.ds(CP, CP), block(1, -1)] = (state[:, :LANES] * up).astype(BF16)
        s2[pl.ds(CP, CP), block(1, height)] = (state[:, LANES:] * down).astype(BF16)
        sides, tangent = network(conv(lambda i: se[i]), centre)
        place = lax.rem(lane, LANES // 2)
        inside = jnp.where(place == spot(-1), up, jnp.where(place == spot(height), down, 1.0))
        slope_edge[...] = jnp.where(kept_cells(), tangent()[:, LANES:], 0.0)
        return tuple((sides[:, k * LANES : (k + 1) * LANES] * inside).astype(BF16).astype(F32) for k in (0, 1))

    pl.semaphore_wait(barrier, pairs - 1 + 3 * (has_up.astype(jnp.int32) + has_down.astype(jnp.int32)))
    send_state()

    for load in loads[1:]:
        load.wait()
    def fixed(value, top):
        return jnp.round(value * (HALF_WORDS / top)).astype(jnp.int32)

    def packet_words(which):
        first, second, third, fourth = (fixed(rows_of(which, w_ref.at[k]), 1.0) for k in range(4))
        return (
            (first - HALF_WORD) * WORD + second,
            (third - HALF_WORD) * WORD + fourth,
            rows_of(which, cell_ref) * WORD + fixed(rows_of(which, prec_ref), TOP_PRECISION),
            jnp.round(rows_of(which, val_ref) * VALUE_STEPS).astype(jnp.int32),
        )

    for k, word in enumerate(packet_words(1 - side)):
        given[:, k, :] = word
    to_mate = pltpu.make_async_remote_copy(
        src_ref=given, dst_ref=packed.at[1], send_sem=gsend.at[0], recv_sem=grecv.at[0],
        device_id=mate, device_id_type=MESH,
    )
    to_mate.start()
    for k, word in enumerate(packet_words(side)):
        packed[0, :, k, :] = word

    def post(other, where):
        pltpu.make_async_remote_copy(
            src_ref=packed.at[:, other], dst_ref=recv.at[:, my_pair],
            send_sem=psend, recv_sem=precv, device_id=where, device_id_type=MESH,
        ).start()

    wpad[...] = jnp.zeros((LANES, hid), F32)
    bias = cb_ref[...]
    bias_parts = []
    for _ in range(3):
        part = bias.astype(BF16).astype(F32)
        bias_parts.append(part)
        bias = bias - part
    spare = lax.broadcasted_iota(jnp.int32, (hid - 3 * CP, hid), 0)
    bias_rows = jnp.zeros((hid - 3 * CP, hid), F32)
    for k, part in enumerate(bias_parts):
        bias_rows = jnp.where(spare == k, part, bias_rows)
    for i in range(3):
        for j in range(3):
            wpad[pl.ds(0, chan), :] = cw_ref[3 * i + j].astype(F32)
            wk[i, pl.ds(j * CP, CP), :] = wpad[pl.ds(0, CP), :].astype(BF16)
        wk[i, pl.ds(3 * CP, hid - 3 * CP), :] = (bias_rows if i == 1 else jnp.zeros_like(bias_rows)).astype(BF16)
        wt_ref[i] = jnp.transpose(wk[i].astype(F32)).astype(BF16)
    wpad[pl.ds(0, chan), :] = ow_ref[...].astype(F32)
    wo_ref[...] = wpad[pl.ds(0, CP), :].astype(BF16)
    wot_ref[...] = jnp.transpose(wpad[...]).astype(BF16)
    for c in range(chan):
        grad_ref[pl.ds(c * height, height), :] = bp_ref[0, c] * (x_ref[c].astype(F32) - xb_ref[c].astype(F32))

    def ones(breadth):
        return jnp.ones((hid - 3 * CP, breadth), BF16)

    s1[pl.ds(3 * CP, hid - 3 * CP), :] = ones((height + 4) * LANES)
    s2[pl.ds(3 * CP, hid - 3 * CP), :] = ones((height + 2) * LANES)
    for i in range(3):
        se[i, pl.ds(3 * CP, hid - 3 * CP), :] = ones(WIDE)

    column_wide = lax.broadcasted_iota(jnp.int32, (hid, WIDE), 1)
    column_wide = lax.rem(column_wide, LANES)
    edge_wide = jnp.logical_or(column_wide == 0, column_wide == LANES - 1)
    early = range(1, chunks - 1)

    def first_conv(n):
        return conv_chunk(s1, 2, n)

    def first_step(n, pre):
        s2[pl.ds(CP, CP), block(1, 2 * n, 2)] = forward_chunk(pre, s1, 2, n, slope1, True)

    def early_step(n, pre):
        to_some(n - 1, len(early), post)
        first_step(n, pre)

    to_mate.wait_recv()
    recv[:, my_pair] = packed[:, my_pair]
    pipelined(early, first_conv, early_step)
    receive_state()
    shift_far_rows()
    pipelined((0, chunks - 1), first_conv, first_step)
    beside, at_edge = first_rim(spread_columns())
    merge_columns(at_edge, beside)

    def second_step(n, pre):
        sobs[n] = forward_chunk(pre, s2, 1, n, slope2, False)

    pipelined(range(chunks), lambda n: conv_chunk(s2, 1, n), second_step)
    hid_lane = lane_iota(hid)
    tangents = jnp.zeros((hid, LANES), F32)
    for r in range(height):
        tangents = jnp.where((hid_lane + 1) // 2 == r + 2, rolled(slope2[:, block(0, r)], spot(r)), tangents)
    tangents = jnp.where(hid_lane < LANES // 2, tangents, rolled(tangents, LANES // 2 + 1))
    slope_edge2[...] = jnp.where(kept_cells(), tangents, 0.0)

    others = pl.ds(0, pairs - 1)
    pltpu.make_async_remote_copy(
        src_ref=packed.at[:, others], dst_ref=recv.at[:, others], send_sem=psend, recv_sem=precv,
        device_id=ids[RIGHT], device_id_type=MESH,
    ).wait()

    def unfixed(value, top):
        return value.astype(F32) * (top / HALF_WORDS)

    for which in range(2):

        def field(k, value, which=which):
            opened[pl.ds(which * pairs * 8 + k, pairs, stride=8), :] = value

        words = recv[which, :, 2, :]
        field(0, (words >> 24).astype(F32))
        field(1, ((words >> 16) & (LANES - 1)).astype(F32))
        field(7, unfixed(words & (WORD - 1), TOP_PRECISION))
        for k in range(2):
            words = recv[which, :, k, :]
            field(2 + 2 * k, unfixed((words >> 16) + HALF_WORD, 1.0))
            field(3 + 2 * k, unfixed(words & (WORD - 1), 1.0))
        field(6, recv[which, :, 3, :].astype(F32) * (1.0 / VALUE_STEPS))

    def patch_of(group, u):
        k = group * GROUP + u
        which, pair_id = k // pairs, lax.rem(k, pairs)
        at_side = jnp.where(which == 0, side, 1 - side)
        owner = (2 * (pair_id // n_lon) + at_side) * n_lon + lax.rem(pair_id, n_lon)
        return swath_ref[0, owner]

    column = lax.broadcasted_iota(jnp.int32, (LANES, LANES), 0).astype(F32).astype(BF16)
    channel = lax.broadcasted_iota(jnp.int32, (CP, LANES), 0).astype(F32)
    zero = jnp.zeros((LANES, LANES), BF16)

    def estimate(group, carry):
        def start(u):
            k = group * GROUP + u
            packet = opened[pl.ds(pl.multiple_of(k * 8, 8), 8), :]

            def row(which):
                return jnp.broadcast_to(packet[which : which + 1].astype(BF16), (LANES, LANES))

            at = row(1)
            here, after = column == at, column == at + 1
            table = jnp.concatenate(
                [
                    jnp.where(here, row(2), jnp.where(after, row(3), zero)),
                    jnp.where(here, row(4), jnp.where(after, row(5), zero)),
                ],
                axis=0,
            )
            bsc[k] = table
            return packet, dot(sobs[patch_of(group, u)], table)

        def finish(u, given):
            k = group * GROUP + u
            packet, found = given
            picked = channel == packet[0:1]
            gap = jnp.sum(jnp.where(picked, found, 0.0), axis=0, keepdims=True) - packet[6:7]
            inn[k // pairs, lax.rem(k, pairs)] = gap
            qsc[k] = jnp.where(picked, packet[7:8] * gap, 0.0).astype(BF16)

        pipelined(range(GROUP), start, finish, LAG)
        return carry

    lax.fori_loop(0, owners // GROUP, estimate, 0)
    hist[0] = jnp.zeros((CP, WIDE), F32)

    def pull(group, last):
        slots = [last]

        def start(u):
            k = group * GROUP + u
            return lax.dot_general(qsc[k], bsc[k], (((1,), (1,)), ((), ())), preferred_element_type=F32)

        def finish(u, share):
            k = group * GROUP + u
            patch = patch_of(group, u)
            before = sum(jnp.where(patch == m, slots[-1][m], 0) for m in range(chunks))
            hist[k + 1] = hist[before] + share
            slots.append(tuple(jnp.where(patch == m, k + 1, slots[-1][m]) for m in range(chunks)))

        pipelined(range(GROUP), start, finish, LAG)
        return slots[-1]

    last = lax.fori_loop(0, owners // GROUP, pull, (jnp.int32(0),) * chunks)
    inn_recv[:, my_pair] = inn[:, my_pair]

    def give_back(other, where):
        pltpu.make_async_remote_copy(
            src_ref=inn.at[:, other], dst_ref=inn_recv.at[:, my_pair],
            send_sem=isend, recv_sem=irecv, device_id=where, device_id_type=MESH,
        ).start()

    def tap(i, j, r):
        return ybuf[pl.ds((3 * (i + 1) + j + 1) * CP, CP), pl.ds(r * LANES, LANES)]

    def summed(j, r):
        total = None
        for i in (-1, 0, 1):
            if 0 <= r - i < height:
                part = tap(i, j, r - i)
                total = part if total is None else total + part
        return total

    def rim_sources(t):
        table = dict.fromkeys((LEFT, RIGHT, UL, UR, DL, DR), bcol.at[t])
        return table | {UP: brow.at[t, 0], DOWN: brow.at[t, 1]}

    def rim_targets(t):
        table = {d: rcol.at[t, k] for k, d in enumerate((LEFT, RIGHT, UL, UR, DL, DR))}
        return table | {UP: rrow.at[t, 0], DOWN: rrow.at[t, 1]}

    def spread_of(cotangent, slope):
        breadth = cotangent.shape[1]
        rounded = jnp.concatenate([cotangent.astype(BF16), jnp.zeros((LANES - CP, breadth), BF16)], axis=0)
        return (dot(wot_ref[...], rounded) * slope).astype(BF16)

    def products(cotangent, slope):
        def start(n):
            return spread_of(cotangent(n), slope[:, pl.ds(n * WIDE, WIDE)])

        def finish(n, spread):
            for i in range(3):
                ybuf[pl.ds(3 * i * CP, 3 * CP), pl.ds(n * WIDE, WIDE)] = dot(wk[i, pl.ds(0, 3 * CP), :], spread)

        pipelined(range(chunks), start, finish)

    def inner(t_low, t_mid, t_high):
        return (
            t_mid
            + jnp.where(first_lane, 0.0, rolled(t_high, 1))
            + jnp.where(last_lane, 0.0, rolled(t_low, -1))
        )

    def own_sums(own):
        for r in range(height):
            ubuf[0, :, block(1, r)] = inner(*(summed(j, r) for j in (-1, 0, 1))) + own(r)

    def local_sums(t):
        columns = jnp.zeros((CP, LANES), F32)
        for r in range(-1, height + 1):
            t_low, t_mid, t_high = (summed(j, r) for j in (-1, 0, 1))
            ubuf[t, :, block(1, r)] = inner(t_low, t_mid, t_high)
            columns = gathered(columns, r, jnp.where(first_lane, t_low, t_high))
        return columns

    def send_rim(t, above, below, columns):
        brow[t, 0] = above.astype(BF16)
        brow[t, 1] = below.astype(BF16)
        bcol[t] = columns.astype(BF16)
        src, dst = rim_sources(t), rim_targets(t)
        for d in (LEFT, RIGHT, UL, UR, DL, DR, UP, DOWN):
            send(src[d], dst[opposite[d]], t, d, bsend, brecv)

    def receive_rows(t):
        dst = rim_targets(t)
        for d in (UP, DOWN):
            wait_recv(dst[d], t, d, bsend, brecv)
        for there, row in ((has_up, 0), (has_down, 1)):

            @pl.when(jnp.logical_not(there))
            def _():
                rrow[t, row] = jnp.zeros((CP, LANES), BF16)

        return rrow[t, 0].astype(F32), rrow[t, 1].astype(F32)

    def receive_columns(t):
        dst = rim_targets(t)
        for d in (LEFT, RIGHT, UL, UR, DL, DR):
            wait_recv(dst[d], t, d, bsend, brecv)
        for there, slots in ((has_up, (2, 3)), (has_down, (4, 5))):

            @pl.when(jnp.logical_not(there))
            def _():
                for slot in slots:
                    rcol[t, slot] = jnp.zeros((CP, LANES), BF16)

        from_left, from_right, ul, ur, dl, dr = (rcol[t, k].astype(F32) for k in range(6))
        inside = jnp.logical_and(slot_of >= 2, slot_of < height + 2)
        inflow = jnp.where(inside, jnp.where(even, rolled(from_left, 1), rolled(from_right, -1)), 0.0)
        top, bottom, past, before = spot(0), spot(height - 1), spot(height), spot(-1)
        for value, came, goes in (
            (ul, past - 1, top), (ur, past, top - 1), (dl, before - 1, bottom), (dr, before, bottom - 1),
        ):
            inflow = inflow + jnp.where(lane == goes, rolled(value, goes - came), 0.0)
        return inflow

    far = height - 1
    outside = slot_of <= height + 2

    def rim_products(first_part, cells, slopes):
        late = spread_of(jnp.concatenate(cells, axis=1), jnp.concatenate(slopes, axis=1))
        for i in range(3):
            xbuf[pl.ds(3 * i * CP, 3 * CP), pl.ds(first_part * LANES, late.shape[1])] = dot(
                wk[i, pl.ds(0, 3 * CP), :], late
            )

    def late_tap(i, j, part):
        return xbuf[pl.ds((3 * (i + 1) + j + 1) * CP, CP), pl.ds(part * LANES, LANES)]

    def late_row(part, i):
        return tuple(late_tap(i, j, part) for j in (-1, 0, 1))

    def late_columns(j):
        return sum(rolled(late_tap(i, j, 2), 2 * i) for i in (-1, 0, 1))

    def outward(to_low, to_high):
        return jnp.where(outside, jnp.where(even, to_low, rolled(to_high, -LANES // 2 - 1)), 0.0)

    def pull_row(r):
        return hist[last[r // 2]][:, (r % 2) * LANES : (r % 2 + 1) * LANES]

    at_edge = jnp.zeros((CP, LANES), F32)
    for r in range(height):
        at_edge = gathered(at_edge, r, pull_row(r))
    rim_products(
        0, [pull_row(0), pull_row(far), apart(at_edge)],
        [slope2[:, pl.ds(0, LANES)], slope2[:, pl.ds(far * LANES, LANES)], slope_edge2[...]],
    )
    send_rim(
        0, inner(*late_row(0, -1)), inner(*late_row(1, 1)), outward(late_columns(-1), late_columns(1))
    )
    products(lambda n: hist[last[n]], slope2)
    own_sums(pull_row)

    to_some(0, 1, give_back)
    products(lambda n: ubuf[0, :, block(1, 2 * n, 2)], slope1)
    columns = local_sums(1)
    at_edge = jnp.zeros((CP, LANES), F32)
    for r in range(height):
        at_edge = gathered(at_edge, r, ubuf[0, :, block(1, r)])
    above, below = receive_rows(0)
    rim_products(0, [above, below], [slope1[:, pl.ds(0, LANES)], slope1[:, pl.ds(far * LANES, LANES)]])
    for part, base in ((0, 0), (1, far)):
        for i in (-1, 0, 1):
            t_low, _, t_high = late_row(part, i)
            columns = columns + gathered(
                jnp.zeros((CP, LANES), F32), base + i, jnp.where(first_lane, t_low, t_high)
            )
    at_edge = at_edge + gathered(gathered(jnp.zeros((CP, LANES), F32), 0, above), far, below)
    inflow = receive_columns(0)
    at_edge = at_edge + inflow
    rim_products(2, [apart(at_edge)], [slope_edge[...]])
    to_low, to_same, to_high = (late_columns(j) for j in (-1, 0, 1))
    columns = columns + outward(to_low, to_high)
    same = joined(to_same)
    next_in = jnp.where(even, rolled(to_low, -LANES // 2 - 2), rolled(to_high, 1))
    second = jnp.logical_or(lane == 1, lane == LANES - 2)

    def from_columns(r, outermost):
        return jnp.where(edge, rolled(outermost, -spot(r)), 0.0) + jnp.where(second, rolled(next_in, -spot(r)), 0.0)

    send_rim(
        1,
        ubuf[1, :, block(1, -1)] + inner(*late_row(0, -1)) + from_columns(-1, same),
        ubuf[1, :, block(1, height)] + inner(*late_row(1, 1)) + from_columns(height, same),
        columns,
    )
    pltpu.make_async_remote_copy(
        src_ref=inn.at[:, others], dst_ref=inn_recv.at[:, others], send_sem=isend, recv_sem=irecv,
        device_id=ids[RIGHT], device_id_type=MESH,
    ).wait()
    innov_to_mate = pltpu.make_async_remote_copy(
        src_ref=inn_recv.at[1], dst_ref=inn_mate, send_sem=gsend.at[1], recv_sem=grecv.at[1],
        device_id=mate, device_id_type=MESH,
    )
    innov_to_mate.start()
    outermost = same + inflow
    for r in range(height):
        value = ubuf[0, :, block(1, r)] + ubuf[1, :, block(1, r)] + from_columns(r, outermost)
        if r < 2:
            value = value + inner(*late_row(0, r))
        if r >= far - 1:
            value = value + inner(*late_row(1, r - far))
        if r == 0:
            value = value + above
        if r == far:
            value = value + below
        ubuf[0, :, block(1, r)] = value
    above, below = receive_rows(1)
    inflow = receive_columns(1)
    for r in range(height):
        value = ubuf[0, :, block(1, r)] + jnp.where(edge, rolled(inflow, -spot(r)), 0.0)
        if r == 0:
            value = value + above
        if r == far:
            value = value + below
        here = pl.ds(r, chan, stride=height)
        grad_ref[here, :] = grad_ref[here, :] + value[:chan]

    innov_to_mate.wait()
    to_mate.wait_send()
    for h in range(halves):
        part = pl.ds(h * n_lon, n_lon)
        for which, ref in ((side, inn_recv.at[0]), (1 - side, inn_mate)):
            rows = pl.ds(pl.multiple_of((2 * h + which) * n_lon, n_lon), n_lon)
            innov_ref[rows, :] = ref[part].reshape(n_lon, LANES)
    for d in range(8):
        wait_send(state_sources[d], 0, d, fsend, frecv)
    for t in range(2):
        src = rim_sources(t)
        for d in range(8):
            wait_send(src[d], t, d, bsend, brecv)


def hand_over(gradient_in, innov_in, gradient_out, innov_out, gradient_held, innov_held, sems):
    chan = gradient_in.shape[0]
    cuts = [chan * k // PIECES for k in range(PIECES + 1)]
    parts = [pl.ds(a, b - a) for a, b in zip(cuts, cuts[1:])]
    routes = [(gradient_in.at[p], gradient_held.at[p], gradient_out.at[p]) for p in parts]
    routes.append((innov_in, innov_held, innov_out))
    reads = [pltpu.make_async_copy(src, held, sems.at[0, k]) for k, (src, held, _) in enumerate(routes)]
    writes = [pltpu.make_async_copy(held, dst, sems.at[1, k]) for k, (_, held, dst) in enumerate(routes)]
    for read in reads:
        read.start()
    for read, write in zip(reads, writes):
        read.wait()
        write.start()
    for write in writes:
        write.wait()


def local(
    n_lat, n_lon,
    initial_state, background_state, background_precision, conv_weight, conv_bias, out_weight,
    swath_patch, obs_cell, obs_weights, obs_value, obs_precision,
):
    chan, height, breadth = initial_state.shape
    hid = conv_weight.shape[2]
    owners = n_lat * n_lon
    chunks = height // 2
    cells = height * breadth
    vmem = pl.BlockSpec(memory_space=pltpu.VMEM)
    hbm = pl.BlockSpec(memory_space=pltpu.HBM)
    smem = pl.BlockSpec(memory_space=pltpu.SMEM)
    dma = pltpu.SemaphoreType.DMA
    gradient, innov = pl.pallas_call(
        functools.partial(kernel, n_lat, n_lon, hid),
        out_shape=(
            jax.ShapeDtypeStruct((chan * height, LANES), F32),
            jax.ShapeDtypeStruct((owners, LANES), F32),
        ),
        in_specs=[hbm, hbm, smem, vmem, vmem, vmem, smem] + [hbm] * 4,
        out_specs=(vmem, vmem),
        scratch_shapes=[
            pltpu.VMEM((chan, height, breadth), BF16),
            pltpu.VMEM((chan, height, breadth), BF16),
            pltpu.VMEM((owners, LANES), jnp.int32),
            pltpu.VMEM((4, owners, LANES), F32),
            pltpu.VMEM((owners, LANES), F32),
            pltpu.VMEM((owners, LANES), F32),
            pltpu.VMEM((LANES, hid), F32),
            pltpu.VMEM((3, hid, hid), BF16),
            pltpu.VMEM((3, hid, hid), BF16),
            pltpu.VMEM((CP, hid), BF16),
            pltpu.VMEM((hid, LANES), BF16),
            pltpu.VMEM((CP * height, LANES), F32),
            pltpu.VMEM((owners // 2, 4, LANES), jnp.int32),
            pltpu.VMEM((2, owners // 2, 4, LANES), jnp.int32),
            pltpu.VMEM((2, owners // 2, 4, LANES), jnp.int32),
            pltpu.VMEM((owners * 8, LANES), F32),
            pltpu.VMEM((hid, (height + 4) * LANES), BF16),
            pltpu.VMEM((hid, (height + 2) * LANES), BF16),
            pltpu.VMEM((3, hid, WIDE), BF16),
            pltpu.VMEM((chunks, CP, WIDE), BF16),
            pltpu.VMEM((hid, cells), F32),
            pltpu.VMEM((hid, cells), F32),
            pltpu.VMEM((hid, LANES), F32),
            pltpu.VMEM((hid, LANES), F32),
            pltpu.VMEM((2, CP, LANES), BF16),
            pltpu.VMEM((6, CP, LANES), BF16),
            pltpu.VMEM((owners, WIDE, LANES), BF16),
            pltpu.VMEM((owners, CP, LANES), BF16),
            pltpu.VMEM((2, owners // 2, 1, LANES), F32),
            pltpu.VMEM((2, owners // 2, 1, LANES), F32),
            pltpu.VMEM((owners // 2, 1, LANES), F32),
            pltpu.VMEM((owners + 1, CP, WIDE), F32),
            pltpu.VMEM((9 * CP, cells), F32),
            pltpu.VMEM((9 * CP, 3 * LANES), F32),
            pltpu.VMEM((2, CP, (height + 2) * LANES), F32),
            pltpu.VMEM((2, 2, CP, LANES), BF16),
            pltpu.VMEM((2, CP, LANES), BF16),
            pltpu.VMEM((2, 2, CP, LANES), BF16),
            pltpu.VMEM((2, 6, CP, LANES), BF16),
            dma((1, 8)), dma((1, 8)), dma((2, 8)), dma((2, 8)),
            dma, dma, dma, dma, dma((2,)), dma((2,)), dma((6,)),
        ],
        compiler_params=pltpu.CompilerParams(
            collective_id=0, has_side_effects=True, vmem_limit_bytes=56 * 1024 * 1024
        ),
    )(
        initial_state, background_state, background_precision[None], conv_weight, conv_bias[None], out_weight, swath_patch,
        obs_cell[0], obs_weights[:, 0], obs_value[0], obs_precision[0],
    )
    return pl.pallas_call(
        hand_over,
        out_shape=(
            jax.ShapeDtypeStruct((chan, height, breadth), F32),
            jax.ShapeDtypeStruct((1, owners, LANES), F32),
        ),
        in_specs=[hbm, hbm],
        out_specs=(hbm, hbm),
        scratch_shapes=[
            pltpu.VMEM((chan, height, breadth), F32),
            pltpu.VMEM((1, owners, LANES), F32),
            dma((2, PIECES + 1)),
        ],
        compiler_params=pltpu.CompilerParams(vmem_limit_bytes=56 * 1024 * 1024),
    )(gradient.reshape(chan, height, breadth), innov[None])


def solution(mesh):
    tile = P(None, "lat", "lon")
    owner = ("lat", "lon")
    in_specs = (
        tile, tile, P(), P(), P(), P(),
        P(owner, None), P(owner, None, None), P(None, owner, None, None), P(owner, None, None), P(owner, None, None),
    )
    return jax.shard_map(
        functools.partial(local, mesh.shape["lat"], mesh.shape["lon"]),
        mesh=mesh, in_specs=in_specs, out_specs=(tile, P(owner, None, None)), check_vma=False,
    )
```

```python
import functools

import jax
import jax.numpy as jnp
from jax import lax
from jax.experimental import pallas as pl
from jax.experimental.pallas import tpu as pltpu
from jax.sharding import PartitionSpec as P

MESH = pl.DeviceIdType.MESH
F32 = jnp.float32
BF16 = jnp.bfloat16
CP = 80
LANES = 128
WIDE = 256
ROOT_HALF = 0.7071067811865476
NORM_DENSITY = 0.3989422804014327
UP, DOWN, LEFT, RIGHT, UL, UR, DL, DR = range(8)
GROUP = 32
LAG = 3
PIECES = 2
WORD = 65536
HALF_WORD = 32768
HALF_WORDS = 65535.0
TOP_PRECISION = 3.0
VALUE_STEPS = 2.0**28


def dot(a, b):
    return jnp.dot(a, b, preferred_element_type=F32)


def lane_iota(rows):
    return lax.broadcasted_iota(jnp.int32, (rows, LANES), 1)


def kernel(
    n_lat, n_lon, hid,
    x_hbm, xb_hbm, bp_ref, cw_ref, cb_ref, ow_ref, swath_ref, cell_hbm, w_hbm, val_hbm, prec_hbm,
    grad_ref, innov_ref,
    x_ref, xb_ref, cell_ref, w_ref, val_ref, prec_ref, wpad, wk, wt_ref, wo_ref, wot_ref, x32, given, packed, recv, opened, s1, s2, se, sobs, slope1, slope2, slope_edge, slope_edge2, csend, hcol,
    bsc, qsc, inn, inn_recv, inn_mate, hist, ybuf, xbuf, ubuf, brow, bcol, rrow, rcol,
    fsend, frecv, bsend, brecv, psend, precv, isend, irecv, gsend, grecv, loaded,
):
    chan, height = x_ref.shape[0], x_ref.shape[1]
    owners = n_lat * n_lon
    chunks = height // 2
    lat = lax.axis_index("lat")
    lon = lax.axis_index("lon")
    has_up = lat > 0
    has_down = lat < n_lat - 1
    left = lax.rem(lon + n_lon - 1, n_lon)
    right = lax.rem(lon + 1, n_lon)
    ids = {
        UP: (lat - 1, lon), DOWN: (lat + 1, lon), LEFT: (lat, left), RIGHT: (lat, right),
        UL: (lat - 1, left), UR: (lat - 1, right), DL: (lat + 1, left), DR: (lat + 1, right),
    }
    opposite = {UP: DOWN, DOWN: UP, LEFT: RIGHT, RIGHT: LEFT, UL: DR, DR: UL, UR: DL, DL: UR}

    barrier = pltpu.get_barrier_semaphore()

    def wrapped(value, count):
        return value - jnp.where(value >= count, count, 0)

    side, half = lax.rem(lat, 2), lat // 2
    halves = n_lat // 2
    pairs = halves * n_lon
    mate = {"lat": lat + 1 - 2 * side}
    my_pair = half * n_lon + lon
    rounds = [(step, ahead) for step in range(halves) for ahead in range(n_lon) if step or ahead]

    def to_some(part, parts, act):
        for step, ahead in rounds[len(rounds) * part // parts : len(rounds) * (part + 1) // parts]:
            there, column = wrapped(half + step, halves), wrapped(lon + ahead, n_lon)
            act(there * n_lon + column, (2 * there + side, column))

    def rows_of(which, ref):
        return jnp.concatenate(
            [ref[pl.ds(pl.multiple_of((2 * h + which) * n_lon, n_lon), n_lon), :] for h in range(halves)], axis=0
        )

    def greet(_, where):
        pl.semaphore_signal(barrier, inc=1, device_id=where, device_id_type=MESH)

    across = {UP: has_up, UL: has_up, UR: has_up, DOWN: has_down, DL: has_down, DR: has_down}

    loads = [
        pltpu.make_async_copy(src, dst, loaded.at[k])
        for k, (src, dst) in enumerate(
            (
                (x_hbm, x_ref), (xb_hbm, xb_ref), (cell_hbm, cell_ref),
                (w_hbm, w_ref), (val_hbm, val_ref), (prec_hbm, prec_ref),
            )
        )
    ]
    for load in loads:
        load.start()
    to_some(0, 1, greet)
    for d, there in across.items():
        pl.when(there)(functools.partial(greet, None, ids[d]))

    x32[pl.ds(chan * height, (CP - chan) * height), :] = jnp.zeros(((CP - chan) * height, LANES), F32)
    loads[0].wait()
    x32[pl.ds(0, chan * height), :] = x_ref[...].astype(F32).reshape(chan * height, LANES)
    lane = lane_iota(CP)
    first_lane = lane == 0
    last_lane = lane == LANES - 1

    def block(rim, r, count=1):
        return pl.ds((r + rim) * LANES, count * LANES)

    def rolled(value, shift):
        return pltpu.roll(value, shift % LANES, 1) if shift % LANES else value

    def spot(r):
        return 2 * (r + 2)

    even = lax.rem(lane, 2) == 0
    edge = jnp.logical_or(first_lane, last_lane)
    slot_of = (lane + 1) // 2

    def joined(value):
        return jnp.where(even, value, rolled(value, -LANES // 2 - 1))

    def apart(value):
        return jnp.where(lane < LANES // 2, value, rolled(value, LANES // 2 + 1))

    def gathered(total, r, row):
        return jnp.where(slot_of == r + 2, rolled(row, spot(r)), total)

    pair_of = lane // 2
    to_left = jnp.zeros((CP, LANES), F32)
    to_right = jnp.zeros((CP, LANES), F32)
    for r in range(height):
        row = x32[pl.ds(r, CP, stride=height), :]
        s1[pl.ds(CP, CP), block(2, r)] = row.astype(BF16)
        s1[pl.ds(0, CP), block(2, r)] = rolled(row, 1).astype(BF16)
        s1[pl.ds(2 * CP, CP), block(2, r)] = rolled(row, -1).astype(BF16)
        to_left = jnp.where(pair_of == r + 2, rolled(row, spot(r)), to_left)
        to_right = jnp.where(pair_of == r + 2, rolled(row, spot(r) + 2), to_right)
    csend[0] = to_left.astype(BF16)
    csend[1] = to_right.astype(BF16)

    def guarded(d):
        if d in (UP, UL, UR):
            return pl.when(has_up)
        if d in (DOWN, DL, DR):
            return pl.when(has_down)
        return lambda f: f()

    def send(src, dst, t, d, sends, recvs):
        copy = pltpu.make_async_remote_copy(
            src_ref=src, dst_ref=dst, send_sem=sends.at[t, d], recv_sem=recvs.at[t, opposite[d]],
            device_id=ids[d], device_id_type=MESH,
        )
        guarded(d)(copy.start)

    def wait_recv(dst, t, d, sends, recvs):
        copy = pltpu.make_async_remote_copy(
            src_ref=dst, dst_ref=dst, send_sem=sends.at[t, d], recv_sem=recvs.at[t, d],
            device_id=ids[d], device_id_type=MESH,
        )
        guarded(d)(copy.wait_recv)

    def wait_send(src, t, d, sends, recvs):
        copy = pltpu.make_async_remote_copy(
            src_ref=src, dst_ref=src, send_sem=sends.at[t, d], recv_sem=recvs.at[t, d],
            device_id=ids[d], device_id_type=MESH,
        )
        guarded(d)(copy.wait_send)

    def pair(r):
        return s1.at[pl.ds(CP, CP), block(2, r, 2)]

    state_sources = {
        UP: pair(0), DOWN: pair(height - 2),
        LEFT: csend.at[0], UL: csend.at[0], DL: csend.at[0],
        RIGHT: csend.at[1], UR: csend.at[1], DR: csend.at[1],
    }
    state_targets = {UP: pair(-2), DOWN: pair(height)}
    for k, d in enumerate((LEFT, RIGHT, UL, UR, DL, DR)):
        state_targets[d] = hcol.at[k]

    def send_state():
        for d in (UP, DOWN, LEFT, RIGHT, UL, UR, DL, DR):
            send(state_sources[d], state_targets[opposite[d]], 0, d, fsend, frecv)

    def receive_state():
        for d in range(8):
            wait_recv(state_targets[d], 0, d, fsend, frecv)
        for there, r, slots in ((has_up, -2, (2, 3)), (has_down, height, (4, 5))):

            @pl.when(jnp.logical_not(there))
            def _():
                s1[pl.ds(CP, CP), block(2, r, 2)] = jnp.zeros((CP, WIDE), BF16)
                for slot in slots:
                    hcol[slot] = jnp.zeros((CP, LANES), BF16)

    def shift_far_rows():
        for r in (-2, -1, height, height + 1):
            row = s1[pl.ds(CP, CP), block(2, r)].astype(F32)
            s1[pl.ds(0, CP), block(2, r)] = rolled(row, 1).astype(BF16)
            s1[pl.ds(2 * CP, CP), block(2, r)] = rolled(row, -1).astype(BF16)

    def merge_columns(at_edge, beside):
        at_edge, beside = joined(at_edge), joined(beside)
        for r in range(-1, height + 1):
            row = jnp.where(edge, rolled(at_edge, -spot(r)), s2[pl.ds(CP, CP), block(1, r)].astype(F32))
            outer = rolled(beside, -spot(r))
            s2[pl.ds(0, CP), block(1, r)] = jnp.where(first_lane, outer, rolled(row, 1)).astype(BF16)
            s2[pl.ds(CP, CP), block(1, r)] = row.astype(BF16)
            s2[pl.ds(2 * CP, CP), block(1, r)] = jnp.where(last_lane, outer, rolled(row, -1)).astype(BF16)

    def with_corners(side, above, below):
        middle = jnp.logical_and(pair_of >= 2, pair_of < height + 2)
        outer = jnp.where(pair_of < 2, rolled(above, -2 * height), rolled(below, 2 * height))
        return jnp.where(middle, side, outer)

    def spread_columns():
        from_left, from_right, ul, ur, dl, dr = (hcol[k].astype(F32) for k in range(6))
        low = with_corners(from_left, ul, dl)
        high = with_corners(from_right, ur, dr)
        first = csend[0].astype(F32)
        last = csend[1].astype(F32)
        for r in (-2, -1, height, height + 1):
            row = s1[pl.ds(CP, CP), block(2, r)].astype(F32)
            first = jnp.where(pair_of == r + 2, rolled(row, spot(r)), first)
            last = jnp.where(pair_of == r + 2, rolled(row, spot(r) + 2), last)
        on_left = lane < LANES // 2
        lefts = (low, rolled(low, -1), first, rolled(first, -1))
        rights = tuple(rolled(v, LANES // 2 - k) for v in (last, high) for k in (0, 1))
        beside = tuple(jnp.where(on_left, lefts[j], rights[j + 1]) for j in range(3))
        at_edge = tuple(jnp.where(on_left, lefts[j + 1], rights[j]) for j in range(3))
        for i in range(3):
            for j in range(3):
                part = pl.ds(j * CP, CP)
                se[i, part, pl.ds(0, LANES)] = rolled(beside[j], 2 * (1 - i)).astype(BF16)
                se[i, part, pl.ds(LANES, LANES)] = rolled(at_edge[j], 2 * (1 - i)).astype(BF16)
        return jnp.concatenate([beside[1], at_edge[1]], axis=1)

    def conv(window):
        return sum(dot(wt_ref[i], window(i)) for i in range(3))

    def network(pre, centre):
        cdf = 0.5 * (1.0 + lax.erf(pre * ROOT_HALF))
        update = dot(wo_ref[...], (pre * cdf).astype(BF16))
        return centre.astype(F32) + update, lambda: cdf + pre * jnp.exp(-0.5 * pre * pre) * NORM_DENSITY

    def conv_chunk(s, rim, n):
        return conv(lambda i: s[:, block(rim, 2 * n + i - 1, 2)])

    def forward_chunk(pre, s, rim, n, slope, inner_only):
        state, tangent = network(pre, s[pl.ds(CP, CP), block(rim, 2 * n, 2)])
        slope[:, pl.ds(n * WIDE, WIDE)] = jnp.where(edge_wide, 0.0, tangent()) if inner_only else tangent()
        return state.astype(BF16)

    def pipelined(order, start, finish, lag=1):
        order = list(order)
        held = [start(n) for n in order[:lag]]
        for k, n in enumerate(order):
            if k + lag < len(order):
                held.append(start(order[k + lag]))
            finish(n, held.pop(0))

    def kept_cells():
        here = lax.rem(lane_iota(hid), LANES // 2)
        return jnp.logical_and(lax.rem(here, 2) == 0, jnp.logical_and(here >= spot(0), here <= spot(height - 1)))

    def first_rim(centre):
        up, down = has_up.astype(F32), has_down.astype(F32)
        rows = (-1, height)
        state, _ = network(
            conv(lambda i: jnp.concatenate([s1[:, block(2, r + i - 1)] for r in rows], axis=1)),
            jnp.concatenate([s1[pl.ds(CP, CP), block(2, r)] for r in rows], axis=1),
        )
        s2[pl.ds(CP, CP), block(1, -1)] = (state[:, :LANES] * up).astype(BF16)
        s2[pl.ds(CP, CP), block(1, height)] = (state[:, LANES:] * down).astype(BF16)
        sides, tangent = network(conv(lambda i: se[i]), centre)
        place = lax.rem(lane, LANES // 2)
        inside = jnp.where(place == spot(-1), up, jnp.where(place == spot(height), down, 1.0))
        slope_edge[...] = jnp.where(kept_cells(), tangent()[:, LANES:], 0.0)
        return tuple((sides[:, k * LANES : (k + 1) * LANES] * inside).astype(BF16).astype(F32) for k in (0, 1))

    pl.semaphore_wait(barrier, pairs - 1 + 3 * (has_up.astype(jnp.int32) + has_down.astype(jnp.int32)))
    send_state()

    for load in loads[1:]:
        load.wait()
    def fixed(value, top):
        return jnp.round(value * (HALF_WORDS / top)).astype(jnp.int32)

    def packet_words(which):
        first, second, third, fourth = (fixed(rows_of(which, w_ref.at[k]), 1.0) for k in range(4))
        return (
            (first - HALF_WORD) * WORD + second,
            (third - HALF_WORD) * WORD + fourth,
            rows_of(which, cell_ref) * WORD + fixed(rows_of(which, prec_ref), TOP_PRECISION),
            jnp.round(rows_of(which, val_ref) * VALUE_STEPS).astype(jnp.int32),
        )

    for k, word in enumerate(packet_words(1 - side)):
        given[:, k, :] = word
    to_mate = pltpu.make_async_remote_copy(
        src_ref=given, dst_ref=packed.at[1], send_sem=gsend.at[0], recv_sem=grecv.at[0],
        device_id=mate, device_id_type=MESH,
    )
    to_mate.start()
    for k, word in enumerate(packet_words(side)):
        packed[0, :, k, :] = word

    def post(other, where):
        pltpu.make_async_remote_copy(
            src_ref=packed.at[:, other], dst_ref=recv.at[:, my_pair],
            send_sem=psend, recv_sem=precv, device_id=where, device_id_type=MESH,
        ).start()

    wpad[...] = jnp.zeros((LANES, hid), F32)
    bias = cb_ref[...]
    bias_parts = []
    for _ in range(3):
        part = bias.astype(BF16).astype(F32)
        bias_parts.append(part)
        bias = bias - part
    spare = lax.broadcasted_iota(jnp.int32, (hid - 3 * CP, hid), 0)
    bias_rows = jnp.zeros((hid - 3 * CP, hid), F32)
    for k, part in enumerate(bias_parts):
        bias_rows = jnp.where(spare == k, part, bias_rows)
    for i in range(3):
        for j in range(3):
            wpad[pl.ds(0, chan), :] = cw_ref[3 * i + j].astype(F32)
            wk[i, pl.ds(j * CP, CP), :] = wpad[pl.ds(0, CP), :].astype(BF16)
        wk[i, pl.ds(3 * CP, hid - 3 * CP), :] = (bias_rows if i == 1 else jnp.zeros_like(bias_rows)).astype(BF16)
        wt_ref[i] = jnp.transpose(wk[i].astype(F32)).astype(BF16)
    wpad[pl.ds(0, chan), :] = ow_ref[...].astype(F32)
    wo_ref[...] = wpad[pl.ds(0, CP), :].astype(BF16)
    wot_ref[...] = jnp.transpose(wpad[...]).astype(BF16)
    grad_ref[pl.ds(chan * height, (CP - chan) * height), :] = jnp.zeros(((CP - chan) * height, LANES), F32)
    for c in range(chan):
        grad_ref[pl.ds(c * height, height), :] = bp_ref[0, c] * (x_ref[c].astype(F32) - xb_ref[c].astype(F32))

    def ones(breadth):
        return jnp.ones((hid - 3 * CP, breadth), BF16)

    s1[pl.ds(3 * CP, hid - 3 * CP), :] = ones((height + 4) * LANES)
    s2[pl.ds(3 * CP, hid - 3 * CP), :] = ones((height + 2) * LANES)
    for i in range(3):
        se[i, pl.ds(3 * CP, hid - 3 * CP), :] = ones(WIDE)

    column_wide = lax.broadcasted_iota(jnp.int32, (hid, WIDE), 1)
    column_wide = lax.rem(column_wide, LANES)
    edge_wide = jnp.logical_or(column_wide == 0, column_wide == LANES - 1)
    early = range(1, chunks - 1)

    def first_conv(n):
        return conv_chunk(s1, 2, n)

    def first_step(n, pre):
        s2[pl.ds(CP, CP), block(1, 2 * n, 2)] = forward_chunk(pre, s1, 2, n, slope1, True)

    def early_step(n, pre):
        to_some(n - 1, len(early), post)
        first_step(n, pre)

    to_mate.wait_recv()
    recv[:, my_pair] = packed[:, my_pair]
    pipelined(early, first_conv, early_step)
    receive_state()
    shift_far_rows()
    pipelined((0, chunks - 1), first_conv, first_step)
    beside, at_edge = first_rim(spread_columns())
    merge_columns(at_edge, beside)

    def second_step(n, pre):
        sobs[n] = forward_chunk(pre, s2, 1, n, slope2, False)

    pipelined(range(chunks), lambda n: conv_chunk(s2, 1, n), second_step)
    hid_lane = lane_iota(hid)
    tangents = jnp.zeros((hid, LANES), F32)
    for r in range(height):
        tangents = jnp.where((hid_lane + 1) // 2 == r + 2, rolled(slope2[:, block(0, r)], spot(r)), tangents)
    tangents = jnp.where(hid_lane < LANES // 2, tangents, rolled(tangents, LANES // 2 + 1))
    slope_edge2[...] = jnp.where(kept_cells(), tangents, 0.0)

    others = pl.ds(0, pairs - 1)
    pltpu.make_async_remote_copy(
        src_ref=packed.at[:, others], dst_ref=recv.at[:, others], send_sem=psend, recv_sem=precv,
        device_id=ids[RIGHT], device_id_type=MESH,
    ).wait()

    def unfixed(value, top):
        return value.astype(F32) * (top / HALF_WORDS)

    for which in range(2):

        def field(k, value, which=which):
            opened[pl.ds(which * pairs * 8 + k, pairs, stride=8), :] = value

        words = recv[which, :, 2, :]
        field(0, (words >> 24).astype(F32))
        field(1, ((words >> 16) & (LANES - 1)).astype(F32))
        field(7, unfixed(words & (WORD - 1), TOP_PRECISION))
        for k in range(2):
            words = recv[which, :, k, :]
            field(2 + 2 * k, unfixed((words >> 16) + HALF_WORD, 1.0))
            field(3 + 2 * k, unfixed(words & (WORD - 1), 1.0))
        field(6, recv[which, :, 3, :].astype(F32) * (1.0 / VALUE_STEPS))

    def patch_of(group, u):
        k = group * GROUP + u
        which, pair_id = k // pairs, lax.rem(k, pairs)
        at_side = jnp.where(which == 0, side, 1 - side)
        owner = (2 * (pair_id // n_lon) + at_side) * n_lon + lax.rem(pair_id, n_lon)
        return swath_ref[0, owner]

    column = lax.broadcasted_iota(jnp.int32, (LANES, LANES), 0).astype(F32).astype(BF16)
    channel = lax.broadcasted_iota(jnp.int32, (CP, LANES), 0).astype(F32)
    zero = jnp.zeros((LANES, LANES), BF16)

    def estimate(group, carry):
        def start(u):
            k = group * GROUP + u
            packet = opened[pl.ds(pl.multiple_of(k * 8, 8), 8), :]

            def row(which):
                return jnp.broadcast_to(packet[which : which + 1].astype(BF16), (LANES, LANES))

            at = row(1)
            here, after = column == at, column == at + 1
            table = jnp.concatenate(
                [
                    jnp.where(here, row(2), jnp.where(after, row(3), zero)),
                    jnp.where(here, row(4), jnp.where(after, row(5), zero)),
                ],
                axis=0,
            )
            bsc[k] = table
            return packet, dot(sobs[patch_of(group, u)], table)

        def finish(u, given):
            k = group * GROUP + u
            packet, found = given
            picked = channel == packet[0:1]
            gap = jnp.sum(jnp.where(picked, found, 0.0), axis=0, keepdims=True) - packet[6:7]
            inn[k // pairs, lax.rem(k, pairs)] = gap
            qsc[k] = jnp.where(picked, packet[7:8] * gap, 0.0).astype(BF16)

        pipelined(range(GROUP), start, finish, LAG)
        return carry

    lax.fori_loop(0, owners // GROUP, estimate, 0)
    hist[0] = jnp.zeros((CP, WIDE), F32)

    def pull(group, last):
        slots = [last]

        def start(u):
            k = group * GROUP + u
            return lax.dot_general(qsc[k], bsc[k], (((1,), (1,)), ((), ())), preferred_element_type=F32)

        def finish(u, share):
            k = group * GROUP + u
            patch = patch_of(group, u)
            before = sum(jnp.where(patch == m, slots[-1][m], 0) for m in range(chunks))
            hist[k + 1] = hist[before] + share
            slots.append(tuple(jnp.where(patch == m, k + 1, slots[-1][m]) for m in range(chunks)))

        pipelined(range(GROUP), start, finish, LAG)
        return slots[-1]

    last = lax.fori_loop(0, owners // GROUP, pull, (jnp.int32(0),) * chunks)
    inn_recv[:, my_pair] = inn[:, my_pair]

    def give_back(other, where):
        pltpu.make_async_remote_copy(
            src_ref=inn.at[:, other], dst_ref=inn_recv.at[:, my_pair],
            send_sem=isend, recv_sem=irecv, device_id=where, device_id_type=MESH,
        ).start()

    def tap(i, j, r):
        return ybuf[pl.ds((3 * (i + 1) + j + 1) * CP, CP), pl.ds(r * LANES, LANES)]

    def summed(j, r):
        total = None
        for i in (-1, 0, 1):
            if 0 <= r - i < height:
                part = tap(i, j, r - i)
                total = part if total is None else total + part
        return total

    def rim_sources(t):
        table = dict.fromkeys((LEFT, RIGHT, UL, UR, DL, DR), bcol.at[t])
        return table | {UP: brow.at[t, 0], DOWN: brow.at[t, 1]}

    def rim_targets(t):
        table = {d: rcol.at[t, k] for k, d in enumerate((LEFT, RIGHT, UL, UR, DL, DR))}
        return table | {UP: rrow.at[t, 0], DOWN: rrow.at[t, 1]}

    def spread_of(cotangent, slope):
        breadth = cotangent.shape[1]
        rounded = jnp.concatenate([cotangent.astype(BF16), jnp.zeros((LANES - CP, breadth), BF16)], axis=0)
        return (dot(wot_ref[...], rounded) * slope).astype(BF16)

    def products(cotangent, slope):
        def start(n):
            return spread_of(cotangent(n), slope[:, pl.ds(n * WIDE, WIDE)])

        def finish(n, spread):
            for i in range(3):
                ybuf[pl.ds(3 * i * CP, 3 * CP), pl.ds(n * WIDE, WIDE)] = dot(wk[i, pl.ds(0, 3 * CP), :], spread)

        pipelined(range(chunks), start, finish)

    def inner(t_low, t_mid, t_high):
        return (
            t_mid
            + jnp.where(first_lane, 0.0, rolled(t_high, 1))
            + jnp.where(last_lane, 0.0, rolled(t_low, -1))
        )

    def own_sums(own):
        for r in range(height):
            ubuf[0, :, block(1, r)] = inner(*(summed(j, r) for j in (-1, 0, 1))) + own(r)

    def local_sums(t):
        columns = jnp.zeros((CP, LANES), F32)
        for r in range(-1, height + 1):
            t_low, t_mid, t_high = (summed(j, r) for j in (-1, 0, 1))
            ubuf[t, :, block(1, r)] = inner(t_low, t_mid, t_high)
            columns = gathered(columns, r, jnp.where(first_lane, t_low, t_high))
        return columns

    def send_rim(t, above, below, columns):
        brow[t, 0] = above.astype(BF16)
        brow[t, 1] = below.astype(BF16)
        bcol[t] = columns.astype(BF16)
        src, dst = rim_sources(t), rim_targets(t)
        for d in (LEFT, RIGHT, UL, UR, DL, DR, UP, DOWN):
            send(src[d], dst[opposite[d]], t, d, bsend, brecv)

    def receive_rows(t):
        dst = rim_targets(t)
        for d in (UP, DOWN):
            wait_recv(dst[d], t, d, bsend, brecv)
        for there, row in ((has_up, 0), (has_down, 1)):

            @pl.when(jnp.logical_not(there))
            def _():
                rrow[t, row] = jnp.zeros((CP, LANES), BF16)

        return rrow[t, 0].astype(F32), rrow[t, 1].astype(F32)

    def receive_columns(t):
        dst = rim_targets(t)
        for d in (LEFT, RIGHT, UL, UR, DL, DR):
            wait_recv(dst[d], t, d, bsend, brecv)
        for there, slots in ((has_up, (2, 3)), (has_down, (4, 5))):

            @pl.when(jnp.logical_not(there))
            def _():
                for slot in slots:
                    rcol[t, slot] = jnp.zeros((CP, LANES), BF16)

        from_left, from_right, ul, ur, dl, dr = (rcol[t, k].astype(F32) for k in range(6))
        inside = jnp.logical_and(slot_of >= 2, slot_of < height + 2)
        inflow = jnp.where(inside, jnp.where(even, rolled(from_left, 1), rolled(from_right, -1)), 0.0)
        top, bottom, past, before = spot(0), spot(height - 1), spot(height), spot(-1)
        for value, came, goes in (
            (ul, past - 1, top), (ur, past, top - 1), (dl, before - 1, bottom), (dr, before, bottom - 1),
        ):
            inflow = inflow + jnp.where(lane == goes, rolled(value, goes - came), 0.0)
        return inflow

    far = height - 1
    outside = slot_of <= height + 2

    def rim_products(first_part, cells, slopes):
        late = spread_of(jnp.concatenate(cells, axis=1), jnp.concatenate(slopes, axis=1))
        for i in range(3):
            xbuf[pl.ds(3 * i * CP, 3 * CP), pl.ds(first_part * LANES, late.shape[1])] = dot(
                wk[i, pl.ds(0, 3 * CP), :], late
            )

    def late_tap(i, j, part):
        return xbuf[pl.ds((3 * (i + 1) + j + 1) * CP, CP), pl.ds(part * LANES, LANES)]

    def late_row(part, i):
        return tuple(late_tap(i, j, part) for j in (-1, 0, 1))

    def late_columns(j):
        return sum(rolled(late_tap(i, j, 2), 2 * i) for i in (-1, 0, 1))

    def outward(to_low, to_high):
        return jnp.where(outside, jnp.where(even, to_low, rolled(to_high, -LANES // 2 - 1)), 0.0)

    def pull_row(r):
        return hist[last[r // 2]][:, (r % 2) * LANES : (r % 2 + 1) * LANES]

    at_edge = jnp.zeros((CP, LANES), F32)
    for r in range(height):
        at_edge = gathered(at_edge, r, pull_row(r))
    rim_products(
        0, [pull_row(0), pull_row(far), apart(at_edge)],
        [slope2[:, pl.ds(0, LANES)], slope2[:, pl.ds(far * LANES, LANES)], slope_edge2[...]],
    )
    send_rim(
        0, inner(*late_row(0, -1)), inner(*late_row(1, 1)), outward(late_columns(-1), late_columns(1))
    )
    products(lambda n: hist[last[n]], slope2)
    own_sums(pull_row)

    to_some(0, 1, give_back)
    products(lambda n: ubuf[0, :, block(1, 2 * n, 2)], slope1)
    columns = local_sums(1)
    at_edge = jnp.zeros((CP, LANES), F32)
    for r in range(height):
        at_edge = gathered(at_edge, r, ubuf[0, :, block(1, r)])
    above, below = receive_rows(0)
    rim_products(0, [above, below], [slope1[:, pl.ds(0, LANES)], slope1[:, pl.ds(far * LANES, LANES)]])
    for part, base in ((0, 0), (1, far)):
        for i in (-1, 0, 1):
            t_low, _, t_high = late_row(part, i)
            columns = columns + gathered(
                jnp.zeros((CP, LANES), F32), base + i, jnp.where(first_lane, t_low, t_high)
            )
    at_edge = at_edge + gathered(gathered(jnp.zeros((CP, LANES), F32), 0, above), far, below)
    inflow = receive_columns(0)
    at_edge = at_edge + inflow
    rim_products(2, [apart(at_edge)], [slope_edge[...]])
    to_low, to_same, to_high = (late_columns(j) for j in (-1, 0, 1))
    columns = columns + outward(to_low, to_high)
    same = joined(to_same)
    next_in = jnp.where(even, rolled(to_low, -LANES // 2 - 2), rolled(to_high, 1))
    second = jnp.logical_or(lane == 1, lane == LANES - 2)

    def from_columns(r, outermost):
        return jnp.where(edge, rolled(outermost, -spot(r)), 0.0) + jnp.where(second, rolled(next_in, -spot(r)), 0.0)

    send_rim(
        1,
        ubuf[1, :, block(1, -1)] + inner(*late_row(0, -1)) + from_columns(-1, same),
        ubuf[1, :, block(1, height)] + inner(*late_row(1, 1)) + from_columns(height, same),
        columns,
    )
    pltpu.make_async_remote_copy(
        src_ref=inn.at[:, others], dst_ref=inn_recv.at[:, others], send_sem=isend, recv_sem=irecv,
        device_id=ids[RIGHT], device_id_type=MESH,
    ).wait()
    innov_to_mate = pltpu.make_async_remote_copy(
        src_ref=inn_recv.at[1], dst_ref=inn_mate, send_sem=gsend.at[1], recv_sem=grecv.at[1],
        device_id=mate, device_id_type=MESH,
    )
    innov_to_mate.start()
    outermost = same + inflow
    for r in range(height):
        value = ubuf[0, :, block(1, r)] + ubuf[1, :, block(1, r)] + from_columns(r, outermost)
        if r < 2:
            value = value + inner(*late_row(0, r))
        if r >= far - 1:
            value = value + inner(*late_row(1, r - far))
        if r == 0:
            value = value + above
        if r == far:
            value = value + below
        ubuf[0, :, block(1, r)] = value
    above, below = receive_rows(1)
    inflow = receive_columns(1)
    for r in range(height):
        value = ubuf[0, :, block(1, r)] + jnp.where(edge, rolled(inflow, -spot(r)), 0.0)
        if r == 0:
            value = value + above
        if r == far:
            value = value + below
        here = pl.ds(r, CP, stride=height)
        grad_ref[here, :] = grad_ref[here, :] + value

    innov_to_mate.wait()
    to_mate.wait_send()
    for h in range(halves):
        part = pl.ds(h * n_lon, n_lon)
        for which, ref in ((side, inn_recv.at[0]), (1 - side, inn_mate)):
            rows = pl.ds(pl.multiple_of((2 * h + which) * n_lon, n_lon), n_lon)
            innov_ref[rows, :] = ref[part].reshape(n_lon, LANES)
    for d in range(8):
        wait_send(state_sources[d], 0, d, fsend, frecv)
    for t in range(2):
        src = rim_sources(t)
        for d in range(8):
            wait_send(src[d], t, d, bsend, brecv)


def hand_over(gradient_in, innov_in, gradient_out, innov_out, gradient_held, innov_held, sems):
    chan = gradient_out.shape[0]
    cuts = [chan * k // PIECES for k in range(PIECES + 1)]
    parts = [pl.ds(a, b - a) for a, b in zip(cuts, cuts[1:])]
    routes = [(gradient_in.at[p], gradient_held.at[p], gradient_out.at[p]) for p in parts]
    routes.append((innov_in, innov_held, innov_out))
    reads = [pltpu.make_async_copy(src, held, sems.at[0, k]) for k, (src, held, _) in enumerate(routes)]
    writes = [pltpu.make_async_copy(held, dst, sems.at[1, k]) for k, (_, held, dst) in enumerate(routes)]
    for read in reads:
        read.start()
    for read, write in zip(reads, writes):
        read.wait()
        write.start()
    for write in writes:
        write.wait()


def local(
    n_lat, n_lon,
    initial_state, background_state, background_precision, conv_weight, conv_bias, out_weight,
    swath_patch, obs_cell, obs_weights, obs_value, obs_precision,
):
    chan, height, breadth = initial_state.shape
    hid = conv_weight.shape[2]
    owners = n_lat * n_lon
    chunks = height // 2
    cells = height * breadth
    vmem = pl.BlockSpec(memory_space=pltpu.VMEM)
    hbm = pl.BlockSpec(memory_space=pltpu.HBM)
    smem = pl.BlockSpec(memory_space=pltpu.SMEM)
    dma = pltpu.SemaphoreType.DMA
    gradient, innov = pl.pallas_call(
        functools.partial(kernel, n_lat, n_lon, hid),
        out_shape=(
            jax.ShapeDtypeStruct((CP * height, LANES), F32),
            jax.ShapeDtypeStruct((owners, LANES), F32),
        ),
        in_specs=[hbm, hbm, smem, vmem, vmem, vmem, smem] + [hbm] * 4,
        out_specs=(vmem, vmem),
        scratch_shapes=[
            pltpu.VMEM((chan, height, breadth), BF16),
            pltpu.VMEM((chan, height, breadth), BF16),
            pltpu.VMEM((owners, LANES), jnp.int32),
            pltpu.VMEM((4, owners, LANES), F32),
            pltpu.VMEM((owners, LANES), F32),
            pltpu.VMEM((owners, LANES), F32),
            pltpu.VMEM((LANES, hid), F32),
            pltpu.VMEM((3, hid, hid), BF16),
            pltpu.VMEM((3, hid, hid), BF16),
            pltpu.VMEM((CP, hid), BF16),
            pltpu.VMEM((hid, LANES), BF16),
            pltpu.VMEM((CP * height, LANES), F32),
            pltpu.VMEM((owners // 2, 4, LANES), jnp.int32),
            pltpu.VMEM((2, owners // 2, 4, LANES), jnp.int32),
            pltpu.VMEM((2, owners // 2, 4, LANES), jnp.int32),
            pltpu.VMEM((owners * 8, LANES), F32),
            pltpu.VMEM((hid, (height + 4) * LANES), BF16),
            pltpu.VMEM((hid, (height + 2) * LANES), BF16),
            pltpu.VMEM((3, hid, WIDE), BF16),
            pltpu.VMEM((chunks, CP, WIDE), BF16),
            pltpu.VMEM((hid, cells), F32),
            pltpu.VMEM((hid, cells), F32),
            pltpu.VMEM((hid, LANES), F32),
            pltpu.VMEM((hid, LANES), F32),
            pltpu.VMEM((2, CP, LANES), BF16),
            pltpu.VMEM((6, CP, LANES), BF16),
            pltpu.VMEM((owners, WIDE, LANES), BF16),
            pltpu.VMEM((owners, CP, LANES), BF16),
            pltpu.VMEM((2, owners // 2, 1, LANES), F32),
            pltpu.VMEM((2, owners // 2, 1, LANES), F32),
            pltpu.VMEM((owners // 2, 1, LANES), F32),
            pltpu.VMEM((owners + 1, CP, WIDE), F32),
            pltpu.VMEM((9 * CP, cells), F32),
            pltpu.VMEM((9 * CP, 3 * LANES), F32),
            pltpu.VMEM((2, CP, (height + 2) * LANES), F32),
            pltpu.VMEM((2, 2, CP, LANES), BF16),
            pltpu.VMEM((2, CP, LANES), BF16),
            pltpu.VMEM((2, 2, CP, LANES), BF16),
            pltpu.VMEM((2, 6, CP, LANES), BF16),
            dma((1, 8)), dma((1, 8)), dma((2, 8)), dma((2, 8)),
            dma, dma, dma, dma, dma((2,)), dma((2,)), dma((6,)),
        ],
        compiler_params=pltpu.CompilerParams(
            collective_id=0, has_side_effects=True, vmem_limit_bytes=56 * 1024 * 1024
        ),
    )(
        initial_state, background_state, background_precision[None], conv_weight, conv_bias[None], out_weight, swath_patch,
        obs_cell[0], obs_weights[:, 0], obs_value[0], obs_precision[0],
    )
    return pl.pallas_call(
        hand_over,
        out_shape=(
            jax.ShapeDtypeStruct((chan, height, breadth), F32),
            jax.ShapeDtypeStruct((1, owners, LANES), F32),
        ),
        in_specs=[hbm, hbm],
        out_specs=(hbm, hbm),
        scratch_shapes=[
            pltpu.VMEM((chan, height, breadth), F32),
            pltpu.VMEM((1, owners, LANES), F32),
            dma((2, PIECES + 1)),
        ],
        compiler_params=pltpu.CompilerParams(vmem_limit_bytes=56 * 1024 * 1024),
    )(gradient.reshape(CP, height, breadth), innov[None])


def solution(mesh):
    tile = P(None, "lat", "lon")
    owner = ("lat", "lon")
    in_specs = (
        tile, tile, P(), P(), P(), P(),
        P(owner, None), P(owner, None, None), P(None, owner, None, None), P(owner, None, None), P(owner, None, None),
    )
    return jax.shard_map(
        functools.partial(local, mesh.shape["lat"], mesh.shape["lon"]),
        mesh=mesh, in_specs=in_specs, out_specs=(tile, P(owner, None, None)), check_vma=False,
    )
```
